32 devices in a mesh: rows: 8 (over z, x), ch: 4 (over y, core).
Axes of the slice: x: 2, y: 2, z: 4, core: 2. Of those that a mesh axis runs over, the one named last changes fastest.
Arguments:
- features: bfloat16 [2, 512, 4096], P(None, 'ch', 'rows'), may hold values from -6 to 6
- crop_ids: int32 [2, 4096], replicated, may hold values from 0 to 5, as said below
- timesteps: int32 [2], replicated, may hold values from 0 to 999
- clip_embed: float32 [2, 2048], replicated, may hold values from -6 to 6
- context: bfloat16 [2, 128, 2048], replicated, may hold values from -6 to 6
- norm1_gain: float32 [512], P('ch'), may hold values from 0.5 to 1.5
- norm1_bias: float32 [512], P('ch'), may hold values from -1.5 to 1.5
- conv1_weight: bfloat16 [512, 3, 3, 512], P('ch'), may hold values from -0.09375 to 0.09375
- conv1_bias: float32 [512], P('ch'), may hold values from -1.5 to 1.5
- embed_weight: bfloat16 [2, 512, 2048], P(None, 'ch'), may hold values from -0.125 to 0.125
- embed_bias: float32 [2, 512], P(None, 'ch'), may hold values from -1.5 to 1.5
- norm2_gain: float32 [512], P('ch'), may hold values from 0.5 to 1.5
- norm2_bias: float32 [512], P('ch'), may hold values from -1.5 to 1.5
- conv2_weight: bfloat16 [512, 3, 3, 512], P('ch'), may hold values from -0.09375 to 0.09375
- conv2_bias: float32 [512], P('ch'), may hold values from -1.5 to 1.5
- norm3_gain: float32 [512], P('ch'), may hold values from 0.5 to 1.5
- norm3_bias: float32 [512], P('ch'), may hold values from -1.5 to 1.5
- qkv_weight: bfloat16 [3, 512, 512], P(None, 'ch'), may hold values from -0.25 to 0.25
- qkv_bias: float32 [2, 512], P(None, 'ch'), may hold values from -1.5 to 1.5
- encoder_weight: bfloat16 [2, 512, 2048], P(None, 'ch'), may hold values from -0.125 to 0.125
- encoder_bias: float32 [2, 512], P(None, 'ch'), may hold values from -1.5 to 1.5
- proj_weight: bfloat16 [512, 512], P('ch'), may hold values from -2 to 2
- proj_bias: float32 [512], P('ch'), may hold values from -1.5 to 1.5
- out_grad: bfloat16 [2, 512, 4096], P(None, 'ch', 'rows'), may hold values from -6 to 6
Outputs:
- output: bfloat16 [2, 512, 4096], P(None, 'ch', 'rows')
- features_grad: bfloat16 [2, 512, 4096], P(None, 'ch', 'rows')
- norm1_gain_grad: float32 [512], P('ch')
- norm1_bias_grad: float32 [512], P('ch')
- conv1_weight_grad: float32 [512, 3, 3, 512], P('ch')
- conv1_bias_grad: float32 [512], P('ch')
- embed_weight_grad: float32 [2, 512, 2048], P(None, 'ch')
- embed_bias_grad: float32 [2, 512], P(None, 'ch')
- norm2_gain_grad: float32 [512], P('ch')
- norm2_bias_grad: float32 [512], P('ch')
- conv2_weight_grad: float32 [512, 3, 3, 512], P('ch')
- conv2_bias_grad: float32 [512], P('ch')
- norm3_gain_grad: float32 [512], P('ch')
- norm3_bias_grad: float32 [512], P('ch')
- qkv_weight_grad: float32 [3, 512, 512], P(None, 'ch')
- qkv_bias_grad: float32 [2, 512], P(None, 'ch')
- encoder_weight_grad: float32 [2, 512, 2048], P(None, 'ch')
- encoder_bias_grad: float32 [2, 512], P(None, 'ch')
- proj_weight_grad: float32 [512, 512], P('ch')
- proj_bias_grad: float32 [512], P('ch')
The draws below stay inside these ranges and needn't reach their ends.
Inputs may be any that keep to these rules, and one draw needn't show every extreme that they name: `crop_ids`: in every micro-batch each of the 6 crop ids marks one rectangle of pixels; one crop spans all 64 rows.
All inputs are finite; a program needn't handle non-finite values.
Results may differ from the reference program's by a relative error of at most 0.015.
Values may be sent and summed in bfloat16 or wider, within the bound.
No kernel may reach another device: no remote copies, remote signals or barrier semaphores. Data moves between devices by JAX's collectives and lax.ppermute only.
A program may use at most 384 MiB of HBM per device.

```python
import math
import jax
import jax.numpy as jnp
from jax import lax

C = 512
HEADS = 8
HD = 64
GROUPS = 32
EMB = 2048
ENC = 2048
CTX = 128
W = 64
MB = 2
NCROP = 6
H = 64


def draw_crop_ids(key, part):
    key = jax.random.fold_in(key, 7)

    def draw_strip(strip_key):
        splits = jax.random.split(strip_key, 3)
        cut_col = jax.random.randint(splits[0], (), W // 2, 3 * W // 4 + 1)
        cut_rows = jax.random.permutation(splits[1], H - 1)[:NCROP - 2] + 1
        row_index = jnp.arange(H, dtype=jnp.int32)
        band_index = jnp.sum((row_index[:, None] >= cut_rows[None, :]).astype(jnp.int32), axis=1)
        col_index = jnp.arange(W, dtype=jnp.int32)
        local_ids = jnp.where(col_index[None, :] < cut_col, 0, 1 + band_index[:, None])
        relabel = jax.random.permutation(splits[2], NCROP).astype(jnp.int32)
        return relabel[local_ids].astype(jnp.int32).reshape(H * W)
    return jax.vmap(draw_strip)(jax.random.split(key, MB))


def steps_of(rng, dims, cuts, low, largest):
    gain, own = 1.0, jax.random.fold_in(rng, 6)
    for dim, parts in cuts:
        steps = jnp.exp(jax.random.uniform(jax.random.fold_in(own, dim), (parts,), jnp.float32, low / len(cuts), largest / len(cuts)))
        gain = gain * jnp.repeat(steps, dims[dim] // parts).reshape([-1 if axis == dim else 1 for axis in range(len(dims))])
    return gain


def bell_draw(rng, shape, scale, limit, cuts=(), kind=jnp.bfloat16):
    loudness = steps_of(rng, shape, cuts, -0.22, 0.18) if cuts else 1.0
    values = jax.random.normal(rng, shape, jnp.float32) * scale * loudness
    return jnp.minimum(jnp.maximum(values, -limit), limit).astype(kind)


def setup_inputs(seed: int = 0) -> dict:
    key_list = jax.random.split(jax.random.key(seed), 25)
    return {
        "features": bell_draw(key_list[0], (MB, C, H * W), 1.0, 6.0, ((1, 4), (2, 8))),
        "crop_ids": draw_crop_ids(jax.random.fold_in(key_list[24], 71), 0),
        "timesteps": jax.random.randint(key_list[2], (MB,), 0, 1000).astype(jnp.int32),
        "clip_embed": bell_draw(key_list[3], (MB, EMB), 1.0, 6.0, (), jnp.float32),
        "context": bell_draw(key_list[4], (MB, CTX, ENC), 1.0, 6.0),
        "norm1_gain": jnp.clip(1.0 + 0.1 * jax.random.normal(key_list[5], (C,), jnp.float32), 0.5, 1.5),
        "norm1_bias": bell_draw(key_list[6], (C,), 0.3, 1.5, ((0, 4),), jnp.float32),
        "conv1_weight": bell_draw(key_list[7], (C, 3, 3, C), (9 * C) ** -0.5, 0.09375, ((0, 4),)),
        "conv1_bias": bell_draw(key_list[8], (C,), 0.3, 1.5, ((0, 4),), jnp.float32),
        "embed_weight": bell_draw(key_list[9], (2, C, EMB), EMB ** -0.5, 0.125, ((1, 4),)),
        "embed_bias": bell_draw(key_list[10], (2, C), 0.3, 1.5, ((1, 4),), jnp.float32),
        "norm2_gain": jnp.clip(1.0 + 0.1 * jax.random.normal(key_list[11], (C,), jnp.float32), 0.5, 1.5),
        "norm2_bias": bell_draw(key_list[12], (C,), 0.3, 1.5, ((0, 4),), jnp.float32),
        "conv2_weight": bell_draw(key_list[13], (C, 3, 3, C), (9 * C) ** -0.5, 0.09375, ((0, 4),)),
        "conv2_bias": bell_draw(key_list[14], (C,), 0.3, 1.5, ((0, 4),), jnp.float32),
        "norm3_gain": jnp.clip(1.0 + 0.1 * jax.random.normal(key_list[15], (C,), jnp.float32), 0.5, 1.5),
        "norm3_bias": bell_draw(key_list[16], (C,), 0.3, 1.5, ((0, 4),), jnp.float32),
        "qkv_weight": bell_draw(key_list[17], (3, C, C), C ** -0.5, 0.25, ((1, 4),)),
        "qkv_bias": bell_draw(key_list[18], (2, C), 0.3, 1.5, ((1, 4),), jnp.float32),
        "encoder_weight": bell_draw(key_list[19], (2, C, ENC), ENC ** -0.5, 0.125, ((1, 4),)),
        "encoder_bias": bell_draw(key_list[20], (2, C), 0.3, 1.5, ((1, 4),), jnp.float32),
        "proj_weight": bell_draw(key_list[21], (C, C), 8 ** -0.5, 2.0, ((0, 4),)),
        "proj_bias": bell_draw(key_list[22], (C,), 0.3, 1.5, ((0, 4),), jnp.float32),
        "out_grad": bell_draw(key_list[23], (MB, C, H * W), 1.0, 6.0, ((1, 4), (2, 8))),
    }


PRECISE = lax.Precision.HIGHEST
EPSILON = 1e-05
MASKED = -1e+30

@jax.custom_vjp
def low(v):
    return lax.optimization_barrier(v.astype(jnp.bfloat16)).astype(jnp.float32)

@jax.custom_vjp
def low_back(v):
    return v

def low_keep(v):
    return (low(v), None)

def low_pass(kept, grad):
    return (grad,)

def back_keep(v):
    return (v, None)

def back_low(kept, grad):
    return (low(grad),)
low.defvjp(low_keep, low_pass)
low_back.defvjp(back_keep, back_low)

def embed_time(timesteps, clip_embed):
    half_width = EMB // 2
    frequency = jnp.exp(-math.log(10000.0) * jnp.arange(half_width, dtype=jnp.float32) / half_width)
    angles = timesteps.astype(jnp.float32)[:, None] * frequency[None, :]
    return jnp.concatenate([jnp.cos(angles), jnp.sin(angles)], axis=1) + clip_embed

def group_norm(values, onehot, gains, biases):
    group_size = C // GROUPS
    counts = lax.optimization_barrier(jnp.sum(onehot, axis=0))[:, None] * group_size
    first_sum = lax.optimization_barrier(jnp.sum(jnp.dot(onehot.T, values, precision=PRECISE).reshape(NCROP, GROUPS, group_size), axis=2))
    second_sum = lax.optimization_barrier(jnp.sum(jnp.dot(onehot.T, values * values, precision=PRECISE).reshape(NCROP, GROUPS, group_size), axis=2))
    averages = first_sum / counts
    inv_std = lax.rsqrt(second_sum / counts - averages * averages + EPSILON)
    mean_pixels = jnp.dot(onehot, jnp.repeat(averages, group_size, axis=1), precision=PRECISE)
    scale_pixels = jnp.dot(onehot, jnp.repeat(inv_std, group_size, axis=1), precision=PRECISE)
    return (values - mean_pixels) * scale_pixels * gains + biases

def conv_masked(hidden, labels, weight, biases):
    padded = jnp.pad(hidden, ((1, 1), (1, 1), (0, 0)))
    label_pad = jnp.pad(labels, 1, constant_values=-1)
    summed = jnp.zeros((H * W, weight.shape[3]), jnp.float32) + biases
    for row_off in range(3):
        for col_off in range(3):
            matching = (label_pad[row_off:row_off + H, col_off:col_off + W] == labels).astype(jnp.float32)
            tap_vals = (padded[row_off:row_off + H, col_off:col_off + W] * matching[:, :, None]).reshape(H * W, C)
            summed = summed + jnp.dot(tap_vals, weight[row_off, col_off], precision=PRECISE)
    return summed

def attend(queries, keys_pix, vals_pix, keys_ctx, vals_ctx, labels):
    pixel_count = queries.shape[0]
    scaling = HD ** (-0.5)
    block_rows = 512 if pixel_count % 512 == 0 else pixel_count
    key_heads = jnp.concatenate([keys_ctx, keys_pix], axis=0).reshape(-1, HEADS, HD)
    val_heads = jnp.concatenate([vals_ctx, vals_pix], axis=0).reshape(-1, HEADS, HD)
    key_labels = jnp.concatenate([jnp.full((CTX,), -1, jnp.int32), labels.astype(jnp.int32)])

    def block(pieces):
        query_block, label_block = pieces
        scores = low_back(jnp.einsum('phd,khd->hpk', query_block, key_heads, precision=PRECISE) * scaling)
        allowed = (label_block[:, None] == key_labels[None, :]) | (key_labels[None, :] < 0)
        scores = jnp.where(allowed[None], scores, MASKED)
        highest = lax.optimization_barrier(jnp.max(scores, axis=-1, keepdims=True))
        exponent = jnp.exp(scores - highest)
        probs = low(exponent / lax.optimization_barrier(jnp.sum(exponent, axis=-1, keepdims=True)))
        return jnp.einsum('hpk,khd->phd', probs, val_heads, precision=PRECISE)
    blocks = pixel_count // block_rows
    result = lax.map(jax.checkpoint(block), (queries.reshape(blocks, block_rows, HEADS, HD), labels.reshape(blocks, block_rows)))
    return result.reshape(pixel_count, C)

def reference(features, crop_ids, timesteps, clip_embed, context, norm1_gain, norm1_bias, conv1_weight, conv1_bias, embed_weight, embed_bias, norm2_gain, norm2_bias, conv2_weight, conv2_bias, norm3_gain, norm3_bias, qkv_weight, qkv_bias, encoder_weight, encoder_bias, proj_weight, proj_bias, out_grad):
    embedded = jax.nn.silu(embed_time(timesteps, clip_embed))
    context_f = context.astype(jnp.float32)
    weights = (norm1_gain, norm1_bias, conv1_weight, conv1_bias, embed_weight, embed_bias, norm2_gain, norm2_bias, conv2_weight, conv2_bias, norm3_gain, norm3_bias, qkv_weight, qkv_bias, encoder_weight, encoder_bias, proj_weight, proj_bias)
    weights = tuple((item.astype(jnp.float32) for item in weights))

    def layer(inputs_cf, gain_one, bias_one, conv_w1_cf, conv_b1, embed_w_cf, embed_b, gain_two, bias_two, conv_w2_cf, conv_b2, gain_three, bias_three, qkv_w_cf, qkv_b, encoder_w_cf, encoder_b, proj_w, proj_b):
        inputs = jnp.transpose(inputs_cf, (0, 2, 1))
        conv_w1 = jnp.transpose(conv_w1_cf, (1, 2, 3, 0))
        conv_w2 = jnp.transpose(conv_w2_cf, (1, 2, 3, 0))
        embed_w = jnp.transpose(embed_w_cf, (2, 0, 1))
        qkv_w = jnp.transpose(qkv_w_cf, (2, 0, 1))
        encoder_w = jnp.transpose(encoder_w_cf, (2, 0, 1))
        outputs = []
        for member in range(MB):
            flat_labels = crop_ids[member].astype(jnp.int32)
            labels = flat_labels.reshape(H, W)
            onehot = (flat_labels[:, None] == jnp.arange(NCROP, dtype=jnp.int32)[None, :]).astype(jnp.float32)
            flattened = inputs[member]
            hidden = low(jax.nn.silu(group_norm(flattened, onehot, gain_one, bias_one)))
            conv_one = low_back(conv_masked(hidden.reshape(H, W, C), labels, conv_w1, conv_b1))
            modulate = jnp.dot(embedded[member][None, :], embed_w.reshape(EMB, 2 * C), precision=PRECISE).reshape(2, C) + embed_b
            normed = group_norm(conv_one, onehot, gain_two, bias_two) * (1.0 + modulate[0]) + modulate[1]
            hidden = low(jax.nn.silu(normed))
            conv_two = low_back(conv_masked(hidden.reshape(H, W, C), labels, conv_w2, conv_b2))
            resid = flattened + conv_two
            attend_in = low(group_norm(resid, onehot, gain_three, bias_three))
            projected = jnp.dot(attend_in, qkv_w.reshape(C, 3 * C), precision=PRECISE).reshape(H * W, 3, C)
            queries = low_back(low(projected[:, 0] + qkv_b[0]))
            keys_pix = low_back(low(projected[:, 1]))
            vals_pix = low_back(low(projected[:, 2] + qkv_b[1]))
            encoded = jnp.dot(context_f[member], encoder_w.reshape(ENC, 2 * C), precision=PRECISE).reshape(CTX, 2, C) + encoder_b
            keys_ctx = low_back(low(encoded[:, 0]))
            vals_ctx = low_back(low(encoded[:, 1]))
            attended = low_back(low(attend(queries, keys_pix, vals_pix, keys_ctx, vals_ctx, flat_labels)))
            outputs.append(resid + jnp.dot(attended, proj_w, precision=PRECISE) + proj_b)
        return jnp.transpose(jnp.stack(outputs), (0, 2, 1))
    result, pullback = jax.vjp(layer, features.astype(jnp.float32), *weights)
    grads = pullback(out_grad.astype(jnp.float32))
    return (result.astype(jnp.bfloat16), grads[0].astype(jnp.bfloat16), grads[1], grads[2], grads[3], grads[4], grads[5], grads[6], grads[7], grads[8], grads[9], grads[10], grads[11], grads[12], grads[13], grads[14], grads[15], grads[16], grads[17], grads[18])
```

```python
import functools
import math

import jax
import jax.numpy as jnp
from jax import lax
from jax.experimental import pallas as pl
from jax.experimental.pallas import tpu as pltpu
from jax.sharding import PartitionSpec as P

C = 512
HD = 64
GSZ = 16
EMB = 2048
W = 64
NCROP = 6
NC = 8
HP = 2 * W
CK = 32
TAPS = [(di, dj) for di in (-1, 0, 1) for dj in (-1, 0, 1)]

PRECISE = lax.Precision.HIGHEST
EPSILON = 1e-05
FAR = 2.0**100
SCORE = HD**-0.5
LOG2E = 1.4426950408889634
F32 = jnp.float32
BF = jnp.bfloat16


def spread(vals, lab):
    acc = vals[:, 0:1]
    for n in range(1, NCROP):
        acc = jnp.where(lab == n, vals[:, n : n + 1], acc)
    return acc


def crop_columns(first, second, lab):
    rows = first.shape[0]
    lane = lax.broadcasted_iota(jnp.int32, (rows, 128), 1)
    acc = jnp.zeros((rows, 128), F32)
    for n in range(NCROP):
        inside = lab == n
        one = jnp.sum(jnp.where(inside, first, 0.0), axis=1, keepdims=True)
        two = jnp.sum(jnp.where(inside, second, 0.0), axis=1, keepdims=True)
        acc = jnp.where(lane == n, one, acc)
        acc = jnp.where(lane == NC + n, two, acc)
    return acc


def put_column(acc, column, at):
    lane = lax.broadcasted_iota(jnp.int32, acc.shape, 1)
    return jnp.where(lane == at, column, acc)


def grouped(vals):
    rows, width = vals.shape
    parts = jnp.sum(vals.reshape(rows // GSZ, GSZ, width), axis=1, keepdims=True)
    return jnp.broadcast_to(parts, (rows // GSZ, GSZ, width)).reshape(rows, width)


def turned(block):
    rows, cols = block.shape
    if rows < 128:
        block = jnp.concatenate([block, jnp.zeros((128 - rows, cols), F32)], axis=0)
    return jnp.transpose(block)


def read_stats(recv_ref, which, cnt):
    members = recv_ref.shape[0]
    block = recv_ref[0, which]
    for g in range(1, members):
        other = recv_ref[g, which]
        block = jnp.concatenate([block[:16] + other[:16], block[16:]], axis=0)
    cols = turned(block)
    sums = grouped(cols[:, :16])
    mean = sums[:, :NC] / cnt
    inv = lax.rsqrt(sums[:, NC:16] / cnt - mean * mean + EPSILON)
    return mean, inv, cols[:, 16:17], cols[:, 17:18], cols[:, 18:19], cols[:, 19:20]


def read_sums(recv_ref, which):
    members = recv_ref.shape[0]
    block = recv_ref[0, which][:16]
    for g in range(1, members):
        block = block + recv_ref[g, which][:16]
    return turned(block)


def affine_of(stats):
    mean, inv, gain, bias, scale, offset = stats
    a = inv * gain * (1.0 + scale)
    b = (bias - mean * inv * gain) * (1.0 + scale) + offset
    return a, b


def sigmoid(v):
    return 0.5 * (1.0 + jnp.tanh(0.5 * v))


def slope(v):
    s = sigmoid(v)
    return s * (1.0 + v * (1.0 - s))


def lay_taps(cols_ref, row, h, masks):
    width = h.shape[1]
    for dj in (-1, 0, 1):
        moved = h if dj == 0 else pltpu.roll(h, (-dj) % width, 1)
        for di in (-1, 0, 1):
            tap = 3 * (di + 1) + dj + 1
            shifted = moved if di == 0 else pltpu.roll(moved, (-W * di) % width, 1)
            cols_ref[tap, pl.ds(row, CK), :] = (shifted * masks[tap : tap + 1, :]).astype(BF)


def conv_tiles(w_ref, cols_ref, out_ref, bias, tile=256):
    width = cols_ref.shape[2]

    def body(i, _):
        at = pl.ds(pl.multiple_of(i * tile, tile), tile)
        acc = jnp.dot(w_ref[0], cols_ref[0, :, at], preferred_element_type=F32)
        for t in range(1, 9):
            acc = acc + jnp.dot(w_ref[t], cols_ref[t, :, at], preferred_element_type=F32)
        out_ref[:, at] = acc if bias is None else acc + bias
        return 0

    lax.fori_loop(0, width // tile, body, 0)


def chunks(count, body):
    lax.fori_loop(0, count, lambda i, c: (body(pl.multiple_of(i * CK, CK)), c)[1], 0)


def send_rows(out_ref, st_ref, params):
    rows = jnp.transpose(st_ref[...])[:16]
    if params is not None:
        rows = jnp.concatenate([rows, params], axis=0)
    for k in range(out_ref.shape[0]):
        out_ref[k] = rows


def k_stats(x_ref, lab_ref, par_ref, out_ref, st_ref):
    n = x_ref.shape[1] - 2 * HP
    lab = lab_ref[:, HP : HP + n]

    def body(i):
        v = x_ref[pl.ds(i, CK), HP : HP + n].astype(F32)
        st_ref[pl.ds(i, CK), :] = crop_columns(v, v * v, lab)

    chunks(x_ref.shape[0] // CK, body)
    send_rows(out_ref, st_ref, par_ref[...])


def k_conv(nch, offs, resid, *refs):
    me_ref, recv_ref, cnt_ref, lab_ref, mask_ref, w_ref, b_ref, par_ref = refs[:8]
    slots = refs[8 : 8 + nch]
    refs = refs[8 + nch :]
    if resid:
        x_ref, refs = refs[0], refs[1:]
        low_ref, pay_ref, h_ref, full_ref = refs[:4]
        refs = refs[4:]
    else:
        low_ref, pay_ref, h_ref = refs[:3]
        refs = refs[3:]
    cols_ref, acc_ref, a_ref, b2_ref, st_ref = refs
    me = me_ref[0]
    ch, e = acc_ref.shape
    n = e - 2 * HP
    lab = lab_ref[...]
    masks = mask_ref[...]
    for c in range(nch):
        a, b = affine_of(read_stats(recv_ref, c, cnt_ref[...]))
        a_ref[c * ch : (c + 1) * ch, :] = a
        b2_ref[c * ch : (c + 1) * ch, :] = b
    for s in range(nch):
        base = pl.multiple_of((me ^ offs[s]) * ch, ch)

        def body(i, s=s, base=base):
            row = pl.multiple_of(base + i, CK)
            v = slots[s][pl.ds(i, CK), :].astype(F32)
            pre = v * spread(a_ref[pl.ds(row, CK), :], lab) + spread(b2_ref[pl.ds(row, CK), :], lab)
            low = (pre * sigmoid(pre)).astype(BF)
            h_ref[pl.ds(row, CK), :] = low
            lay_taps(cols_ref, row, low.astype(F32), masks)

        chunks(ch // CK, body)
    conv_tiles(w_ref, cols_ref, acc_ref, b_ref[...])
    labc = lab[:, HP : HP + n]

    def finish(i):
        if resid:
            v = acc_ref[pl.ds(i, CK), HP : HP + n] + x_ref[pl.ds(i, CK), HP : HP + n].astype(F32)
            full_ref[pl.ds(i, CK), :] = v
            low_ref[pl.ds(i, CK), :] = v.astype(BF)
        else:
            low_ref[pl.ds(i, CK), :] = acc_ref[pl.ds(i, CK), :].astype(BF)
            v = acc_ref[pl.ds(i, CK), HP : HP + n]
        st_ref[pl.ds(i, CK), :] = crop_columns(v, v * v, labc)

    chunks(ch // CK, finish)
    send_rows(pay_ref, st_ref, par_ref[...])


def k_qkv(nch, offs, *refs):
    me_ref, recv_ref, cnt_ref, lab_ref, w_ref, qb_ref, vb_ref = refs[:7]
    slots = refs[7 : 7 + nch]
    res_ref, att_ref, q_ref, k_ref, v_ref, a_ref, b_ref = refs[7 + nch :]
    me = me_ref[0]
    ch, n = q_ref.shape
    lab = lab_ref[:, HP : HP + n]
    for c in range(nch):
        a, b = affine_of(read_stats(recv_ref, c, cnt_ref[...]))
        a_ref[c * ch : (c + 1) * ch, :] = a
        b_ref[c * ch : (c + 1) * ch, :] = b
    for s in range(nch):
        base = pl.multiple_of((me ^ offs[s]) * ch, ch)

        def body(i, s=s, base=base):
            row = pl.multiple_of(base + i, CK)
            low = slots[s][pl.ds(i, CK), :]
            res_ref[pl.ds(row, CK), :] = low
            out = low.astype(F32) * spread(a_ref[pl.ds(row, CK), :], lab) + spread(
                b_ref[pl.ds(row, CK), :], lab
            )
            att_ref[pl.ds(row, CK), :] = out.astype(BF)

        chunks(ch // CK, body)
    tile = 256

    def mul(i, _):
        at = pl.ds(pl.multiple_of(i * tile, tile), tile)
        x = att_ref[:, at]
        q_ref[:, at] = (jnp.dot(w_ref[0], x, preferred_element_type=F32) + qb_ref[...]).astype(BF)
        k_ref[:, at] = jnp.dot(w_ref[1], x, preferred_element_type=F32).astype(BF)
        v_ref[:, at] = (jnp.dot(w_ref[2], x, preferred_element_type=F32) + vb_ref[...]).astype(BF)
        return 0

    lax.fori_loop(0, n // tile, mul, 0)


def k_gout(nch, offs, *refs):
    me_ref, w_ref = refs[:2]
    slots = refs[2 : 2 + nch]
    g_ref, ga_ref = refs[2 + nch :]
    me = me_ref[0]
    ch, n = ga_ref.shape
    for s in range(nch):
        base = pl.multiple_of((me ^ offs[s]) * ch, ch)
        g_ref[pl.ds(base, ch), :] = slots[s][...]
    ga_ref[...] = jnp.dot(w_ref[...], g_ref[:, HP : HP + n], preferred_element_type=F32).astype(BF)


def k_turn(nch, offs, npair, *refs):
    me_ref = refs[0]
    ins = refs[1 : 1 + npair * nch]
    outs = refs[1 + npair * nch : 1 + npair * nch + npair]
    me = me_ref[0]
    for p in range(npair):
        scr = refs[1 + npair * nch + npair + p]
        taps = outs[p].shape[0]
        for t in range(taps):
            for s in range(nch):
                ref = ins[p * nch + s]
                rows = ref.shape[1]
                base = pl.multiple_of((me ^ offs[s]) * rows, rows)
                scr[pl.ds(base, rows), :] = ref[t].astype(F32)
            outs[p][t] = jnp.transpose(scr[...]).astype(BF)


def nt(a, b):
    return lax.dot_general(a, b, (((1,), (1,)), ((), ())), preferred_element_type=F32)


def tn(a, b):
    return lax.dot_general(a, b, (((0,), (0,)), ((), ())), preferred_element_type=F32)


def k_attend(kmap, vmap, nk, nv, *refs):
    q_ref, ga_ref, oneq_ref, onek_ref, ck_ref, cv_ref = refs[:6]
    kparts = refs[6 : 6 + nk]
    vparts = refs[6 + nk : 6 + nk + nv]
    out_ref, dq_ref, dk_ref, dv_ref, dck_ref, dcv_ref = refs[6 + nk + nv : 12 + nk + nv]
    ks_ref, vs_ref, e_ref, s_ref, ak_ref, av_ref, ga_s, o_s, dq_s = refs[12 + nk + nv :]
    ch, n = q_ref.shape
    heads = ch // HD
    slots = len(kmap)
    keys = slots * n
    tq = e_ref.shape[0]
    con = SCORE * LOG2E
    for h in range(heads):
        hs = slice(h * HD, (h + 1) * HD)
        for s in range(slots):
            i, j = kmap[s]
            ks_ref[h, 0:HD, s * n : (s + 1) * n] = kparts[i][j, hs, :]
            i, j = vmap[s]
            vs_ref[h, :, s * n : (s + 1) * n] = vparts[i][j, hs, :]
        ks_ref[h, HD : HD + 16, 0:keys] = onek_ref[...]
        ks_ref[h, 0:HD, keys:] = ck_ref[hs, :]
        ks_ref[h, HD : HD + 16, keys:] = jnp.zeros((16, 128), BF)
        vs_ref[h, :, keys:] = cv_ref[hs, :]
    ak_ref[...] = jnp.zeros_like(ak_ref)
    av_ref[...] = jnp.zeros_like(av_ref)
    spans = [(s * n, n) for s in range(slots)] + [(keys, 128)]

    for h in range(heads):
        hs = slice(h * HD, (h + 1) * HD)

        def block(b, _, h=h, hs=hs):
            at = pl.ds(pl.multiple_of(b * tq, tq), tq)
            qb = q_ref[hs, at]
            gb = ga_ref[hs, at]
            qa = jnp.transpose(
                jnp.concatenate([qb.astype(F32), oneq_ref[:, at].astype(F32)], axis=0)
            ).astype(BF)
            gt = jnp.transpose(gb.astype(F32))
            gtb = gt.astype(BF)
            top = jnp.full((tq, 128), -jnp.inf, F32)
            for k0, kn in spans:
                sc = jnp.dot(qa, ks_ref[h, :, k0 : k0 + kn], preferred_element_type=F32)
                s_ref[:, k0 : k0 + kn] = sc
                for u in range(kn // 128):
                    top = jnp.maximum(top, sc[:, u * 128 : (u + 1) * 128])
            top = jnp.max(top, axis=1, keepdims=True) * con
            tot = jnp.zeros((tq, 128), F32)
            acc = jnp.zeros((tq, HD), F32)
            for k0, kn in spans:
                ex = jnp.exp2(s_ref[:, k0 : k0 + kn] * con - top)
                for u in range(kn // 128):
                    tot = tot + ex[:, u * 128 : (u + 1) * 128]
                exb = ex.astype(BF)
                e_ref[:, k0 : k0 + kn] = exb
                acc = acc + nt(exb, vs_ref[h, :, k0 : k0 + kn])
            inv = 1.0 / jnp.sum(tot, axis=1, keepdims=True)
            acc = acc * inv
            delta = jnp.sum(acc * gt, axis=1, keepdims=True)
            out_ref[hs, at] = jnp.transpose(acc).astype(BF)
            ql = jnp.transpose(qa[:, :HD].astype(F32) * (inv * SCORE)).astype(BF)
            gl = jnp.transpose(gt * inv).astype(BF)
            dq = jnp.zeros((tq, HD), F32)
            for k0, kn in spans:
                dp = jnp.dot(gtb, vs_ref[h, :, k0 : k0 + kn], preferred_element_type=F32)
                exb = e_ref[:, k0 : k0 + kn]
                ds = (exb.astype(F32) * (dp - delta)).astype(BF)
                dq = dq + nt(ds, ks_ref[h, 0:HD, k0 : k0 + kn])
                ak_ref[hs, k0 : k0 + kn] += jnp.dot(ql, ds, preferred_element_type=F32)
                av_ref[hs, k0 : k0 + kn] += jnp.dot(gl, exb, preferred_element_type=F32)
            dq_ref[hs, at] = jnp.transpose(dq * (inv * SCORE)).astype(BF)
            return 0

        lax.fori_loop(0, n // tq, block, 0)
    for s in range(slots):
        dk_ref[s] = ak_ref[:, s * n : (s + 1) * n].astype(BF)
        dv_ref[s] = av_ref[:, s * n : (s + 1) * n].astype(BF)
    dck_ref[...] = ak_ref[:, keys:]
    dcv_ref[...] = av_ref[:, keys:]


def k_proj(nch, offs, *refs):
    me_ref, g_ref, res_ref, pb_ref = refs[:4]
    atts = refs[4 : 4 + nch]
    pws = refs[4 + nch : 4 + 2 * nch]
    out_ref, wg_ref, st_ref, att_s, pw_s = refs[4 + 2 * nch :]
    me = me_ref[0]
    ch, n = res_ref.shape
    for s in range(nch):
        base = pl.multiple_of((me ^ offs[s]) * ch, ch)
        att_s[pl.ds(base, ch), :] = atts[s][...]
        pw_s[pl.ds(base, ch), :] = pws[s][...].astype(F32)
    pw = jnp.transpose(pw_s[...]).astype(BF)
    mixed = jnp.dot(pw, att_s[...], preferred_element_type=F32)
    out_ref[...] = (res_ref[...] + mixed + pb_ref[...]).astype(BF)
    wg_ref[...] = nt(atts[0][...], g_ref[:, HP : HP + n]).astype(BF)
    own = g_ref[pl.ds(pl.multiple_of(me * ch, ch), ch), HP : HP + n].astype(F32)
    acc = put_column(jnp.zeros((ch, 128), F32), jnp.sum(own, axis=1, keepdims=True), 0)
    st_ref[...] = jnp.transpose(acc)[:8]


def k_gattend(nch, offs, *refs):
    me_ref, recv_ref, cnt_ref, lab_ref, w_ref, res_ref = refs[:6]
    slots = [refs[6 + j * nch : 6 + (j + 1) * nch] for j in range(3)]
    ga_ref, pay_ref, d_s, acc_ref, a_ref, b_ref, st_ref = refs[6 + 3 * nch :]
    me = me_ref[0]
    n = ga_ref.shape[1]
    ch = C // nch
    lab = lab_ref[:, HP : HP + n]
    for c in range(nch):
        mean, inv = read_stats(recv_ref, c, cnt_ref[...])[:2]
        a_ref[c * ch : (c + 1) * ch, :] = inv
        b_ref[c * ch : (c + 1) * ch, :] = -mean * inv
    for j in range(3):
        for s in range(nch):
            base = pl.multiple_of((me ^ offs[s]) * ch, ch)
            d_s[j, pl.ds(base, ch), :] = slots[j][s][...]
    tile = 256

    def mul(i, _):
        at = pl.ds(pl.multiple_of(i * tile, tile), tile)
        acc = jnp.dot(w_ref[0], d_s[0, :, at], preferred_element_type=F32)
        acc = acc + jnp.dot(w_ref[1], d_s[1, :, at], preferred_element_type=F32)
        acc_ref[:, at] = acc + jnp.dot(w_ref[2], d_s[2, :, at], preferred_element_type=F32)
        return 0

    lax.fori_loop(0, n // tile, mul, 0)

    def body(i):
        ga = acc_ref[pl.ds(i, CK), :]
        ga_ref[pl.ds(i, CK), :] = ga.astype(BF)
        normed = res_ref[pl.ds(i, CK), :].astype(F32) * spread(
            a_ref[pl.ds(i, CK), :], lab
        ) + spread(b_ref[pl.ds(i, CK), :], lab)
        st_ref[pl.ds(i, CK), :] = crop_columns(ga, ga * normed, lab)

    chunks(C // CK, body)
    rows = jnp.transpose(st_ref[...])[:16]
    for k in range(pay_ref.shape[0]):
        pay_ref[k] = rows


def k_qkvgrad(dq_ref, dk_ref, dv_ref, att_ref, wg_ref, st_ref):
    x = att_ref[...]
    ch = dq_ref.shape[0]
    acc = jnp.zeros((ch, 128), F32)
    for j, ref in enumerate((dq_ref, dk_ref, dv_ref)):
        d = ref[...]
        wg_ref[j] = nt(d, x).astype(BF)
        acc = put_column(acc, jnp.sum(d.astype(F32), axis=1, keepdims=True), j)
    st_ref[...] = jnp.transpose(acc)[:8]


def norm_back(mean, inv, gain, t1, t2, cnt):
    m1 = grouped(gain * t1) / cnt
    m2 = grouped(gain * t2) / cnt
    return inv * gain, -inv * inv * m2, inv * (mean * inv * m2 - m1)


def k_back2(nch, *refs):
    (me_ref, recv3_ref, recvt_ref, recv2_ref, cnt_ref, lab_ref, mask_ref, w_ref) = refs[:8]
    ga_ref, gat_ref, gab_ref, res_ref, rest_ref, resb_ref, g_ref, c1_ref = refs[8:16]
    gp_ref, pay_ref, gc_ref, gr_ref = refs[16:20]
    cols_ref, acc_ref, a_ref, b_ref, c_ref, st_ref, full_ref = refs[20:]
    me = me_ref[0]
    ch, e = acc_ref.shape
    n = e - 2 * HP
    lab = lab_ref[...]
    masks = mask_ref[...]
    cnt = cnt_ref[...]
    tsum = recvt_ref[0]
    for g in range(1, recvt_ref.shape[0]):
        tsum = tsum + recvt_ref[g]
    for c in range(nch):
        sl = slice(c * ch, (c + 1) * ch)
        mean, inv, gain = read_stats(recv3_ref, c, cnt)[:3]
        t = turned(tsum[:, sl])
        a, b, cc = norm_back(mean, inv, gain, t[:, :NC], t[:, NC:16], cnt)
        a_ref[sl, :] = a
        b_ref[sl, :] = b
        c_ref[sl, :] = cc

    def body(i):
        row = pl.ds(i, CK)
        ga = jnp.concatenate([gat_ref[row, :], ga_ref[row, :], gab_ref[row, :]], axis=1).astype(F32)
        v = jnp.concatenate([rest_ref[row, :], res_ref[row, :], resb_ref[row, :]], axis=1).astype(
            F32
        )
        gr = (
            g_ref[row, :].astype(F32)
            + ga * spread(a_ref[row, :], lab)
            + v * spread(b_ref[row, :], lab)
            + spread(c_ref[row, :], lab)
        )
        full_ref[row, :] = gr
        lay_taps(cols_ref, i, gr.astype(BF).astype(F32), masks)

    chunks(C // CK, body)
    own = pl.multiple_of(me * ch, ch)
    gr_ref[...] = full_ref[pl.ds(own, ch), HP : HP + n]
    conv_tiles(w_ref, cols_ref, acc_ref, None)
    stats = None
    mean, inv, gain, bias, scale, offset = read_stats_dyn(recv2_ref, me, cnt)
    a, b = affine_of((mean, inv, gain, bias, scale, offset))
    a_ref[0:ch, :] = a
    b_ref[0:ch, :] = b
    c_ref[0:ch, :] = inv
    a_ref[ch : 2 * ch, :] = -mean * inv

    def finish(i):
        row = pl.ds(i, CK)
        v = c1_ref[row, :].astype(F32)
        pre = v * spread(a_ref[row, :], lab) + spread(b_ref[row, :], lab)
        gp = acc_ref[row, :] * slope(pre)
        gp_ref[row, :] = gp.astype(BF)
        labc = lab[:, HP : HP + n]
        normed = v[:, HP : HP + n] * spread(c_ref[row, :], labc) + spread(
            a_ref[pl.ds(pl.multiple_of(ch + i, CK), CK), :], labc
        )
        gpc = gp[:, HP : HP + n]
        low = gr_ref[row, :].astype(BF)
        gc_ref[row, :] = low
        acc = crop_columns(gpc, gpc * normed, labc)
        st_ref[row, :] = acc

    chunks(ch // CK, finish)
    send_rows(pay_ref, st_ref, None)


def read_stats_dyn(recv_ref, which, cnt):
    members = recv_ref.shape[0]
    block = recv_ref[0, which]
    for g in range(1, members):
        other = recv_ref[g, which]
        block = jnp.concatenate([block[:16] + other[:16], block[16:]], axis=0)
    cols = turned(block)
    sums = grouped(cols[:, :16])
    mean = sums[:, :NC] / cnt
    inv = lax.rsqrt(sums[:, NC:16] / cnt - mean * mean + EPSILON)
    return mean, inv, cols[:, 16:17], cols[:, 17:18], cols[:, 18:19], cols[:, 19:20]


def wgrad_body(gc, h_ref, masks, cols_ref, wg_ref):
    n = gc.shape[1]

    def body(i):
        lay_taps(cols_ref, i, h_ref[pl.ds(i, CK), :].astype(F32), masks)

    chunks(C // CK, body)
    for t in range(9):
        wg_ref[t] = nt(gc, cols_ref[t, :, HP : HP + n]).astype(BF)


def k_wgrad2(mask_ref, gc_ref, h_ref, wg_ref, st_ref, cols_ref):
    gc = gc_ref[...]
    wgrad_body(gc, h_ref, mask_ref[...], cols_ref, wg_ref)
    acc = jnp.zeros((gc.shape[0], 128), F32)
    acc = put_column(acc, jnp.sum(gc.astype(F32), axis=1, keepdims=True), 0)
    st_ref[...] = jnp.transpose(acc)[:8]


def conv1_back(recv2_ref, recvu_ref, which, cnt):
    mean, inv, gain, _, scale, _ = read_stats_dyn(recv2_ref, which, cnt)
    u = read_sums(recvu_ref, which)
    return norm_back(mean, inv, gain * (1.0 + scale), u[:, :NC], u[:, NC:16], cnt)


def k_wgrad1(
    me_ref, recv2_ref, recvu_ref, cnt_ref, lab_ref, mask_ref, gp_ref, c1_ref, h_ref, wg_ref, st_ref,
    cols_ref, gc_ref,
):
    n = gc_ref.shape[1]
    lab = lab_ref[:, HP : HP + n]
    a, b, c = conv1_back(recv2_ref, recvu_ref, me_ref[0], cnt_ref[...])
    gc = (
        gp_ref[:, HP : HP + n].astype(F32) * spread(a, lab)
        + c1_ref[:, HP : HP + n].astype(F32) * spread(b, lab)
        + spread(c, lab)
    ).astype(BF)
    gc_ref[...] = gc
    wgrad_body(gc, h_ref, mask_ref[...], cols_ref, wg_ref)
    acc = jnp.zeros((gc.shape[0], 128), F32)
    acc = put_column(acc, jnp.sum(gc.astype(F32), axis=1, keepdims=True), 0)
    st_ref[...] = jnp.transpose(acc)[:8]


def k_back1(nch, offs, *refs):
    me_ref, recv1_ref, recv2_ref, recvu_ref, cnt_ref, lab_ref, mask_ref, w_ref, x_ref, small_ref = (
        refs[:10]
    )
    gps = refs[10 : 10 + nch]
    c1s = refs[10 + nch : 10 + 2 * nch]
    gp1_ref, pay_ref = refs[10 + 2 * nch : 12 + 2 * nch]
    cols_ref, acc_ref, a_ref, b_ref, c_ref, st_ref = refs[12 + 2 * nch :]
    me = me_ref[0]
    ch, e = acc_ref.shape
    n = e - 2 * HP
    lab = lab_ref[...]
    masks = mask_ref[...]
    cnt = cnt_ref[...]
    for c in range(nch):
        sl = slice(c * ch, (c + 1) * ch)
        a, b, cc = conv1_back(recv2_ref, recvu_ref, c, cnt)
        a_ref[sl, :] = a
        b_ref[sl, :] = b
        c_ref[sl, :] = cc
    for s in range(nch):
        base = pl.multiple_of((me ^ offs[s]) * ch, ch)

        def body(i, s=s, base=base):
            row = pl.multiple_of(base + i, CK)
            at = pl.ds(row, CK)
            gc = (
                gps[s][pl.ds(i, CK), :].astype(F32) * spread(a_ref[at, :], lab)
                + c1s[s][pl.ds(i, CK), :].astype(F32) * spread(b_ref[at, :], lab)
                + spread(c_ref[at, :], lab)
            )
            lay_taps(cols_ref, row, gc.astype(BF).astype(F32), masks)

        chunks(ch // CK, body)
    conv_tiles(w_ref, cols_ref, acc_ref, None)
    stats = read_stats_dyn(recv1_ref, me, cnt)
    a, b = affine_of(stats)
    a_ref[0:ch, :] = a
    b_ref[0:ch, :] = b
    c_ref[0:ch, :] = stats[1]
    c_ref[ch : 2 * ch, :] = -stats[0] * stats[1]
    labc = lab[:, HP : HP + n]

    def finish(i):
        row = pl.ds(i, CK)
        v = x_ref[row, HP : HP + n].astype(F32)
        pre = v * spread(a_ref[row, :], labc) + spread(b_ref[row, :], labc)
        gp = acc_ref[row, HP : HP + n] * slope(pre)
        gp1_ref[row, :] = gp
        normed = v * spread(c_ref[row, :], labc) + spread(
            c_ref[pl.ds(pl.multiple_of(ch + i, CK), CK), :], labc
        )
        st_ref[row, :] = crop_columns(gp, gp * normed, labc)

    chunks(ch // CK, finish)
    send_rows(pay_ref, st_ref, small_ref[...])


def k_last(me_ref, recv1_ref, recvv_ref, cnt_ref, lab_ref, gp_ref, x_ref, gr_ref, out_ref, sum_ref):
    ch, n = gp_ref.shape
    half = recvv_ref.shape[0] // 2
    lab = lab_ref[:, HP : HP + n]
    for m in range(2):
        tot = recvv_ref[m * half]
        for g in range(1, half):
            tot = tot + recvv_ref[m * half + g]
        sum_ref[m] = tot
    cnt = cnt_ref[...]
    mean, inv, gain = read_stats_dyn(recv1_ref, me_ref[0], cnt)[:3]
    v = turned(sum_ref[me_ref[1]][:16])
    a, b, c = norm_back(mean, inv, gain, v[:, :NC], v[:, NC:16], cnt)
    out = (
        gr_ref[...]
        + gp_ref[...] * spread(a, lab)
        + x_ref[:, HP : HP + n].astype(F32) * spread(b, lab)
        + spread(c, lab)
    )
    out_ref[...] = out.astype(BF)


SM = pl.BlockSpec(memory_space=pltpu.SMEM)
VM = pl.BlockSpec(memory_space=pltpu.VMEM)


def call(kernel, args, outs, scratch=(), smem=1, flops=0, limit=48):
    bytes_all = sum(math.prod(a.shape) * a.dtype.itemsize for a in list(args) + list(outs))
    return pl.pallas_call(
        kernel,
        out_shape=tuple(outs),
        in_specs=[SM] * smem + [VM] * (len(args) - smem),
        out_specs=tuple(VM for _ in outs),
        scratch_shapes=list(scratch),
        compiler_params=pltpu.CompilerParams(vmem_limit_bytes=limit * 2**20),
        cost_estimate=pl.CostEstimate(flops=flops, bytes_accessed=bytes_all, transcendentals=0),
    )(*args)


def sd(shape, dtype):
    return jax.ShapeDtypeStruct(shape, dtype)


def swap(x, axis, bit):
    count = lax.axis_size(axis)
    return lax.ppermute(x, axis, [(i, i ^ bit) for i in range(count)])


def bits_of(count):
    return [1 << i for i in range(count.bit_length() - 1)]


def offsets(count):
    offs = [0]
    for bit in reversed(bits_of(count)):
        offs = offs + [o ^ bit for o in offs]
    return offs


def gather_ch(x):
    slots = [x]
    for bit in reversed(bits_of(lax.axis_size("ch"))):
        slots = slots + [swap(s, "ch", bit) for s in slots]
    return slots


def gather_rows(x, bits):
    parts, places, offs = [x[None]], [(0, 0)], [0]
    for bit in bits:
        whole = parts[0] if len(parts) == 1 else jnp.concatenate(parts, axis=0)
        base = len(parts)
        parts = parts + [swap(whole, "rows", bit)]
        places = places + [(base, i) for i in range(len(offs))]
        offs = offs + [o ^ bit for o in offs]
    table = dict(zip(offs, places, strict=True))
    return parts, [table[o] for o in range(len(offs))]


def scatter_rows(x, bits):
    offs = list(range(x.shape[0]))
    for bit in bits:
        keep = [i for i, o in enumerate(offs) if not o & bit]
        give = [offs.index(offs[i] ^ bit) for i in keep]
        mine = jnp.stack([x[i] for i in keep])
        theirs = jnp.stack([x[i] for i in give])
        got = swap(theirs, "rows", bit)
        x = (mine.astype(F32) + got.astype(F32)).astype(BF)
        offs = [offs[i] for i in keep]
    return x[0]


def per_device(
    features,
    crop_ids,
    timesteps,
    clip_embed,
    context,
    norm1_gain,
    norm1_bias,
    conv1_weight,
    conv1_bias,
    embed_weight,
    embed_bias,
    norm2_gain,
    norm2_bias,
    conv2_weight,
    conv2_bias,
    norm3_gain,
    norm3_bias,
    qkv_weight,
    qkv_bias,
    encoder_weight,
    encoder_bias,
    proj_weight,
    proj_bias,
    out_grad,
):
    batches, ch, pixels = features.shape
    rows_n = lax.axis_size("rows")
    nch = lax.axis_size("ch")
    half = rows_n // 2
    r = lax.axis_index("rows")
    me = lax.axis_index("ch")
    m, j = r // half, r % half
    even = r % 2 == 0
    n = 2 * pixels
    e = n + 2 * HP
    local_rows = n // W
    copies = half * nch
    offs = offsets(nch)
    flat = rows_n * nch
    teams = [list(range(copies)), list(range(copies, flat))]
    halves = [list(range(half)), list(range(half, rows_n))]
    me1 = jnp.reshape(me, (1,)).astype(jnp.int32)

    evens, odds = range(0, rows_n, 2), range(1, rows_n, 2)
    first_perm = [(i, i // 2) for i in evens] + [(i, half + i // 2) for i in odds]
    second_perm = [(i, half + i // 2) for i in evens] + [(i, i // 2) for i in odds]

    def halo_perm(up, down):
        pairs = [(i, up * half + i // 2 - 1) for i in evens if i // 2 > 0]
        return pairs + [(i, down * half + i // 2 + 1) for i in odds if i // 2 < half - 1]

    def reshard(x, halo):
        a = jnp.where(even, x[0], x[1])
        b = jnp.where(even, x[1], x[0])
        one = lax.ppermute(a, "rows", first_perm)
        two = lax.ppermute(b, "rows", second_perm)
        low = jnp.where(m == 0, one, two)
        high = jnp.where(m == 0, two, one)
        edge = jnp.where(even, x[:, :, :HP], x[:, :, pixels - HP :])
        three = lax.ppermute(jnp.where(even, edge[0], edge[1]), "rows", halo_perm(0, 1))
        four = lax.ppermute(jnp.where(even, edge[1], edge[0]), "rows", halo_perm(1, 0))
        below = jnp.where(m == 0, three, four)
        above = jnp.where(m == 0, four, three)
        return jnp.concatenate([above, low, high, below], axis=1)

    def reshard_back(y):
        low, high = y[:, :pixels], y[:, pixels:]
        one = lax.ppermute(jnp.where(m == 0, low, high), "rows", [(b, a) for a, b in first_perm])
        two = lax.ppermute(jnp.where(m == 0, high, low), "rows", [(b, a) for a, b in second_perm])
        return jnp.stack([jnp.where(even, one, two), jnp.where(even, two, one)])

    def to_next(x):
        return lax.ppermute(
            x, "rows", [(i, i + 1) for i in range(rows_n - 1) if i % half != half - 1]
        )

    def to_prev(x):
        return lax.ppermute(x, "rows", [(i, i - 1) for i in range(1, rows_n) if i % half != 0])

    def team_exchange(x):
        got = lax.all_to_all(x, ("rows", "ch"), 0, 0, axis_index_groups=teams)
        return got.reshape((half, nch) + x.shape[1:])

    ids = lax.dynamic_index_in_dim(crop_ids, m, 0, keepdims=False)
    grid = jnp.pad(ids.reshape(-1, W), ((2, 2), (0, 0)), constant_values=-1)
    lab20 = lax.dynamic_slice_in_dim(grid, j * local_rows, local_rows + 4, 0)
    near = jnp.pad(lab20, 1, constant_values=-2)
    height = local_rows + 4
    masks = jnp.stack(
        [
            (near[1 + di : 1 + di + height, 1 + dj : 1 + dj + W] == lab20) & (lab20 >= 0)
            for di, dj in TAPS
        ]
    ).astype(F32)
    masks = jnp.pad(masks.reshape(9, e), ((0, 7), (0, 0)))
    lab = lab20.reshape(1, e)
    crops = jnp.arange(NC, dtype=jnp.int32)
    counted = jnp.sum((ids[None, :] == crops[:, None]).astype(F32), axis=1)
    cnt = jnp.maximum(counted, 1.0)[None, :] * GSZ

    x_own = reshard(features, True)

    half_width = EMB // 2
    frequency = jnp.exp(-math.log(10000.0) * jnp.arange(half_width, dtype=F32) / half_width)
    angles = timesteps.astype(F32)[:, None] * frequency[None, :]
    embedded = jax.nn.silu(
        jnp.concatenate([jnp.cos(angles), jnp.sin(angles)], axis=1) + clip_embed
    )
    modulation = (
        jnp.einsum("be,jce->bjc", embedded, embed_weight.astype(F32), precision=PRECISE)
        + embed_bias
    )
    mod_here = lax.dynamic_index_in_dim(modulation, m, 0, keepdims=False)
    zero = jnp.zeros((1, ch), F32)

    def params(*rows):
        given = [x.reshape(1, ch).astype(F32) for x in rows]
        return jnp.concatenate(given + [zero] * (8 - len(given)), axis=0)

    par1 = params(norm1_gain, norm1_bias)
    par2 = params(norm2_gain, norm2_bias, mod_here[0], mod_here[1])
    par3 = params(norm3_gain, norm3_bias)

    x_slots = gather_ch(x_own)
    pay = sd((copies, 24, ch), F32)
    st = pltpu.VMEM((ch, 128), F32)
    (pay1,) = call(k_stats, (x_own, lab, par1), (pay,), [st], smem=0)
    recv1 = team_exchange(pay1)
    w1 = conv1_weight.transpose(1, 2, 0, 3).reshape(9, ch, C)
    w2 = conv2_weight.transpose(1, 2, 0, 3).reshape(9, ch, C)
    conv_scratch = [
        pltpu.VMEM((9, C, e), BF),
        pltpu.VMEM((ch, e), F32),
        pltpu.VMEM((C, NC), F32),
        pltpu.VMEM((C, NC), F32),
    ]
    conv_flops = 2 * 9 * ch * C * e
    low1, pay2, h1 = call(
        functools.partial(k_conv, nch, offs, False),
        (me1, recv1, cnt, lab, masks, w1, conv1_bias[:, None], par2, *x_slots),
        (sd((ch, e), BF), pay, sd((C, e), BF)),
        conv_scratch + [st],
        flops=conv_flops,
    )
    c1_slots = gather_ch(low1)
    recv2 = team_exchange(pay2)
    low2, pay3, h2, resid = call(
        functools.partial(k_conv, nch, offs, True),
        (me1, recv2, cnt, lab, masks, w2, conv2_bias[:, None], par3, *c1_slots, x_own),
        (sd((ch, n), BF), pay, sd((C, e), BF), sd((ch, n), F32)),
        conv_scratch + [st],
        flops=conv_flops,
    )
    r_slots = gather_ch(low2)
    recv3 = team_exchange(pay3)
    res_full, att_in, q, k, v = call(
        functools.partial(k_qkv, nch, offs),
        (me1, recv3, cnt, lab, qkv_weight, qkv_bias[0][:, None], qkv_bias[1][:, None], *r_slots),
        (sd((C, n), BF), sd((C, n), BF), sd((ch, n), BF), sd((ch, n), BF), sd((ch, n), BF)),
        [pltpu.VMEM((C, NC), F32), pltpu.VMEM((C, NC), F32)],
        flops=2 * 3 * ch * C * n,
    )
    row_bits = bits_of(half)
    k_parts, k_map = gather_rows(k, row_bits)
    v_parts, v_map = gather_rows(v, list(reversed(row_bits)))

    g_slots = gather_ch(reshard(out_grad, True))
    g_full, grad_att = call(
        functools.partial(k_gout, nch, offs),
        (me1, proj_weight, *g_slots),
        (sd((C, e), BF), sd((ch, n), BF)),
        flops=2 * ch * C * n,
    )
    sliced = []
    for w in (w1, w2):
        flipped = w[::-1]
        for o in offs:
            piece = lax.dynamic_slice_in_dim(flipped, (me ^ o) * ch, ch, 2)
            sliced.append(piece if o == 0 else swap(piece, "ch", o))
    w1t, w2t = call(
        functools.partial(k_turn, nch, offs, 2),
        (me1, *sliced),
        (sd((9, ch, C), BF), sd((9, ch, C), BF)),
        [pltpu.VMEM((C, ch), F32)] * 2,
    )
    (wqt,) = call(
        functools.partial(k_turn, nch, offs, 1),
        (me1, *gather_ch(qkv_weight)),
        (sd((3, C, C), BF),),
        [pltpu.VMEM((C, C), F32)],
    )
    pw_slots = []
    for o in offs:
        piece = lax.dynamic_slice_in_dim(proj_weight, (me ^ o) * ch, ch, 1)
        pw_slots.append(piece if o == 0 else swap(piece, "ch", o))
    ctx = lax.dynamic_index_in_dim(context, m, 0, keepdims=False)
    encoded = (
        jnp.einsum("te,jde->jdt", ctx, encoder_weight, preferred_element_type=F32)
        + encoder_bias[:, :, None]
    ).astype(BF)

    tiles = ids.reshape(half, n)
    key_ids = jnp.concatenate(
        [lax.dynamic_slice_in_dim(tiles, j ^ o, 1, 0) for o in range(half)], axis=1
    )
    crops16 = jnp.arange(16, dtype=jnp.int32)[:, None]
    one_k = jnp.where((key_ids == crops16) | (crops16 >= NC), 0.0, -FAR).astype(BF)
    one_q = (lab[:, HP : HP + n] == crops16).astype(BF)
    heads = ch // HD
    keys = half * n + 128
    tq = 256 if half * n <= 4096 else 128
    attended, dq, dk_all, dv_all, dck, dcv = call(
        functools.partial(k_attend, k_map, v_map, len(k_parts), len(v_parts)),
        (q, grad_att, one_q, one_k, encoded[0], encoded[1], *k_parts, *v_parts),
        (
            sd((ch, n), BF),
            sd((ch, n), BF),
            sd((half, ch, n), BF),
            sd((half, ch, n), BF),
            sd((ch, 128), F32),
            sd((ch, 128), F32),
        ),
        [
            pltpu.VMEM((heads, HD + 16, keys), BF),
            pltpu.VMEM((heads, HD, keys), BF),
            pltpu.VMEM((tq, keys), BF),
            pltpu.VMEM((tq, keys), F32),
            pltpu.VMEM((ch, keys), F32),
            pltpu.VMEM((ch, keys), F32),
            pltpu.VMEM((8, 128), F32),
            pltpu.VMEM((8, 128), F32),
            pltpu.VMEM((8, 128), F32),
        ],
        smem=0,
        flops=6 * 2 * heads * n * keys * HD,
        limit=60,
    )
    dk = scatter_rows(dk_all, list(reversed(row_bits)))
    dv = scatter_rows(dv_all, row_bits)
    dq_slots = gather_ch(dq)
    a_slots = gather_ch(attended)
    out_own, proj_wg, proj_st = call(
        functools.partial(k_proj, nch, offs),
        (me1, g_full, resid, proj_bias[:, None], *a_slots, *pw_slots),
        (sd((ch, n), BF), sd((ch, C), BF), sd((8, ch), F32)),
        [pltpu.VMEM((C, n), BF), pltpu.VMEM((C, ch), F32)],
        flops=4 * ch * C * n,
    )
    output = reshard_back(out_own)
    dk_slots = gather_ch(dk)
    dv_slots = gather_ch(dv)
    ga, pay_t = call(
        functools.partial(k_gattend, nch, offs),
        (me1, recv3, cnt, lab, wqt, res_full, *dq_slots, *dk_slots, *dv_slots),
        (sd((C, n), BF), sd((half, 16, C), F32)),
        [
            pltpu.VMEM((3, C, n), BF),
            pltpu.VMEM((C, n), F32),
            pltpu.VMEM((C, NC), F32),
            pltpu.VMEM((C, NC), F32),
            pltpu.VMEM((C, 128), F32),
        ],
        flops=2 * 3 * C * C * n,
    )
    recv_t = lax.all_to_all(pay_t, "rows", 0, 0, axis_index_groups=halves)
    res_top, res_bot = to_next(res_full[:, n - HP :]), to_prev(res_full[:, :HP])
    ga_top, ga_bot = to_next(ga[:, n - HP :]), to_prev(ga[:, :HP])
    qkv_wg, qkv_st = call(
        k_qkvgrad,
        (dq, dk, dv, att_in),
        (sd((3, ch, C), BF), sd((8, ch), F32)),
        smem=0,
        flops=2 * 3 * ch * C * n,
    )
    ctx_part = jnp.stack([dck, dcv])
    ctx_both = jnp.stack([jnp.where(m == i, ctx_part, 0.0) for i in range(batches)]).astype(BF)
    proj_sum, ctx_sum, qkv_sum = lax.psum((proj_wg, ctx_both, qkv_wg), "rows")

    gp2, pay_u, gc2, grad_resid = call(
        functools.partial(k_back2, nch),
        (
            me1, recv3, recv_t, recv2, cnt, lab, masks, w2t,
            ga, ga_top, ga_bot, res_full, res_top, res_bot, g_full, low1,
        ),
        (sd((ch, e), BF), sd((copies, 16, ch), F32), sd((ch, n), BF), sd((ch, n), F32)),
        [
            pltpu.VMEM((9, C, e), BF),
            pltpu.VMEM((ch, e), F32),
            pltpu.VMEM((C, NC), F32),
            pltpu.VMEM((C, NC), F32),
            pltpu.VMEM((C, NC), F32),
            st,
            pltpu.VMEM((C, e), F32),
        ],
        flops=conv_flops,
    )
    gp_slots = gather_ch(gp2)
    recv_u = team_exchange(pay_u)
    wg2, wg2_st = call(
        k_wgrad2,
        (masks, gc2, h2),
        (sd((9, ch, C), BF), sd((8, ch), F32)),
        [pltpu.VMEM((9, C, e), BF)],
        smem=0,
        flops=conv_flops,
    )
    wg2_sum = lax.psum(wg2, "rows")

    wg1, wg1_st = call(
        k_wgrad1,
        (me1, recv2, recv_u, cnt, lab, masks, gp2, low1, h1),
        (sd((9, ch, C), BF), sd((8, ch), F32)),
        [pltpu.VMEM((9, C, e), BF), pltpu.VMEM((ch, n), BF)],
        flops=conv_flops,
    )
    wg1_sum = lax.psum(wg1, "rows")
    t_own = lax.dynamic_slice_in_dim(pay_t[0], me * ch, ch, 1)
    u_own = pay_u[0]

    def row(x):
        return jnp.sum(x, axis=0, keepdims=True)

    smalls = jnp.concatenate(
        [
            wg1_st[0:1],
            wg2_st[0:1],
            row(u_own[:NC]),
            row(u_own[NC:]),
            proj_st[0:1],
            qkv_st[0:1],
            qkv_st[2:3],
            row(t_own[:NC]),
            row(t_own[NC:]),
        ]
        + [zero] * 7,
        axis=0,
    )
    gp1, pay_v = call(
        functools.partial(k_back1, nch, offs),
        (me1, recv1, recv2, recv_u, cnt, lab, masks, w1t, x_own, smalls, *gp_slots, *c1_slots),
        (sd((ch, n), F32), sd((rows_n, 32, ch), F32)),
        [
            pltpu.VMEM((9, C, e), BF),
            pltpu.VMEM((ch, e), F32),
            pltpu.VMEM((C, NC), F32),
            pltpu.VMEM((C, NC), F32),
            pltpu.VMEM((C, NC), F32),
            st,
        ],
        flops=conv_flops,
    )
    recv_v = lax.all_to_all(pay_v, "rows", 0, 0)
    fg, sums = call(
        k_last,
        (
            jnp.stack([me, m]).astype(jnp.int32),
            recv1, recv_v, cnt, lab, gp1, x_own, grad_resid,
        ),
        (sd((ch, n), BF), sd((2, 32, ch), F32)),
    )
    features_grad = reshard_back(fg)

    total = sums[0] + sums[1]
    norm1_bias_grad = jnp.sum(total[:NC], axis=0)
    norm1_gain_grad = jnp.sum(total[NC:16], axis=0)
    u1, u2 = sums[:, 18], sums[:, 19]
    scale_up = 1.0 + modulation[:, 0]
    norm2_bias_grad = jnp.sum(scale_up * u1, axis=0)
    norm2_gain_grad = jnp.sum(scale_up * u2, axis=0)
    mod_grad = jnp.stack([norm2_gain * u2 + norm2_bias * u1, u1], axis=1)
    embed_weight_grad = (
        mod_grad[0][:, :, None] * embedded[0][None, None, :]
        + mod_grad[1][:, :, None] * embedded[1][None, None, :]
    )
    embed_bias_grad = jnp.sum(mod_grad, axis=0)
    encoder_grad = ctx_sum.reshape(batches, 2, ch, -1)
    encoder_weight_grad = jnp.einsum(
        "bjdt,bte->jde", encoder_grad, context, preferred_element_type=F32
    )
    encoder_bias_grad = jnp.sum(encoder_grad.astype(F32), axis=(0, 3))

    def conv_out(x):
        return x.astype(F32).reshape(3, 3, ch, C).transpose(2, 0, 1, 3)

    return (
        output,
        features_grad,
        norm1_gain_grad,
        norm1_bias_grad,
        conv_out(wg1_sum),
        total[16],
        embed_weight_grad,
        embed_bias_grad,
        norm2_gain_grad,
        norm2_bias_grad,
        conv_out(wg2_sum),
        total[17],
        total[24],
        total[23],
        qkv_sum.astype(F32),
        jnp.stack([total[21], total[22]]),
        encoder_weight_grad,
        encoder_bias_grad,
        proj_sum.astype(F32),
        total[20],
    )


def solution(mesh):
    placed = (
        P(None, "ch", "rows"),
        P(),
        P(),
        P(),
        P(),
        P("ch"),
        P("ch"),
        P("ch", None, None, None),
        P("ch"),
        P(None, "ch", None),
        P(None, "ch"),
        P("ch"),
        P("ch"),
        P("ch", None, None, None),
        P("ch"),
        P("ch"),
        P("ch"),
        P(None, "ch", None),
        P(None, "ch"),
        P(None, "ch", None),
        P(None, "ch"),
        P("ch", None),
        P("ch"),
        P(None, "ch", "rows"),
    )
    return jax.shard_map(
        per_device,
        mesh=mesh,
        in_specs=placed,
        out_specs=(
            P(None, "ch", "rows"),
            P(None, "ch", "rows"),
            P("ch"),
            P("ch"),
            P("ch", None, None, None),
            P("ch"),
            P(None, "ch", None),
            P(None, "ch"),
            P("ch"),
            P("ch"),
            P("ch", None, None, None),
            P("ch"),
            P("ch"),
            P("ch"),
            P(None, "ch", None),
            P(None, "ch"),
            P(None, "ch", None),
            P(None, "ch"),
            P("ch", None),
            P("ch"),
        ),
        check_vma=False,
    )
```

```python
import functools
import math

import jax
import jax.numpy as jnp
from jax import lax
from jax.experimental import pallas as pl
from jax.experimental.pallas import tpu as pltpu
from jax.sharding import PartitionSpec as P

C = 512
HD = 64
GSZ = 16
EMB = 2048
W = 64
NCROP = 6
NC = 8
HP = 2 * W
TAPS = [(di, dj) for di in (-1, 0, 1) for dj in (-1, 0, 1)]

PRECISE = lax.Precision.HIGHEST
EPSILON = 1e-05
FAR = 2.0**100
SCORE = HD**-0.5
LOG2E = 1.4426950408889634
F32 = jnp.float32
BF = jnp.bfloat16


def spread(vals, lab):
    acc = vals[:, 0:1]
    for n in range(1, NCROP):
        acc = jnp.where(lab == n, vals[:, n : n + 1], acc)
    return acc


def crop_columns(first, second, lab):
    rows = first.shape[0]
    lane = lax.broadcasted_iota(jnp.int32, (rows, 128), 1)
    acc = jnp.zeros((rows, 128), F32)
    for n in range(NCROP):
        inside = lab == n
        one = jnp.sum(jnp.where(inside, first, 0.0), axis=1, keepdims=True)
        two = jnp.sum(jnp.where(inside, second, 0.0), axis=1, keepdims=True)
        acc = jnp.where(lane == n, one, acc)
        acc = jnp.where(lane == NC + n, two, acc)
    return acc


def put_column(acc, column, at):
    lane = lax.broadcasted_iota(jnp.int32, acc.shape, 1)
    return jnp.where(lane == at, column, acc)


def grouped(vals):
    rows, width = vals.shape
    parts = jnp.sum(vals.reshape(rows // GSZ, GSZ, width), axis=1, keepdims=True)
    return jnp.broadcast_to(parts, (rows // GSZ, GSZ, width)).reshape(rows, width)


def turned(block):
    rows, cols = block.shape
    if rows < 128:
        block = jnp.concatenate([block, jnp.zeros((128 - rows, cols), F32)], axis=0)
    return jnp.transpose(block)


def read_stats(recv_ref, which, cnt):
    members = recv_ref.shape[0]
    block = recv_ref[0, which]
    for g in range(1, members):
        other = recv_ref[g, which]
        block = jnp.concatenate([block[:16] + other[:16], block[16:]], axis=0)
    cols = turned(block)
    sums = grouped(cols[:, :16])
    mean = sums[:, :NC] / cnt
    inv = lax.rsqrt(sums[:, NC:16] / cnt - mean * mean + EPSILON)
    return mean, inv, cols[:, 16:17], cols[:, 17:18], cols[:, 18:19], cols[:, 19:20]


def read_sums(recv_ref, which):
    members = recv_ref.shape[0]
    block = recv_ref[0, which][:16]
    for g in range(1, members):
        block = block + recv_ref[g, which][:16]
    return turned(block)


def affine_of(stats):
    mean, inv, gain, bias, scale, offset = stats
    a = inv * gain * (1.0 + scale)
    b = (bias - mean * inv * gain) * (1.0 + scale) + offset
    return a, b


def sigmoid(v):
    return 0.5 * (1.0 + jnp.tanh(0.5 * v))


def slope(v):
    s = sigmoid(v)
    return s * (1.0 + v * (1.0 - s))


def masked_conv(w_ref, h_ref, y_ref, out_ref, mask_ref, bias):
    ch, width = out_ref.shape
    for g in range(3):
        w = w_ref[3 * g : 3 * g + 3].reshape(3 * ch, C)
        y_ref[g] = jnp.dot(w, h_ref[...], preferred_element_type=F32)
    size = min(ch, 64)

    def body(i, carry):
        i = pl.multiple_of(i * size, size)
        acc = None
        for g in range(3):
            for k in range(3):
                tap = 3 * g + k
                off = W * (g - 1) + k - 1
                y = y_ref[g, pl.ds(pl.multiple_of(k * ch + i, size), size), :]
                y = y if off == 0 else pltpu.roll(y, (-off) % width, 1)
                y = y * mask_ref[tap : tap + 1, :]
                acc = y if acc is None else acc + y
        if bias is not None:
            acc = acc + bias[pl.ds(i, size), :]
        out_ref[pl.ds(i, size), :] = acc
        return carry

    lax.fori_loop(0, ch // size, body, 0)


def chunks(rows, body):
    size = min(128, rows)

    def step(i, carry):
        body(pl.multiple_of(i * size, size), size)
        return carry

    lax.fori_loop(0, rows // size, step, 0)


def send_rows(out_ref, st_ref, params):
    rows = jnp.transpose(st_ref[...])[:16]
    if params is not None:
        rows = jnp.concatenate([rows, params], axis=0)
    for k in range(out_ref.shape[0]):
        out_ref[k] = rows


def k_stats(x_ref, lab_ref, par_ref, out_ref, st_ref):
    n = x_ref.shape[1] - 2 * HP
    lab = lab_ref[:, HP : HP + n]

    def body(i, size):
        v = x_ref[pl.ds(i, size), HP : HP + n].astype(F32)
        st_ref[pl.ds(i, size), :] = crop_columns(v, v * v, lab)

    chunks(x_ref.shape[0], body)
    send_rows(out_ref, st_ref, par_ref[...])


def k_conv(nch, offs, resid, *refs):
    me_ref, recv_ref, cnt_ref, lab_ref, mask_ref, w_ref, b_ref, par_ref = refs[:8]
    slots = refs[8 : 8 + nch]
    refs = refs[8 + nch :]
    if resid:
        x_ref, refs = refs[0], refs[1:]
        low_ref, pay_ref, h_ref, full_ref = refs[:4]
        refs = refs[4:]
    else:
        low_ref, pay_ref, h_ref = refs[:3]
        refs = refs[3:]
    y_ref, acc_ref, a_ref, b2_ref, st_ref = refs
    me = me_ref[0]
    ch, e = acc_ref.shape
    n = e - 2 * HP
    lab = lab_ref[...]
    for c in range(nch):
        a, b = affine_of(read_stats(recv_ref, c, cnt_ref[...]))
        a_ref[c * ch : (c + 1) * ch, :] = a
        b2_ref[c * ch : (c + 1) * ch, :] = b
    for s in range(nch):
        base = pl.multiple_of((me ^ offs[s]) * ch, ch)

        def body(i, size, s=s, base=base):
            row = pl.multiple_of(base + i, size)
            v = slots[s][pl.ds(i, size), :].astype(F32)
            pre = v * spread(a_ref[pl.ds(row, size), :], lab) + spread(b2_ref[pl.ds(row, size), :], lab)
            low = (pre * sigmoid(pre)).astype(BF)
            h_ref[pl.ds(row, size), :] = low

        chunks(ch, body)
    masked_conv(w_ref, h_ref, y_ref, acc_ref, mask_ref, b_ref)
    labc = lab[:, HP : HP + n]

    def finish(i, size):
        if resid:
            v = acc_ref[pl.ds(i, size), HP : HP + n] + x_ref[pl.ds(i, size), HP : HP + n].astype(F32)
            full_ref[pl.ds(i, size), :] = v
            low_ref[pl.ds(i, size), :] = v.astype(BF)
        else:
            low_ref[pl.ds(i, size), :] = acc_ref[pl.ds(i, size), :].astype(BF)
            v = acc_ref[pl.ds(i, size), HP : HP + n]
        st_ref[pl.ds(i, size), :] = crop_columns(v, v * v, labc)

    chunks(ch, finish)
    send_rows(pay_ref, st_ref, par_ref[...])


def k_qkv(nch, offs, *refs):
    me_ref, recv_ref, cnt_ref, lab_ref, w_ref, qb_ref, vb_ref = refs[:7]
    slots = refs[7 : 7 + nch]
    res_ref, att_ref, q_ref, k_ref, v_ref, a_ref, b_ref = refs[7 + nch :]
    me = me_ref[0]
    ch, n = q_ref.shape
    lab = lab_ref[:, HP : HP + n]
    for c in range(nch):
        a, b = affine_of(read_stats(recv_ref, c, cnt_ref[...]))
        a_ref[c * ch : (c + 1) * ch, :] = a
        b_ref[c * ch : (c + 1) * ch, :] = b
    for s in range(nch):
        base = pl.multiple_of((me ^ offs[s]) * ch, ch)

        def body(i, size, s=s, base=base):
            row = pl.multiple_of(base + i, size)
            low = slots[s][pl.ds(i, size), :]
            res_ref[pl.ds(row, size), :] = low
            out = low.astype(F32) * spread(a_ref[pl.ds(row, size), :], lab) + spread(
                b_ref[pl.ds(row, size), :], lab
            )
            att_ref[pl.ds(row, size), :] = out.astype(BF)

        chunks(ch, body)
    tile = 256

    def mul(i, _):
        at = pl.ds(pl.multiple_of(i * tile, tile), tile)
        x = att_ref[:, at]
        q_ref[:, at] = (jnp.dot(w_ref[0], x, preferred_element_type=F32) + qb_ref[...]).astype(BF)
        k_ref[:, at] = jnp.dot(w_ref[1], x, preferred_element_type=F32).astype(BF)
        v_ref[:, at] = (jnp.dot(w_ref[2], x, preferred_element_type=F32) + vb_ref[...]).astype(BF)
        return 0

    lax.fori_loop(0, n // tile, mul, 0)


def k_gout(nch, offs, *refs):
    me_ref, w_ref = refs[:2]
    slots = refs[2 : 2 + nch]
    g_ref, ga_ref = refs[2 + nch :]
    me = me_ref[0]
    ch, n = ga_ref.shape
    for s in range(nch):
        base = pl.multiple_of((me ^ offs[s]) * ch, ch)
        g_ref[pl.ds(base, ch), :] = slots[s][...]
    ga_ref[...] = jnp.dot(w_ref[...], g_ref[:, HP : HP + n], preferred_element_type=F32).astype(BF)


def k_turn(nch, offs, *refs):
    me_ref = refs[0]
    ins = refs[1 : 1 + nch]
    wqs = refs[1 + nch : 1 + 2 * nch]
    w1_ref, w2_ref, wq_ref, pw_ref, scr, scq = refs[1 + 2 * nch :]
    me = me_ref[0]
    ch = w1_ref.shape[1]
    for t in range(19):
        for s in range(nch):
            base = pl.multiple_of((me ^ offs[s]) * ch, ch)
            scr[pl.ds(base, ch), :] = ins[s][t].astype(F32)
        out = jnp.transpose(scr[...]).astype(BF)
        if t < 9:
            w1_ref[8 - t] = out
        elif t < 18:
            w2_ref[17 - t] = out
        else:
            pw_ref[...] = out
    for j in range(3):
        for s in range(nch):
            base = pl.multiple_of((me ^ offs[s]) * ch, ch)
            scq[pl.ds(base, ch), :] = wqs[s][j].astype(F32)
        wq_ref[j] = jnp.transpose(scq[...]).astype(BF)


def nt(a, b):
    return lax.dot_general(a, b, (((1,), (1,)), ((), ())), preferred_element_type=F32)


def tn(a, b):
    return lax.dot_general(a, b, (((0,), (0,)), ((), ())), preferred_element_type=F32)


def k_attend(kmap, vmap, nk, nv, korder, vorder, *refs):
    q_ref, ga_ref, oneq_ref, onek_ref, ck_ref, cv_ref = refs[:6]
    kparts = refs[6 : 6 + nk]
    vparts = refs[6 + nk : 6 + nk + nv]
    out_ref, dq_ref, dk0_ref, dk1_ref, dv0_ref, dv1_ref, dck_ref, dcv_ref = refs[
        6 + nk + nv : 14 + nk + nv
    ]
    ks_ref, vs_ref, e_ref, s_ref, ak_ref, av_ref = refs[14 + nk + nv :]
    ch, n = q_ref.shape
    heads = ch // HD
    slots = len(kmap)
    keys = slots * n
    tq = e_ref.shape[0]
    con = SCORE * LOG2E
    for h in range(heads):
        hs = slice(h * HD, (h + 1) * HD)
        for s in range(slots):
            i, j = kmap[s]
            ks_ref[h, 0:HD, s * n : (s + 1) * n] = kparts[i][j, hs, :]
            i, j = vmap[s]
            vs_ref[h, :, s * n : (s + 1) * n] = vparts[i][j, hs, :]
        ks_ref[h, HD : HD + 16, 0:keys] = onek_ref[...]
        ks_ref[h, 0:HD, keys:] = ck_ref[hs, :]
        ks_ref[h, HD : HD + 16, keys:] = jnp.zeros((16, 128), BF)
        vs_ref[h, :, keys:] = cv_ref[hs, :]
    once = n == tq
    if not once:
        ak_ref[...] = jnp.zeros_like(ak_ref)
        av_ref[...] = jnp.zeros_like(av_ref)
    spans = [(s * n, n) for s in range(slots)] + [(keys, 128)]

    for h in range(heads):
        hs = slice(h * HD, (h + 1) * HD)

        def block(b, _, h=h, hs=hs):
            at = pl.ds(pl.multiple_of(b * tq, tq), tq)
            qb = q_ref[hs, at]
            gb = ga_ref[hs, at]
            qa = jnp.transpose(
                jnp.concatenate([qb.astype(F32), oneq_ref[:, at].astype(F32)], axis=0)
            ).astype(BF)
            gt = jnp.transpose(gb.astype(F32))
            gtb = gt.astype(BF)
            top = jnp.full((tq, 128), -jnp.inf, F32)
            for k0, kn in spans:
                sc = jnp.dot(qa, ks_ref[h, :, k0 : k0 + kn], preferred_element_type=F32)
                s_ref[:, k0 : k0 + kn] = sc
                for u in range(kn // 128):
                    top = jnp.maximum(top, sc[:, u * 128 : (u + 1) * 128])
            top = jnp.max(top, axis=1, keepdims=True) * con
            tot = jnp.zeros((tq, 128), F32)
            acc = jnp.zeros((HD, tq), F32)
            for k0, kn in spans:
                ex = jnp.exp2(s_ref[:, k0 : k0 + kn] * con - top)
                for u in range(kn // 128):
                    tot = tot + ex[:, u * 128 : (u + 1) * 128]
                exb = ex.astype(BF)
                e_ref[:, k0 : k0 + kn] = exb
                acc = acc + nt(vs_ref[h, :, k0 : k0 + kn], exb)
            inv = 1.0 / jnp.sum(tot, axis=1, keepdims=True)
            acc = jnp.transpose(acc) * inv
            delta = jnp.sum(acc * gt, axis=1, keepdims=True)
            out_ref[hs, at] = jnp.transpose(acc).astype(BF)
            ql = jnp.transpose(qa[:, :HD].astype(F32) * (inv * SCORE)).astype(BF)
            gl = jnp.transpose(gt * inv).astype(BF)
            dq = jnp.zeros((HD, tq), F32)
            for k0, kn in spans:
                dp = jnp.dot(gtb, vs_ref[h, :, k0 : k0 + kn], preferred_element_type=F32)
                exb = e_ref[:, k0 : k0 + kn]
                ds = (exb.astype(F32) * (dp - delta)).astype(BF)
                dq = dq + nt(ks_ref[h, 0:HD, k0 : k0 + kn], ds)
                dk = jnp.dot(ql, ds, preferred_element_type=F32)
                dv = jnp.dot(gl, exb, preferred_element_type=F32)
                if not once:
                    dk = dk + ak_ref[hs, k0 : k0 + kn]
                    dv = dv + av_ref[hs, k0 : k0 + kn]
                ak_ref[hs, k0 : k0 + kn] = dk
                av_ref[hs, k0 : k0 + kn] = dv
            dq_ref[hs, at] = jnp.transpose(jnp.transpose(dq) * (inv * SCORE)).astype(BF)
            return 0

        lax.fori_loop(0, n // tq, block, 0)
    for order, acc_ref, outs in (
        (korder, ak_ref, (dk0_ref, dk1_ref)),
        (vorder, av_ref, (dv0_ref, dv1_ref)),
    ):
        for side in range(2):
            for i, s in enumerate(order[side]):
                outs[side][i] = acc_ref[:, s * n : (s + 1) * n].astype(BF)
    dck_ref[...] = ak_ref[:, keys:]
    dcv_ref[...] = av_ref[:, keys:]


def k_proj(nch, offs, *refs):
    me_ref, res_ref, pb_ref, pw_ref = refs[:4]
    atts = refs[4 : 4 + nch]
    out_ref, att_s = refs[4 + nch :]
    me = me_ref[0]
    ch = res_ref.shape[0]
    for s in range(nch):
        base = pl.multiple_of((me ^ offs[s]) * ch, ch)
        att_s[pl.ds(base, ch), :] = atts[s][...]
    mixed = jnp.dot(pw_ref[...], att_s[...], preferred_element_type=F32)
    out_ref[...] = (res_ref[...] + mixed + pb_ref[...]).astype(BF)


def k_gattend(nch, offs, *refs):
    me_ref, recv_ref, cnt_ref, lab_ref, w_ref, res_ref = refs[:6]
    slots = [refs[6 + j * nch : 6 + (j + 1) * nch] for j in range(3)]
    ga_ref, pay_ref, d_s, acc_ref, st_ref = refs[6 + 3 * nch :]
    me = me_ref[0]
    n = ga_ref.shape[1]
    ch = C // nch
    lab = lab_ref[:, HP : HP + n]
    for j in range(3):
        for s in range(nch):
            base = pl.multiple_of((me ^ offs[s]) * ch, ch)
            d_s[j, pl.ds(base, ch), :] = slots[j][s][...]
    tile = 256

    def mul(i, _):
        at = pl.ds(pl.multiple_of(i * tile, tile), tile)
        acc = jnp.dot(w_ref[0], d_s[0, :, at], preferred_element_type=F32)
        acc = acc + jnp.dot(w_ref[1], d_s[1, :, at], preferred_element_type=F32)
        acc = acc + jnp.dot(w_ref[2], d_s[2, :, at], preferred_element_type=F32)
        acc_ref[:, at] = acc
        ga_ref[:, at] = acc.astype(BF)
        return 0

    lax.fori_loop(0, n // tile, mul, 0)
    mean, inv = read_stats(recv_ref, me, cnt_ref[...])[:2]
    own = pl.ds(pl.multiple_of(me * ch, ch), ch)
    ga = acc_ref[own, :]
    normed = (res_ref[own, :].astype(F32) - spread(mean, lab)) * spread(inv, lab)
    st_ref[...] = crop_columns(ga, ga * normed, lab)
    send_rows(pay_ref, st_ref, None)


def k_early(*refs):
    me_ref, dq_ref, dk_ref, dv_ref, in_ref, att_ref, g_ref, dck_ref, dcv_ref = refs[:9]
    out_ref, st_ref = refs[9:]
    ch, n = dq_ref.shape
    strip = me_ref[2]
    acc = jnp.zeros((ch, 128), F32)
    own = g_ref[pl.ds(pl.multiple_of(me_ref[0] * ch, ch), ch), HP : HP + n].astype(F32)
    acc = put_column(acc, jnp.sum(own, axis=1, keepdims=True), 3)
    for t in range(5):
        if t < 3:
            d = (dq_ref, dk_ref, dv_ref)[t][...]
            acc = put_column(acc, jnp.sum(d.astype(F32), axis=1, keepdims=True), t)
            full = nt(d, in_ref[...])
        elif t == 3:
            full = nt(att_ref[...], g_ref[:, HP : HP + n])
        else:
            both = jnp.concatenate([dck_ref[...], dcv_ref[...]], axis=1)
            full = jnp.concatenate(
                [jnp.where(strip == i, both, 0.0) for i in range(2)], axis=1
            )
        out_ref[t] = full.astype(BF)
    st_ref[...] = jnp.transpose(acc)[:8]


def norm_back(mean, inv, gain, t1, t2, cnt):
    m1 = grouped(gain * t1) / cnt
    m2 = grouped(gain * t2) / cnt
    return inv * gain, -inv * inv * m2, inv * (mean * inv * m2 - m1)


def k_back2(nch, *refs):
    (me_ref, recv3_ref, recvt_ref, recv2_ref, cnt_ref, lab_ref, mask_ref, w_ref) = refs[:8]
    ga_ref, gat_ref, gab_ref, res_ref, rest_ref, resb_ref, g_ref, c1_ref = refs[8:16]
    gp_ref, pay_ref, gc_ref, gr_ref = refs[16:20]
    h_ref, y_ref, acc_ref, a_ref, b_ref, c_ref, st_ref, full_ref = refs[20:]
    me = me_ref[0]
    ch, e = acc_ref.shape
    n = e - 2 * HP
    lab = lab_ref[...]
    cnt = cnt_ref[...]
    for c in range(nch):
        sl = slice(c * ch, (c + 1) * ch)
        mean, inv, gain = read_stats(recv3_ref, c, cnt)[:3]
        t = read_sums(recvt_ref, c)
        a, b, cc = norm_back(mean, inv, gain, t[:, :NC], t[:, NC:16], cnt)
        a_ref[sl, :] = a
        b_ref[sl, :] = b
        c_ref[sl, :] = cc

    def body(i, size):
        row = pl.ds(i, size)
        ga = jnp.concatenate([gat_ref[row, :], ga_ref[row, :], gab_ref[row, :]], axis=1).astype(F32)
        v = jnp.concatenate([rest_ref[row, :], res_ref[row, :], resb_ref[row, :]], axis=1).astype(
            F32
        )
        gr = (
            g_ref[row, :].astype(F32)
            + ga * spread(a_ref[row, :], lab)
            + v * spread(b_ref[row, :], lab)
            + spread(c_ref[row, :], lab)
        )
        full_ref[row, :] = gr
        h_ref[row, :] = gr.astype(BF)

    chunks(C, body)
    own = pl.multiple_of(me * ch, ch)
    gr_ref[...] = full_ref[pl.ds(own, ch), HP : HP + n]
    masked_conv(w_ref, h_ref, y_ref, acc_ref, mask_ref, None)
    stats = None
    mean, inv, gain, bias, scale, offset = read_stats(recv2_ref, me, cnt)
    a, b = affine_of((mean, inv, gain, bias, scale, offset))
    a_ref[0:ch, :] = a
    b_ref[0:ch, :] = b
    c_ref[0:ch, :] = inv
    a_ref[ch : 2 * ch, :] = -mean * inv

    def finish(i, size):
        row = pl.ds(i, size)
        v = c1_ref[row, :].astype(F32)
        pre = v * spread(a_ref[row, :], lab) + spread(b_ref[row, :], lab)
        gp = acc_ref[row, :] * slope(pre)
        gp_ref[row, :] = gp.astype(BF)
        labc = lab[:, HP : HP + n]
        normed = v[:, HP : HP + n] * spread(c_ref[row, :], labc) + spread(
            a_ref[pl.ds(pl.multiple_of(ch + i, size), size), :], labc
        )
        gpc = gp[:, HP : HP + n]
        low = gr_ref[row, :].astype(BF)
        gc_ref[row, :] = low
        acc = crop_columns(gpc, gpc * normed, labc)
        st_ref[row, :] = acc

    chunks(ch, finish)
    send_rows(pay_ref, st_ref, None)


def wgrad_body(split, pos, gc, h_ref, mask_ref, outs, st_ref, g_ref, y_ref):
    ch, n = gc.shape
    width = n + 2 * HP
    edge = jnp.zeros((ch, HP), F32)
    wide = jnp.concatenate([edge, gc, edge], axis=1)
    for t, (di, dj) in enumerate(TAPS):
        off = W * di + dj
        moved = wide * mask_ref[t : t + 1, :]
        moved = moved if off == 0 else pltpu.roll(moved, off % width, 1)
        g_ref[t * ch : (t + 1) * ch, :] = moved.astype(BF)
    rows = ch // 4
    for g in range(3):
        y_ref[...] = nt(g_ref[3 * g * ch : 3 * (g + 1) * ch, :], h_ref[...])
        for k in range(3):
            t = 3 * g + k
            if not split:
                outs[0][t] = y_ref[k * ch : (k + 1) * ch, :].astype(BF)
                continue
            for o in range(4):
                at = pl.multiple_of(k * ch + (pos ^ o) * rows, rows)
                outs[o][t] = y_ref[pl.ds(at, rows), :].astype(BF)
    acc = jnp.zeros((ch, 128), F32)
    acc = put_column(acc, jnp.sum(gc, axis=1, keepdims=True), 0)
    st_ref[...] = jnp.transpose(acc)[:8]


def k_wgrad2(split, me_ref, mask_ref, gc_ref, h_ref, *refs):
    outs, (st_ref, g_ref, y_ref) = refs[:-3], refs[-3:]
    gc = gc_ref[...].astype(F32)
    wgrad_body(split, me_ref[1], gc, h_ref, mask_ref, outs, st_ref, g_ref, y_ref)


def k_place(me_ref, *refs):
    parts, out_ref = refs[:-1], refs[-1]
    rows = parts[0].shape[1]
    for o, part in enumerate(parts):
        at = pl.ds(pl.multiple_of((me_ref[1] ^ o) * rows, rows), rows)
        out_ref[:, at, :] = part[...].astype(F32)


def conv1_back(recv2_ref, recvu_ref, which, cnt):
    mean, inv, gain, _, scale, _ = read_stats(recv2_ref, which, cnt)
    u = read_sums(recvu_ref, which)
    return norm_back(mean, inv, gain * (1.0 + scale), u[:, :NC], u[:, NC:16], cnt)


def k_wgrad1(split, *refs):
    me_ref, recv2_ref, recvu_ref, cnt_ref, lab_ref, mask_ref, gp_ref, c1_ref, h_ref = refs[:9]
    outs, (st_ref, g_ref, y_ref) = refs[9:-3], refs[-3:]
    n = gp_ref.shape[1] - 2 * HP
    lab = lab_ref[:, HP : HP + n]
    a, b, c = conv1_back(recv2_ref, recvu_ref, me_ref[0], cnt_ref[...])
    gc = (
        gp_ref[:, HP : HP + n].astype(F32) * spread(a, lab)
        + c1_ref[:, HP : HP + n].astype(F32) * spread(b, lab)
        + spread(c, lab)
    ).astype(BF).astype(F32)
    wgrad_body(split, me_ref[1], gc, h_ref, mask_ref, outs, st_ref, g_ref, y_ref)


def k_back1(nch, offs, *refs):
    me_ref, recv1_ref, recv2_ref, recvu_ref, cnt_ref, lab_ref, mask_ref, w_ref, x_ref = refs[:9]
    wg1_ref, wg2_ref, early_ref, payu_ref, payt_ref = refs[9:14]
    gps = refs[14 : 14 + nch]
    c1s = refs[14 + nch : 14 + 2 * nch]
    gp1_ref, pay_ref = refs[14 + 2 * nch : 16 + 2 * nch]
    h_ref, y_ref, acc_ref, a_ref, b_ref, c_ref, st_ref = refs[16 + 2 * nch :]
    me = me_ref[0]
    ch, e = acc_ref.shape
    n = e - 2 * HP
    lab = lab_ref[...]
    cnt = cnt_ref[...]
    for c in range(nch):
        sl = slice(c * ch, (c + 1) * ch)
        a, b, cc = conv1_back(recv2_ref, recvu_ref, c, cnt)
        a_ref[sl, :] = a
        b_ref[sl, :] = b
        c_ref[sl, :] = cc
    for s in range(nch):
        base = pl.multiple_of((me ^ offs[s]) * ch, ch)

        def body(i, size, s=s, base=base):
            row = pl.multiple_of(base + i, size)
            at = pl.ds(row, size)
            gc = (
                gps[s][pl.ds(i, size), :].astype(F32) * spread(a_ref[at, :], lab)
                + c1s[s][pl.ds(i, size), :].astype(F32) * spread(b_ref[at, :], lab)
                + spread(c_ref[at, :], lab)
            )
            h_ref[at, :] = gc.astype(BF)

        chunks(ch, body)
    masked_conv(w_ref, h_ref, y_ref, acc_ref, mask_ref, None)
    stats = read_stats(recv1_ref, me, cnt)
    a, b = affine_of(stats)
    a_ref[0:ch, :] = a
    b_ref[0:ch, :] = b
    c_ref[0:ch, :] = stats[1]
    c_ref[ch : 2 * ch, :] = -stats[0] * stats[1]
    labc = lab[:, HP : HP + n]

    def finish(i, size):
        row = pl.ds(i, size)
        v = x_ref[row, HP : HP + n].astype(F32)
        pre = v * spread(a_ref[row, :], labc) + spread(b_ref[row, :], labc)
        gp = acc_ref[row, HP : HP + n] * slope(pre)
        gp1_ref[row, :] = gp
        normed = v * spread(c_ref[row, :], labc) + spread(
            c_ref[pl.ds(pl.multiple_of(ch + i, size), size), :], labc
        )
        st_ref[row, :] = crop_columns(gp, gp * normed, labc)

    chunks(ch, finish)
    u, t = payu_ref[0], payt_ref[0]
    smalls = jnp.zeros((16, ch), F32)
    at = lax.broadcasted_iota(jnp.int32, (16, ch), 0)
    for i, line in enumerate(
        (
            wg1_ref[0:1],
            wg2_ref[0:1],
            jnp.sum(u[:NC], axis=0, keepdims=True),
            jnp.sum(u[NC:], axis=0, keepdims=True),
            early_ref[3:4],
            early_ref[0:1],
            early_ref[2:3],
            jnp.sum(t[:NC], axis=0, keepdims=True),
            jnp.sum(t[NC:], axis=0, keepdims=True),
        )
    ):
        smalls = jnp.where(at == i, line, smalls)
    send_rows(pay_ref, st_ref, smalls)


def k_last(*refs):
    me_ref, recv1_ref, recvv_ref, cnt_ref, lab_ref, gp_ref, x_ref, gr_ref, par_ref = refs[:9]
    out_ref, mod_ref, emb_ref, qb_ref = refs[9:13]
    (n1g, n1b, c1b, n2g, n2b, c2b, n3g, n3b, pb) = refs[13:22]
    sum_ref = refs[22]
    ch, n = gp_ref.shape
    half = recvv_ref.shape[0] // 2
    lab = lab_ref[:, HP : HP + n]
    for m in range(2):
        tot = recvv_ref[m * half]
        for g in range(1, half):
            tot = tot + recvv_ref[m * half + g]
        sum_ref[m] = tot
    cnt = cnt_ref[...]
    mean, inv, gain = read_stats(recv1_ref, me_ref[0], cnt)[:3]
    v = turned(sum_ref[me_ref[1]][:16])
    a, b, c = norm_back(mean, inv, gain, v[:, :NC], v[:, NC:16], cnt)
    out = (
        gr_ref[...]
        + gp_ref[...] * spread(a, lab)
        + x_ref[:, HP : HP + n].astype(F32) * spread(b, lab)
        + spread(c, lab)
    )
    out_ref[...] = out.astype(BF)
    both = sum_ref[0] + sum_ref[1]
    n1b[...] = jnp.sum(both[:NC], axis=0, keepdims=True)
    n1g[...] = jnp.sum(both[NC:16], axis=0, keepdims=True)
    for ref, at in ((c1b, 16), (c2b, 17), (pb, 20), (n3b, 23), (n3g, 24)):
        ref[...] = both[at : at + 1]
    qb_ref[...] = both[21:23]
    u1 = [sum_ref[m, 18:19] for m in range(2)]
    u2 = [sum_ref[m, 19:20] for m in range(2)]
    up = [1.0 + par_ref[2 + m : 3 + m] for m in range(2)]
    n2b[...] = up[0] * u1[0] + up[1] * u1[1]
    n2g[...] = up[0] * u2[0] + up[1] * u2[1]
    scales = [par_ref[0:1] * u2[m] + par_ref[1:2] * u1[m] for m in range(2)]
    mod_ref[...] = jnp.concatenate([scales[0], u1[0], scales[1], u1[1]], axis=0)
    emb_ref[...] = jnp.concatenate([scales[0] + scales[1], u1[0] + u1[1]], axis=0)


COST = {"k_stats": 2, "k_conv": 10, "k_qkv": 6, "k_gout": 3, "k_attend": 34, "k_turn": 5, "k_proj": 3, "k_gattend": 7, "k_early": 4, "k_back2": 14, "k_wgrad2": 4, "k_wgrad1": 5, "k_back1": 13, "k_last": 3, "k_place": 3}
SM = pl.BlockSpec(memory_space=pltpu.SMEM)
VM = pl.BlockSpec(memory_space=pltpu.VMEM)


def call(kernel, args, outs, scratch=(), smem=1, flops=0, limit=60):
    name = getattr(kernel, "func", kernel).__name__
    flops = int(COST[name] * 1.15e9)
    bytes_all = sum(math.prod(a.shape) * a.dtype.itemsize for a in list(args) + list(outs))
    return pl.pallas_call(
        kernel,
        out_shape=tuple(outs),
        in_specs=[SM] * smem + [VM] * (len(args) - smem),
        out_specs=tuple(VM for _ in outs),
        scratch_shapes=list(scratch),
        compiler_params=pltpu.CompilerParams(vmem_limit_bytes=limit * 2**20),
        cost_estimate=pl.CostEstimate(flops=flops, bytes_accessed=bytes_all, transcendentals=0),
    )(*args)


def fence(*xs):
    return lax.optimization_barrier(xs)


def sd(shape, dtype):
    return jax.ShapeDtypeStruct(shape, dtype)


def swap(x, axis, bit):
    count = lax.axis_size(axis)
    return lax.ppermute(x, axis, [(i, i ^ bit) for i in range(count)])


def bits_of(count):
    return [1 << i for i in range(count.bit_length() - 1)]


def offsets(count):
    offs = [0]
    for bit in reversed(bits_of(count)):
        offs = offs + [o ^ bit for o in offs]
    return offs


def gather_ch(x):
    slots = [x]
    for bit in reversed(bits_of(lax.axis_size("ch"))):
        slots = slots + [swap(s, "ch", bit) for s in slots]
    return slots


def first_hops(x):
    return [x] + [swap(x, "ch", bit) for bit in reversed(bits_of(lax.axis_size("ch")))]


def last_hops(hops):
    bits = list(reversed(bits_of(lax.axis_size("ch"))))
    slots = [hops[0]]
    for at, bit in enumerate(bits):
        slots = slots + [hops[at + 1]] + [swap(s, "ch", bit) for s in slots[1:]]
    return slots


def gather_rows(x, bits):
    parts, places, offs = [x[None]], [(0, 0)], [0]
    for bit in bits:
        whole = parts[0] if len(parts) == 1 else jnp.concatenate(parts, axis=0)
        base = len(parts)
        parts = parts + [swap(whole, "rows", bit)]
        places = places + [(base, i) for i in range(len(offs))]
        offs = offs + [o ^ bit for o in offs]
    table = dict(zip(offs, places, strict=True))
    return parts, [table[o] for o in range(len(offs))]


def order_of(bits):
    keep = [0]
    for bit in reversed(bits[1:]):
        keep = keep + [o ^ bit for o in keep]
    return keep, [o ^ bits[0] for o in keep]


def add_low(a, b):
    return (a.astype(F32) + b.astype(F32)).astype(BF)


def scatter_rows(keep, got, bits):
    for bit in bits[1:]:
        mid = keep.shape[0] // 2
        give = add_low(keep[mid:], got[mid:])
        keep = add_low(keep[:mid], got[:mid])
        got = swap(give, "rows", bit)
    return add_low(keep[0], got[0])


class Chain:
    def __init__(self, parts, top):
        self.top, self.at, self.keep = top, 0, parts[0]
        self.flight = [swap(p, "rows", o) for o, p in enumerate(parts) if o]

    def advance(self):
        self.at += 1
        got = self.flight
        if self.at == 1:
            total = self.keep.astype(F32)
            for x in got:
                total = total + x.astype(F32)
            self.keep = total.astype(BF)
            self.flight = [swap(self.keep, "rows", self.top)]
        elif self.at == 2:
            self.keep = add_low(self.keep, got[0])
            self.flight = [swap(self.keep, "rows", o) for o in (1, 2, 3)]
        else:
            self.done = [self.keep, *got]


def meet(chains, *xs):
    flights, xs = lax.optimization_barrier(([c.flight for c in chains], xs))
    for c, flight in zip(chains, flights, strict=True):
        c.flight = flight
        c.advance()
    return xs


def per_device(
    features,
    crop_ids,
    timesteps,
    clip_embed,
    context,
    norm1_gain,
    norm1_bias,
    conv1_weight,
    conv1_bias,
    embed_weight,
    embed_bias,
    norm2_gain,
    norm2_bias,
    conv2_weight,
    conv2_bias,
    norm3_gain,
    norm3_bias,
    qkv_weight,
    qkv_bias,
    encoder_weight,
    encoder_bias,
    proj_weight,
    proj_bias,
    out_grad,
):
    batches, ch, pixels = features.shape
    rows_n = lax.axis_size("rows")
    nch = lax.axis_size("ch")
    half = rows_n // 2
    r = lax.axis_index("rows")
    me = lax.axis_index("ch")
    m, j = r // half, r % half
    even = r % 2 == 0
    n = 2 * pixels
    e = n + 2 * HP
    local_rows = n // W
    copies = half * nch
    offs = offsets(nch)
    flat = rows_n * nch
    teams = [list(range(copies)), list(range(copies, flat))]
    me1 = jnp.reshape(me, (1,)).astype(jnp.int32)

    evens, odds = range(0, rows_n, 2), range(1, rows_n, 2)
    first_perm = [(i, i // 2) for i in evens] + [(i, half + i // 2) for i in odds]
    second_perm = [(i, half + i // 2) for i in evens] + [(i, i // 2) for i in odds]

    def halo_perm(up, down):
        pairs = [(i, up * half + i // 2 - 1) for i in evens if i // 2 > 0]
        return pairs + [(i, down * half + i // 2 + 1) for i in odds if i // 2 < half - 1]

    def reshard(x):
        a = jnp.where(even, x[0], x[1])
        b = jnp.where(even, x[1], x[0])
        one = lax.ppermute(a, "rows", first_perm)
        two = lax.ppermute(b, "rows", second_perm)
        edge = jnp.where(even, x[:, :, :HP], x[:, :, pixels - HP :])
        three = lax.ppermute(jnp.where(even, edge[0], edge[1]), "rows", halo_perm(0, 1))
        four = lax.ppermute(jnp.where(even, edge[1], edge[0]), "rows", halo_perm(1, 0))
        return one, two, three, four

    def resharded(one, two, three, four):
        low = jnp.where(m == 0, one, two)
        high = jnp.where(m == 0, two, one)
        below = jnp.where(m == 0, three, four)
        above = jnp.where(m == 0, four, three)
        return jnp.concatenate([above, low, high, below], axis=1)

    def send_back(y):
        low, high = y[:, :pixels], y[:, pixels:]
        one = lax.ppermute(jnp.where(m == 0, low, high), "rows", [(b, a) for a, b in first_perm])
        two = lax.ppermute(jnp.where(m == 0, high, low), "rows", [(b, a) for a, b in second_perm])
        return one, two

    def sent_back(one, two):
        return jnp.stack([jnp.where(even, one, two), jnp.where(even, two, one)])

    def to_next(x):
        return lax.ppermute(
            x, "rows", [(i, i + 1) for i in range(rows_n - 1) if i % half != half - 1]
        )

    def to_prev(x):
        return lax.ppermute(x, "rows", [(i, i - 1) for i in range(1, rows_n) if i % half != 0])

    def team_exchange(x):
        got = lax.all_to_all(x, ("rows", "ch"), 0, 0, axis_index_groups=teams)
        return got.reshape((half, nch) + x.shape[1:])

    ids = lax.dynamic_index_in_dim(crop_ids, m, 0, keepdims=False)
    grid = jnp.pad(ids.reshape(-1, W), ((2, 2), (0, 0)), constant_values=-1)
    lab20 = lax.dynamic_slice_in_dim(grid, j * local_rows, local_rows + 4, 0)
    near = jnp.pad(lab20, 1, constant_values=-2)
    height = local_rows + 4
    masks = jnp.stack(
        [
            (near[1 + di : 1 + di + height, 1 + dj : 1 + dj + W] == lab20) & (lab20 >= 0)
            for di, dj in TAPS
        ]
    ).astype(F32)
    masks = jnp.pad(masks.reshape(9, e), ((0, 7), (0, 0)))
    lab = lab20.reshape(1, e)
    crops = jnp.arange(NC, dtype=jnp.int32)
    counted = jnp.sum((ids[None, :] == crops[:, None]).astype(F32), axis=1)
    cnt = jnp.maximum(counted, 1.0)[None, :] * GSZ

    w1 = conv1_weight.transpose(1, 2, 0, 3).reshape(9, ch, C)
    w2 = conv2_weight.transpose(1, 2, 0, 3).reshape(9, ch, C)


    def packed(o):
        at = (me ^ o) * ch
        return jnp.concatenate(
            [
                lax.dynamic_slice_in_dim(w1, at, ch, 2),
                lax.dynamic_slice_in_dim(w2, at, ch, 2),
                lax.dynamic_slice_in_dim(proj_weight, at, ch, 1)[None],
            ],
            axis=0,
        )

    parts = reshard(jnp.concatenate([features, out_grad], axis=1))
    x_own = resharded(*[x[:ch] for x in parts])
    g_own = resharded(*[x[ch:] for x in parts])
    x_own, w1, w2, proj_weight, clip_embed = fence(x_own, w1, w2, proj_weight, clip_embed)
    packs = [packed(o) for o in offs]

    half_width = EMB // 2
    frequency = jnp.exp(-math.log(10000.0) * jnp.arange(half_width, dtype=F32) / half_width)
    angles = timesteps.astype(F32)[:, None] * frequency[None, :]
    embedded = jax.nn.silu(
        jnp.concatenate([jnp.cos(angles), jnp.sin(angles)], axis=1) + clip_embed
    )
    modulation = (
        jnp.einsum("be,jce->bjc", embedded, embed_weight.astype(F32), precision=PRECISE)
        + embed_bias
    )
    mod_here = lax.dynamic_index_in_dim(modulation, m, 0, keepdims=False)
    zero = jnp.zeros((1, ch), F32)

    def params(*rows):
        given = [x.reshape(1, ch).astype(F32) for x in rows]
        return jnp.concatenate(given + [zero] * (8 - len(given)), axis=0)

    par1 = params(norm1_gain, norm1_bias)
    par2 = params(norm2_gain, norm2_bias, mod_here[0], mod_here[1])
    par3 = params(norm3_gain, norm3_bias)

    x_slots = gather_ch(x_own)
    pay = sd((copies, 24, ch), F32)
    st = pltpu.VMEM((ch, 128), F32)
    (pay1,) = call(k_stats, (x_own, lab, par1), (pay,), [st], smem=0)
    recv1 = team_exchange(pay1)
    x_slots, recv1, g_own, packs = fence(x_slots, recv1, g_own, packs)
    g_slots = first_hops(g_own)
    conv_scratch = [
        pltpu.VMEM((3, 3 * ch, e), F32),
        pltpu.VMEM((ch, e), F32),
        pltpu.VMEM((C, NC), F32),
        pltpu.VMEM((C, NC), F32),
    ]
    conv_flops = 2 * 9 * ch * C * e

    low1, pay2, h1 = call(
        functools.partial(k_conv, nch, offs, False),
        (me1, recv1, cnt, lab, masks, w1, conv1_bias[:, None], par2, *x_slots),
        (sd((ch, e), BF), pay, sd((C, e), BF)),
        conv_scratch + [st],
        flops=conv_flops,
    )
    low1, pay2, g_slots = fence(low1, pay2, g_slots)
    c1_slots = gather_ch(low1)
    recv2 = team_exchange(pay2)
    c1_slots, recv2, g_slots, qkv_weight = fence(c1_slots, recv2, g_slots, qkv_weight)
    g_slots, wq_slots = last_hops(g_slots), first_hops(qkv_weight)
    low2, pay3, h2, resid = call(
        functools.partial(k_conv, nch, offs, True),
        (me1, recv2, cnt, lab, masks, w2, conv2_bias[:, None], par3, *c1_slots, x_own),
        (sd((ch, n), BF), pay, sd((C, e), BF), sd((ch, n), F32)),
        conv_scratch + [st],
        flops=conv_flops,
    )
    low2, pay3, g_slots, wq_slots = fence(low2, pay3, g_slots, wq_slots)
    r_slots = gather_ch(low2)
    recv3 = team_exchange(pay3)
    r_slots, recv3, packs, wq_slots = fence(r_slots, recv3, packs, wq_slots)
    wq_slots = last_hops(wq_slots)
    packs = [w if o == 0 else swap(w, "ch", o) for o, w in zip(offs, packs, strict=True)]
    res_full, att_in, q, k, v = call(
        functools.partial(k_qkv, nch, offs),
        (me1, recv3, cnt, lab, qkv_weight, qkv_bias[0][:, None], qkv_bias[1][:, None], *r_slots),
        (sd((C, n), BF), sd((C, n), BF), sd((ch, n), BF), sd((ch, n), BF), sd((ch, n), BF)),
        [pltpu.VMEM((C, NC), F32), pltpu.VMEM((C, NC), F32)],
        flops=2 * 3 * ch * C * n,
    )
    q, k, v, wq_slots = fence(q, k, v, wq_slots)
    res_top, res_bot = to_next(res_full[:, n - HP :]), to_prev(res_full[:, :HP])
    row_bits = bits_of(half)
    k_parts, k_map = gather_rows(k, row_bits)
    v_parts, v_map = gather_rows(v, list(reversed(row_bits)))
    k_back, v_back = list(reversed(row_bits)), row_bits

    g_full, grad_att = call(
        functools.partial(k_gout, nch, offs),
        (me1, proj_weight, *g_slots),
        (sd((C, e), BF), sd((ch, n), BF)),
        flops=2 * ch * C * n,
    )
    ctx = lax.dynamic_index_in_dim(context, m, 0, keepdims=False)
    encoded = (
        jnp.einsum("te,jde->jdt", ctx, encoder_weight, preferred_element_type=F32)
        + encoder_bias[:, :, None]
    ).astype(BF)

    tiles = ids.reshape(half, n)
    key_ids = jnp.concatenate(
        [lax.dynamic_slice_in_dim(tiles, j ^ o, 1, 0) for o in range(half)], axis=1
    )
    crops16 = jnp.arange(16, dtype=jnp.int32)[:, None]
    one_k = jnp.where((key_ids == crops16) | (crops16 >= NC), 0.0, -FAR).astype(BF)
    one_q = (lab[:, HP : HP + n] == crops16).astype(BF)
    heads = ch // HD
    keys = half * n + 128
    tq = n if half * n <= 4096 else 256
    k_parts, v_parts, res_top, res_bot, grad_att, encoded = fence(
        k_parts, v_parts, res_top, res_bot, grad_att, encoded
    )
    attended, dq, dk0, dk1, dv0, dv1, dck, dcv = call(
        functools.partial(
            k_attend, k_map, v_map, len(k_parts), len(v_parts), order_of(k_back), order_of(v_back)
        ),
        (q, grad_att, one_q, one_k, encoded[0], encoded[1], *k_parts, *v_parts),
        (
            sd((ch, n), BF),
            sd((ch, n), BF),
            sd((half // 2, ch, n), BF),
            sd((half // 2, ch, n), BF),
            sd((half // 2, ch, n), BF),
            sd((half // 2, ch, n), BF),
            sd((ch, 128), F32),
            sd((ch, 128), F32),
        ),
        [
            pltpu.VMEM((heads, HD + 16, keys), BF),
            pltpu.VMEM((heads, HD, keys), BF),
            pltpu.VMEM((tq, keys), BF),
            pltpu.VMEM((tq, keys), F32),
            pltpu.VMEM((ch, keys), F32),
            pltpu.VMEM((ch, keys), F32),
        ],
        smem=0,
        flops=6 * 2 * heads * n * keys * HD,
        limit=60,
    )
    dk0, dk1, dv0, dv1, dq, attended, packs = fence(dk0, dk1, dv0, dv1, dq, attended, packs)
    got_k, got_v = swap(dk1, "rows", k_back[0]), swap(dv1, "rows", v_back[0])
    dq_slots = first_hops(dq)
    w1t, w2t, wqt, pwt = call(
        functools.partial(k_turn, nch, offs),
        (me1, *packs, *wq_slots),
        (sd((9, ch, C), BF), sd((9, ch, C), BF), sd((3, C, C), BF), sd((ch, C), BF)),
        [pltpu.VMEM((C, ch), F32), pltpu.VMEM((C, C), F32)],
    )
    got_k, got_v, w1t, w2t, wqt, pwt, dq_slots, attended = fence(
        got_k, got_v, w1t, w2t, wqt, pwt, dq_slots, attended
    )
    dk = scatter_rows(dk0, got_k, k_back)
    dv = scatter_rows(dv0, got_v, v_back)
    dq_slots, a_slots = last_hops(dq_slots), first_hops(attended)
    dk, dv, dq_slots, a_slots = fence(dk, dv, dq_slots, a_slots)
    a_slots = last_hops(a_slots)
    dk_slots = gather_ch(dk)
    dv_slots = gather_ch(dv)
    ga, pay_t = call(
        functools.partial(k_gattend, nch, offs),
        (me1, recv3, cnt, lab, wqt, res_full, *dq_slots, *dk_slots, *dv_slots),
        (sd((C, n), BF), sd((copies, 16, ch), F32)),
        [
            pltpu.VMEM((3, C, n), BF),
            pltpu.VMEM((C, n), F32),
            st,
        ],
        flops=2 * 3 * C * C * n,
    )
    ga, pay_t, dq, dk, dv, attended, a_slots = fence(ga, pay_t, dq, dk, dv, attended, a_slots)
    recv_t = team_exchange(pay_t)
    ga_top, ga_bot = to_next(ga[:, n - HP :]), to_prev(ga[:, :HP])
    split = rows_n == 8 and ch % 64 == 0
    me4 = jnp.stack([me, r % 4, m]).astype(jnp.int32)
    st8 = sd((8, ch), F32)
    pieces = [sd((9, ch // 4, C), BF)] * 4 if split else [sd((9, ch, C), BF)]

    def begin(parts):
        return Chain(parts, 4) if split else lax.psum(parts[0], "rows")

    def finish(total):
        if not split:
            return total.astype(F32)
        while total.at < 3:
            meet([total])
        return call(k_place, (me4, *total.done), (sd((9, ch, C), F32),))[0]

    def moving(*chains):
        return list(chains) if split else []

    early, early_st = call(
        k_early,
        (me4, dq, dk, dv, att_in, attended, g_full, dck, dcv),
        (sd((5, ch, C), BF), st8),
        flops=2 * 4 * ch * C * n,
    )
    early_sum = lax.psum(early, "rows")
    (out_own,) = call(
        functools.partial(k_proj, nch, offs),
        (me1, resid, proj_bias[:, None], pwt, *a_slots),
        (sd((ch, n), BF),),
        [pltpu.VMEM((C, n), BF)],
        flops=2 * ch * C * n,
    )
    recv_t, ga_top, ga_bot, early_st, out_own = fence(recv_t, ga_top, ga_bot, early_st, out_own)
    out_parts = send_back(out_own)
    gp2, pay_u, gc2, grad_resid = call(
        functools.partial(k_back2, nch),
        (
            me1, recv3, recv_t, recv2, cnt, lab, masks, w2t,
            ga, ga_top, ga_bot, res_full, res_top, res_bot, g_full, low1,
        ),
        (sd((ch, e), BF), sd((copies, 16, ch), F32), sd((ch, n), BF), sd((ch, n), F32)),
        [
            pltpu.VMEM((C, e), BF),
            pltpu.VMEM((3, 3 * ch, e), F32),
            pltpu.VMEM((ch, e), F32),
            pltpu.VMEM((C, NC), F32),
            pltpu.VMEM((C, NC), F32),
            pltpu.VMEM((C, NC), F32),
            st,
            pltpu.VMEM((C, e), F32),
        ],
        flops=conv_flops,
    )
    gp2, pay_u, gc2, out_parts = fence(gp2, pay_u, gc2, out_parts)
    output = sent_back(*out_parts)
    gp_slots = gather_ch(gp2)
    recv_u = team_exchange(pay_u)
    wg_scratch = [pltpu.VMEM((9 * ch, e), BF), pltpu.VMEM((3 * ch, C), F32)]
    *wg2, wg2_st = call(
        functools.partial(k_wgrad2, split),
        (me4, masks, gc2, h2),
        (*pieces, st8),
        wg_scratch,
        flops=conv_flops,
    )

    recv_u, gp_slots, wg2 = fence(recv_u, gp_slots, wg2)
    wg2 = begin(wg2)
    *wg1, wg1_st = call(
        functools.partial(k_wgrad1, split),
        (me4, recv2, recv_u, cnt, lab, masks, gp2, low1, h1),
        (*pieces, st8),
        wg_scratch,
        flops=conv_flops,
    )
    wg1, gp_slots = meet(moving(wg2), wg1, gp_slots)
    wg1 = begin(wg1)
    gp1, pay_v = call(
        functools.partial(k_back1, nch, offs),
        (
            me1, recv1, recv2, recv_u, cnt, lab, masks, w1t, x_own,
            wg1_st, wg2_st, early_st, pay_u, pay_t, *gp_slots, *c1_slots,
        ),
        (sd((ch, n), F32), sd((rows_n, 32, ch), F32)),
        [
            pltpu.VMEM((C, e), BF),
            pltpu.VMEM((3, 3 * ch, e), F32),
            pltpu.VMEM((ch, e), F32),
            pltpu.VMEM((C, NC), F32),
            pltpu.VMEM((C, NC), F32),
            pltpu.VMEM((C, NC), F32),
            st,
        ],
        flops=conv_flops,
    )
    gp1, pay_v = meet(moving(wg2, wg1), gp1, pay_v)
    recv_v = lax.all_to_all(pay_v, "rows", 0, 0)
    (recv_v,) = meet(moving(wg2, wg1), recv_v)
    line = sd((1, ch), F32)
    fg, mod_grad, embed_bias_grad, qkv_bias_grad, *lines = call(
        k_last,
        (
            jnp.stack([me, m]).astype(jnp.int32),
            recv1, recv_v, cnt, lab, gp1, x_own, grad_resid,
            params(norm2_gain, norm2_bias, modulation[0, 0], modulation[1, 0]),
        ),
        (sd((ch, n), BF), sd((4, ch), F32), sd((2, ch), F32), sd((2, ch), F32), *[line] * 9),
        [pltpu.VMEM((2, 32, ch), F32)],
    )
    fg_parts = send_back(fg)
    wg2_sum = finish(wg2)
    fg_parts, early_sum = fence(fg_parts, early_sum)
    features_grad = sent_back(*fg_parts)
    wg1_sum = finish(wg1)

    n1g, n1b, c1b, n2g, n2b, c2b, n3g, n3b, pb = [x.reshape(ch) for x in lines]
    mod_grad = mod_grad.reshape(2, 2, ch)
    embed_weight_grad = (
        mod_grad[0][:, :, None] * embedded[0][None, None, :]
        + mod_grad[1][:, :, None] * embedded[1][None, None, :]
    )
    encoder_grad = early_sum[4].reshape(ch, batches, 2, -1)
    encoder_weight_grad = jnp.einsum(
        "dbjt,bte->jde", encoder_grad, context, preferred_element_type=F32
    )
    encoder_bias_grad = jnp.sum(encoder_grad.astype(F32), axis=(1, 3)).T

    def conv_out(x):
        return x.reshape(3, 3, ch, C).transpose(2, 0, 1, 3)

    return (
        output,
        features_grad,
        n1g,
        n1b,
        conv_out(wg1_sum),
        c1b,
        embed_weight_grad,
        embed_bias_grad,
        n2g,
        n2b,
        conv_out(wg2_sum),
        c2b,
        n3g,
        n3b,
        early_sum[:3].astype(F32),
        qkv_bias_grad,
        encoder_weight_grad,
        encoder_bias_grad,
        early_sum[3].astype(F32),
        pb,
    )


def solution(mesh):
    placed = (
        P(None, "ch", "rows"),
        P(),
        P(),
        P(),
        P(),
        P("ch"),
        P("ch"),
        P("ch", None, None, None),
        P("ch"),
        P(None, "ch", None),
        P(None, "ch"),
        P("ch"),
        P("ch"),
        P("ch", None, None, None),
        P("ch"),
        P("ch"),
        P("ch"),
        P(None, "ch", None),
        P(None, "ch"),
        P(None, "ch", None),
        P(None, "ch"),
        P("ch", None),
        P("ch"),
        P(None, "ch", "rows"),
    )
    return jax.shard_map(
        per_device,
        mesh=mesh,
        in_specs=placed,
        out_specs=(
            P(None, "ch", "rows"),
            P(None, "ch", "rows"),
            P("ch"),
            P("ch"),
            P("ch", None, None, None),
            P("ch"),
            P(None, "ch", None),
            P(None, "ch"),
            P("ch"),
            P("ch"),
            P("ch", None, None, None),
            P("ch"),
            P("ch"),
            P("ch"),
            P(None, "ch", None),
            P(None, "ch"),
            P(None, "ch", None),
            P(None, "ch"),
            P("ch", None),
            P("ch"),
        ),
        check_vma=False,
    )
```

```python
import functools
import math

import jax
import jax.numpy as jnp
from jax import lax
from jax.experimental import pallas as pl
from jax.experimental.pallas import tpu as pltpu
from jax.sharding import PartitionSpec as P

C = 512
HD = 64
GSZ = 16
EMB = 2048
W = 64
NCROP = 6
NC = 8
HP = 2 * W
TAPS = [(di, dj) for di in (-1, 0, 1) for dj in (-1, 0, 1)]

PRECISE = lax.Precision.HIGHEST
EPSILON = 1e-05
FAR = 2.0**100
SCORE = HD**-0.5
LOG2E = 1.4426950408889634
F32 = jnp.float32
BF = jnp.bfloat16


def spread(vals, lab):
    acc = vals[:, 0:1]
    for n in range(1, NCROP):
        acc = jnp.where(lab == n, vals[:, n : n + 1], acc)
    return acc


def crop_columns(first, second, lab):
    rows = first.shape[0]
    lane = lax.broadcasted_iota(jnp.int32, (rows, 128), 1)
    acc = jnp.zeros((rows, 128), F32)
    for n in range(NCROP):
        inside = lab == n
        one = jnp.sum(jnp.where(inside, first, 0.0), axis=1, keepdims=True)
        two = jnp.sum(jnp.where(inside, second, 0.0), axis=1, keepdims=True)
        acc = jnp.where(lane == n, one, acc)
        acc = jnp.where(lane == NC + n, two, acc)
    return acc


def put_column(acc, column, at):
    lane = lax.broadcasted_iota(jnp.int32, acc.shape, 1)
    return jnp.where(lane == at, column, acc)


def grouped(vals):
    rows, width = vals.shape
    parts = jnp.sum(vals.reshape(rows // GSZ, GSZ, width), axis=1, keepdims=True)
    return jnp.broadcast_to(parts, (rows // GSZ, GSZ, width)).reshape(rows, width)


def turned(block):
    rows, cols = block.shape
    if rows < 128:
        block = jnp.concatenate([block, jnp.zeros((128 - rows, cols), F32)], axis=0)
    return jnp.transpose(block)


def read_stats(recv_ref, which, cnt):
    members = recv_ref.shape[0]
    block = recv_ref[0, which]
    for g in range(1, members):
        other = recv_ref[g, which]
        block = jnp.concatenate([block[:16] + other[:16], block[16:]], axis=0)
    cols = turned(block)
    sums = grouped(cols[:, :16])
    mean = sums[:, :NC] / cnt
    inv = lax.rsqrt(sums[:, NC:16] / cnt - mean * mean + EPSILON)
    return mean, inv, cols[:, 16:17], cols[:, 17:18], cols[:, 18:19], cols[:, 19:20]


def read_sums(recv_ref, which):
    members = recv_ref.shape[0]
    block = recv_ref[0, which][:16]
    for g in range(1, members):
        block = block + recv_ref[g, which][:16]
    return turned(block)


def affine_of(stats):
    mean, inv, gain, bias, scale, offset = stats
    a = inv * gain * (1.0 + scale)
    b = (bias - mean * inv * gain) * (1.0 + scale) + offset
    return a, b


def sigmoid(v):
    return 0.5 * (1.0 + jnp.tanh(0.5 * v))


def slope(v):
    s = sigmoid(v)
    return s * (1.0 + v * (1.0 - s))


def masked_conv(w_ref, h_ref, y_ref, out_ref, mask_ref, bias):
    ch, width = out_ref.shape
    for g in range(3):
        w = w_ref[3 * g : 3 * g + 3].reshape(3 * ch, C)
        y_ref[g] = jnp.dot(w, h_ref[...], preferred_element_type=F32)
    size = min(ch, 64)

    def body(i, carry):
        i = pl.multiple_of(i * size, size)
        acc = None
        for g in range(3):
            for k in range(3):
                tap = 3 * g + k
                off = W * (g - 1) + k - 1
                y = y_ref[g, pl.ds(pl.multiple_of(k * ch + i, size), size), :]
                y = y if off == 0 else pltpu.roll(y, (-off) % width, 1)
                y = y * mask_ref[tap : tap + 1, :]
                acc = y if acc is None else acc + y
        if bias is not None:
            acc = acc + bias[pl.ds(i, size), 7:8]
        out_ref[pl.ds(i, size), :] = acc
        return carry

    lax.fori_loop(0, ch // size, body, 0)


def chunks(rows, body):
    size = min(128, rows)

    def step(i, carry):
        body(pl.multiple_of(i * size, size), size)
        return carry

    lax.fori_loop(0, rows // size, step, 0)


def send_rows(out_ref, st_ref, params):
    rows = jnp.transpose(st_ref[...])[:16]
    if params is not None:
        rows = jnp.concatenate([rows, params], axis=0)
    for k in range(out_ref.shape[0]):
        out_ref[k] = rows


def k_stats(x_ref, lab_ref, par_ref, out_ref, st_ref):
    n = x_ref.shape[1] - 2 * HP
    lab = lab_ref[:, HP : HP + n]

    def body(i, size):
        v = x_ref[pl.ds(i, size), HP : HP + n].astype(F32)
        st_ref[pl.ds(i, size), :] = crop_columns(v, v * v, lab)

    chunks(x_ref.shape[0], body)
    send_rows(out_ref, st_ref, par_ref[...])


def k_conv(nch, offs, resid, *refs):
    me_ref, recv_ref, cnt_ref, lab_ref, mask_ref, w_ref, par_ref = refs[:7]
    slots = refs[7 : 7 + nch]
    refs = refs[7 + nch :]
    if resid:
        x_ref, refs = refs[0], refs[1:]
        low_ref, pay_ref, h_ref, full_ref = refs[:4]
        refs = refs[4:]
    else:
        low_ref, pay_ref, h_ref = refs[:3]
        refs = refs[3:]
    y_ref, acc_ref, a_ref, b2_ref, st_ref = refs
    me = me_ref[0]
    ch, e = acc_ref.shape
    n = e - 2 * HP
    lab = lab_ref[...]
    for c in range(nch):
        a, b = affine_of(read_stats(recv_ref, c, cnt_ref[...]))
        a_ref[c * ch : (c + 1) * ch, :] = a
        b2_ref[c * ch : (c + 1) * ch, :] = b
    for s in range(nch):
        base = pl.multiple_of((me ^ offs[s]) * ch, ch)

        def body(i, size, s=s, base=base):
            row = pl.multiple_of(base + i, size)
            v = slots[s][pl.ds(i, size), :].astype(F32)
            pre = v * spread(a_ref[pl.ds(row, size), :], lab) + spread(b2_ref[pl.ds(row, size), :], lab)
            low = (pre * sigmoid(pre)).astype(BF)
            h_ref[pl.ds(row, size), :] = low

        chunks(ch, body)
    st_ref[...] = turned(par_ref[...])
    masked_conv(w_ref, h_ref, y_ref, acc_ref, mask_ref, st_ref)
    labc = lab[:, HP : HP + n]

    def finish(i, size):
        if resid:
            v = acc_ref[pl.ds(i, size), HP : HP + n] + x_ref[pl.ds(i, size), HP : HP + n].astype(F32)
            full_ref[pl.ds(i, size), :] = v
            low_ref[pl.ds(i, size), :] = v.astype(BF)
        else:
            low_ref[pl.ds(i, size), :] = acc_ref[pl.ds(i, size), :].astype(BF)
            v = acc_ref[pl.ds(i, size), HP : HP + n]
        st_ref[pl.ds(i, size), :] = crop_columns(v, v * v, labc)

    chunks(ch, finish)
    send_rows(pay_ref, st_ref, par_ref[...])


def k_qkv(nch, offs, *refs):
    me_ref, recv_ref, cnt_ref, lab_ref, w_ref, par_ref = refs[:6]
    slots = refs[6 : 6 + nch]
    res_ref, att_ref, q_ref, k_ref, v_ref, a_ref, b_ref = refs[6 + nch :]
    biases = turned(par_ref[...])
    me = me_ref[0]
    ch, n = q_ref.shape
    lab = lab_ref[:, HP : HP + n]
    for c in range(nch):
        a, b = affine_of(read_stats(recv_ref, c, cnt_ref[...]))
        a_ref[c * ch : (c + 1) * ch, :] = a
        b_ref[c * ch : (c + 1) * ch, :] = b
    for s in range(nch):
        base = pl.multiple_of((me ^ offs[s]) * ch, ch)

        def body(i, size, s=s, base=base):
            row = pl.multiple_of(base + i, size)
            low = slots[s][pl.ds(i, size), :]
            res_ref[pl.ds(row, size), :] = low
            out = low.astype(F32) * spread(a_ref[pl.ds(row, size), :], lab) + spread(
                b_ref[pl.ds(row, size), :], lab
            )
            att_ref[pl.ds(row, size), :] = out.astype(BF)

        chunks(ch, body)
    tile = 256

    def mul(i, _):
        at = pl.ds(pl.multiple_of(i * tile, tile), tile)
        x = att_ref[:, at]
        q_ref[:, at] = (jnp.dot(w_ref[0], x, preferred_element_type=F32) + biases[:, 0:1]).astype(BF)
        k_ref[:, at] = jnp.dot(w_ref[1], x, preferred_element_type=F32).astype(BF)
        v_ref[:, at] = (jnp.dot(w_ref[2], x, preferred_element_type=F32) + biases[:, 1:2]).astype(BF)
        return 0

    lax.fori_loop(0, n // tile, mul, 0)


def k_gout(nch, offs, *refs):
    me_ref, w_ref = refs[:2]
    slots = refs[2 : 2 + nch]
    g_ref, ga_ref = refs[2 + nch :]
    me = me_ref[0]
    ch, n = ga_ref.shape
    for s in range(nch):
        base = pl.multiple_of((me ^ offs[s]) * ch, ch)
        g_ref[pl.ds(base, ch), :] = slots[s][...]
    ga_ref[...] = jnp.dot(w_ref[...], g_ref[:, HP : HP + n], preferred_element_type=F32).astype(BF)


def k_turn(nch, offs, *refs):
    me_ref = refs[0]
    ins = refs[1 : 1 + nch]
    wqs = refs[1 + nch : 1 + 2 * nch]
    w1_ref, w2_ref, wq_ref, pw_ref, scr, scq = refs[1 + 2 * nch :]
    me = me_ref[0]
    ch = w1_ref.shape[1]
    for t in range(19):
        for s in range(nch):
            base = pl.multiple_of((me ^ offs[s]) * ch, ch)
            scr[pl.ds(base, ch), :] = ins[s][t].astype(F32)
        out = jnp.transpose(scr[...]).astype(BF)
        if t < 9:
            w1_ref[8 - t] = out
        elif t < 18:
            w2_ref[17 - t] = out
        else:
            pw_ref[...] = out
    for j in range(3):
        for s in range(nch):
            base = pl.multiple_of((me ^ offs[s]) * ch, ch)
            scq[pl.ds(base, ch), :] = wqs[s][j].astype(F32)
        wq_ref[j] = jnp.transpose(scq[...]).astype(BF)


def nt(a, b):
    return lax.dot_general(a, b, (((1,), (1,)), ((), ())), preferred_element_type=F32)


def tn(a, b):
    return lax.dot_general(a, b, (((0,), (0,)), ((), ())), preferred_element_type=F32)


def k_attend(kmap, vmap, nk, nv, korder, vorder, *refs):
    q_ref, ga_ref, oneq_ref, onek_ref, ck_ref, cv_ref = refs[:6]
    kparts = refs[6 : 6 + nk]
    vparts = refs[6 + nk : 6 + nk + nv]
    out_ref, dq_ref, dk0_ref, dk1_ref, dv0_ref, dv1_ref, dck_ref, dcv_ref = refs[
        6 + nk + nv : 14 + nk + nv
    ]
    ks_ref, vs_ref, e_ref, s_ref, ak_ref, av_ref = refs[14 + nk + nv :]
    ch, n = q_ref.shape
    heads = ch // HD
    slots = len(kmap)
    keys = slots * n
    tq = e_ref.shape[0]
    con = SCORE * LOG2E
    for h in range(heads):
        hs = slice(h * HD, (h + 1) * HD)
        for s in range(slots):
            i, j = kmap[s]
            ks_ref[h, 0:HD, s * n : (s + 1) * n] = kparts[i][j, hs, :]
            i, j = vmap[s]
            vs_ref[h, :, s * n : (s + 1) * n] = vparts[i][j, hs, :]
        ks_ref[h, HD : HD + 16, 0:keys] = onek_ref[...]
        ks_ref[h, 0:HD, keys:] = ck_ref[hs, :]
        ks_ref[h, HD : HD + 16, keys:] = jnp.zeros((16, 128), BF)
        vs_ref[h, :, keys:] = cv_ref[hs, :]
    once = n == tq
    if not once:
        ak_ref[...] = jnp.zeros_like(ak_ref)
        av_ref[...] = jnp.zeros_like(av_ref)
    spans = [(s * n, n) for s in range(slots)] + [(keys, 128)]

    for h in range(heads):
        hs = slice(h * HD, (h + 1) * HD)

        def block(b, _, h=h, hs=hs):
            at = pl.ds(pl.multiple_of(b * tq, tq), tq)
            qb = q_ref[hs, at]
            gb = ga_ref[hs, at]
            qa = jnp.transpose(
                jnp.concatenate([qb.astype(F32), oneq_ref[:, at].astype(F32)], axis=0)
            ).astype(BF)
            gt = jnp.transpose(gb.astype(F32))
            gtb = gt.astype(BF)
            top = jnp.full((tq, 128), -jnp.inf, F32)
            for k0, kn in spans:
                sc = jnp.dot(qa, ks_ref[h, :, k0 : k0 + kn], preferred_element_type=F32)
                s_ref[:, k0 : k0 + kn] = sc
                for u in range(kn // 128):
                    top = jnp.maximum(top, sc[:, u * 128 : (u + 1) * 128])
            top = jnp.max(top, axis=1, keepdims=True) * con
            tot = jnp.zeros((tq, 128), F32)
            acc = jnp.zeros((HD, tq), F32)
            for k0, kn in spans:
                ex = jnp.exp2(s_ref[:, k0 : k0 + kn] * con - top)
                for u in range(kn // 128):
                    tot = tot + ex[:, u * 128 : (u + 1) * 128]
                exb = ex.astype(BF)
                e_ref[:, k0 : k0 + kn] = exb
                acc = acc + nt(vs_ref[h, :, k0 : k0 + kn], exb)
            inv = 1.0 / jnp.sum(tot, axis=1, keepdims=True)
            acc = jnp.transpose(acc) * inv
            delta = jnp.sum(acc * gt, axis=1, keepdims=True)
            out_ref[hs, at] = jnp.transpose(acc).astype(BF)
            ql = jnp.transpose(qa[:, :HD].astype(F32) * (inv * SCORE)).astype(BF)
            gl = jnp.transpose(gt * inv).astype(BF)
            dq = jnp.zeros((HD, tq), F32)
            for k0, kn in spans:
                dp = jnp.dot(gtb, vs_ref[h, :, k0 : k0 + kn], preferred_element_type=F32)
                exb = e_ref[:, k0 : k0 + kn]
                ds = (exb.astype(F32) * (dp - delta)).astype(BF)
                dq = dq + nt(ks_ref[h, 0:HD, k0 : k0 + kn], ds)
                dk = jnp.dot(ql, ds, preferred_element_type=F32)
                dv = jnp.dot(gl, exb, preferred_element_type=F32)
                if not once:
                    dk = dk + ak_ref[hs, k0 : k0 + kn]
                    dv = dv + av_ref[hs, k0 : k0 + kn]
                ak_ref[hs, k0 : k0 + kn] = dk
                av_ref[hs, k0 : k0 + kn] = dv
            dq_ref[hs, at] = jnp.transpose(jnp.transpose(dq) * (inv * SCORE)).astype(BF)
            return 0

        lax.fori_loop(0, n // tq, block, 0)
    for order, acc_ref, outs in (
        (korder, ak_ref, (dk0_ref, dk1_ref)),
        (vorder, av_ref, (dv0_ref, dv1_ref)),
    ):
        for side in range(2):
            for i, s in enumerate(order[side]):
                outs[side][i] = acc_ref[:, s * n : (s + 1) * n].astype(BF)
    dck_ref[...] = ak_ref[:, keys:]
    dcv_ref[...] = av_ref[:, keys:]


def k_proj(nch, offs, *refs):
    me_ref, res_ref, par_ref, pw_ref = refs[:4]
    atts = refs[4 : 4 + nch]
    out_ref, att_s = refs[4 + nch :]
    me = me_ref[0]
    ch = res_ref.shape[0]
    for s in range(nch):
        base = pl.multiple_of((me ^ offs[s]) * ch, ch)
        att_s[pl.ds(base, ch), :] = atts[s][...]
    mixed = jnp.dot(pw_ref[...], att_s[...], preferred_element_type=F32)
    out_ref[...] = (res_ref[...] + mixed + turned(par_ref[...])[:, 2:3]).astype(BF)


def k_gattend(nch, offs, *refs):
    me_ref, recv_ref, cnt_ref, lab_ref, w_ref, res_ref = refs[:6]
    slots = [refs[6 + j * nch : 6 + (j + 1) * nch] for j in range(3)]
    ga_ref, pay_ref, d_s, acc_ref, st_ref = refs[6 + 3 * nch :]
    me = me_ref[0]
    n = ga_ref.shape[1]
    ch = C // nch
    lab = lab_ref[:, HP : HP + n]
    for j in range(3):
        for s in range(nch):
            base = pl.multiple_of((me ^ offs[s]) * ch, ch)
            d_s[j, pl.ds(base, ch), :] = slots[j][s][...]
    tile = 256

    def mul(i, _):
        at = pl.ds(pl.multiple_of(i * tile, tile), tile)
        acc = jnp.dot(w_ref[0], d_s[0, :, at], preferred_element_type=F32)
        acc = acc + jnp.dot(w_ref[1], d_s[1, :, at], preferred_element_type=F32)
        acc = acc + jnp.dot(w_ref[2], d_s[2, :, at], preferred_element_type=F32)
        acc_ref[:, at] = acc
        ga_ref[:, at] = acc.astype(BF)
        return 0

    lax.fori_loop(0, n // tile, mul, 0)
    mean, inv = read_stats(recv_ref, me, cnt_ref[...])[:2]
    own = pl.ds(pl.multiple_of(me * ch, ch), ch)
    ga = acc_ref[own, :]
    normed = (res_ref[own, :].astype(F32) - spread(mean, lab)) * spread(inv, lab)
    st_ref[...] = crop_columns(ga, ga * normed, lab)
    send_rows(pay_ref, st_ref, None)


def k_early(blocks, *refs):
    me_ref, dq_ref, in_ref, att_ref, g_ref, dck_ref, dcv_ref, out_ref, st_ref = refs
    ch, n = dq_ref.shape
    own = g_ref[pl.ds(pl.multiple_of(me_ref[0] * ch, ch), ch), HP : HP + n].astype(F32)
    acc = put_column(jnp.zeros((ch, 128), F32), jnp.sum(own, axis=1, keepdims=True), 1)
    dq = dq_ref[...]
    acc = put_column(acc, jnp.sum(dq.astype(F32), axis=1, keepdims=True), 0)
    both = jnp.concatenate([dck_ref[...], dcv_ref[...]], axis=1)
    ctx = jnp.concatenate([jnp.where(me_ref[2] == i, both, 0.0) for i in range(2)], axis=1)
    rows = ch // blocks
    for t, full in enumerate(
        (nt(dq, in_ref[...]), nt(att_ref[...], g_ref[:, HP : HP + n]), ctx)
    ):
        full = full.astype(BF)
        for i in range(blocks):
            out_ref[i, t] = full[i * rows : (i + 1) * rows]
    st_ref[...] = jnp.transpose(acc)[:8]


def norm_back(mean, inv, gain, t1, t2, cnt):
    m1 = grouped(gain * t1) / cnt
    m2 = grouped(gain * t2) / cnt
    return inv * gain, -inv * inv * m2, inv * (mean * inv * m2 - m1)


def k_back2(nch, split, *refs):
    (me_ref, recv3_ref, recvt_ref, recv2_ref, cnt_ref, lab_ref, mask_ref, w_ref) = refs[:8]
    ga_ref, res_ref, top_ref, bot_ref, g_ref, c1_ref, h2_ref = refs[8:15]
    more = refs[15:18]
    gp_ref, pay_ref, gr_ref = refs[18:21]
    outs, wst_ref = refs[21:-11], refs[-11]
    h_ref, y_ref, acc_ref, a_ref, b_ref, c_ref, st_ref, full_ref, w_scr, wy_ref = refs[-10:]
    me = me_ref[0]
    ch, e = acc_ref.shape
    n = e - 2 * HP
    lab = lab_ref[...]
    cnt = cnt_ref[...]
    for c in range(nch):
        sl = slice(c * ch, (c + 1) * ch)
        mean, inv, gain = read_stats(recv3_ref, c, cnt)[:3]
        t = read_sums(recvt_ref, c)
        a, b, cc = norm_back(mean, inv, gain, t[:, :NC], t[:, NC:16], cnt)
        a_ref[sl, :] = a
        b_ref[sl, :] = b
        c_ref[sl, :] = cc

    def body(i, size):
        row = pl.ds(i, size)
        low = pl.ds(pl.multiple_of(C + i, size), size)
        ga = jnp.concatenate([top_ref[row, :], ga_ref[row, :], bot_ref[row, :]], axis=1).astype(F32)
        v = jnp.concatenate([top_ref[low, :], res_ref[row, :], bot_ref[low, :]], axis=1).astype(F32)
        gr = (
            g_ref[row, :].astype(F32)
            + ga * spread(a_ref[row, :], lab)
            + v * spread(b_ref[row, :], lab)
            + spread(c_ref[row, :], lab)
        )
        full_ref[row, :] = gr
        h_ref[row, :] = gr.astype(BF)

    chunks(C, body)
    own = pl.multiple_of(me * ch, ch)
    gr_ref[...] = full_ref[pl.ds(own, ch), HP : HP + n]
    masked_conv(w_ref, h_ref, y_ref, acc_ref, mask_ref, None)
    stats = None
    mean, inv, gain, bias, scale, offset = read_stats(recv2_ref, me, cnt)
    a, b = affine_of((mean, inv, gain, bias, scale, offset))
    a_ref[0:ch, :] = a
    b_ref[0:ch, :] = b
    c_ref[0:ch, :] = inv
    a_ref[ch : 2 * ch, :] = -mean * inv

    def finish(i, size):
        row = pl.ds(i, size)
        v = c1_ref[row, :].astype(F32)
        pre = v * spread(a_ref[row, :], lab) + spread(b_ref[row, :], lab)
        gp = acc_ref[row, :] * slope(pre)
        gp_ref[row, :] = gp.astype(BF)
        labc = lab[:, HP : HP + n]
        normed = v[:, HP : HP + n] * spread(c_ref[row, :], labc) + spread(
            a_ref[pl.ds(pl.multiple_of(ch + i, size), size), :], labc
        )
        gpc = gp[:, HP : HP + n]
        acc = crop_columns(gpc, gpc * normed, labc)
        st_ref[row, :] = acc

    chunks(ch, finish)
    send_rows(pay_ref, st_ref, None)
    gc = gr_ref[...].astype(BF).astype(F32)
    wgrad_body(split, me_ref[1], gc, h2_ref, mask_ref, outs, wst_ref, w_scr, wy_ref, more)


def wgrad_body(split, pos, gc, h_ref, mask_ref, outs, st_ref, g_ref, y_ref, more=()):
    ch, n = gc.shape
    width = n + 2 * HP
    edge = jnp.zeros((ch, HP), F32)
    wide = jnp.concatenate([edge, gc, edge], axis=1)
    for t, (di, dj) in enumerate(TAPS):
        off = W * di + dj
        moved = wide * mask_ref[t : t + 1, :]
        moved = moved if off == 0 else pltpu.roll(moved, off % width, 1)
        g_ref[t * ch : (t + 1) * ch, :] = moved.astype(BF)
    rows = ch // 4

    def hand_out(k, t):
        if not split:
            outs[0][t] = y_ref[k * ch : (k + 1) * ch, :].astype(BF)
            return
        for o in range(4):
            at = pl.multiple_of(k * ch + (pos ^ o) * rows, rows)
            outs[o][t] = y_ref[pl.ds(at, rows), :].astype(BF)

    for g in range(3):
        y_ref[...] = nt(g_ref[3 * g * ch : 3 * (g + 1) * ch, :], h_ref[...])
        for k in range(3):
            hand_out(k, 3 * g + k)
    acc = jnp.zeros((ch, 128), F32)
    acc = put_column(acc, jnp.sum(gc, axis=1, keepdims=True), 0)
    if more:
        for k in range(2):
            y_ref[k * ch : (k + 1) * ch, :] = nt(more[k][...], more[2][...])
            hand_out(k, 9 + k)
        column = jnp.sum(more[1][...].astype(F32), axis=1, keepdims=True)
        acc = put_column(acc, column, 1)
    st_ref[...] = jnp.transpose(acc)[:8]


def k_place(me_ref, *refs):
    parts, out_ref = refs[:-1], refs[-1]
    rows = parts[0].shape[1]
    for o, part in enumerate(parts):
        at = pl.ds(pl.multiple_of((me_ref[1] ^ o) * rows, rows), rows)
        out_ref[:, at, :] = part[...].astype(F32)


def k_place2(me_ref, early_ref, *refs):
    parts, (out_ref, qkv_ref, proj_ref) = refs[:-3], refs[-3:]
    rows = parts[0].shape[1]
    for o, part in enumerate(parts):
        at = pl.ds(pl.multiple_of((me_ref[1] ^ o) * rows, rows), rows)
        out_ref[:, at, :] = part[:9].astype(F32)
        qkv_ref[1:3, at, :] = part[9:].astype(F32)
    low = early_ref.shape[2]
    for i in range(early_ref.shape[0]):
        qkv_ref[0, i * low : (i + 1) * low, :] = early_ref[i, 0].astype(F32)
        proj_ref[i * low : (i + 1) * low, :] = early_ref[i, 1].astype(F32)


def conv1_back(recv2_ref, recvu_ref, which, cnt):
    mean, inv, gain, _, scale, _ = read_stats(recv2_ref, which, cnt)
    u = read_sums(recvu_ref, which)
    return norm_back(mean, inv, gain * (1.0 + scale), u[:, :NC], u[:, NC:16], cnt)


def k_wgrad1(split, *refs):
    me_ref, recv2_ref, recvu_ref, cnt_ref, lab_ref, mask_ref, gp_ref, c1_ref, h_ref = refs[:9]
    outs, (st_ref, g_ref, y_ref) = refs[9:-3], refs[-3:]
    n = gp_ref.shape[1] - 2 * HP
    lab = lab_ref[:, HP : HP + n]
    a, b, c = conv1_back(recv2_ref, recvu_ref, me_ref[0], cnt_ref[...])
    gc = (
        gp_ref[:, HP : HP + n].astype(F32) * spread(a, lab)
        + c1_ref[:, HP : HP + n].astype(F32) * spread(b, lab)
        + spread(c, lab)
    ).astype(BF).astype(F32)
    wgrad_body(split, me_ref[1], gc, h_ref, mask_ref, outs, st_ref, g_ref, y_ref)


def k_back1(nch, offs, *refs):
    me_ref, recv1_ref, recv2_ref, recvu_ref, cnt_ref, lab_ref, mask_ref, w_ref, x_ref = refs[:9]
    wg1_ref, wg2_ref, early_ref, payu_ref, payt_ref = refs[9:14]
    gps = refs[14 : 14 + nch]
    c1s = refs[14 + nch : 14 + 2 * nch]
    gp1_ref, pay_ref = refs[14 + 2 * nch : 16 + 2 * nch]
    h_ref, y_ref, acc_ref, a_ref, b_ref, c_ref, st_ref = refs[16 + 2 * nch :]
    me = me_ref[0]
    ch, e = acc_ref.shape
    n = e - 2 * HP
    lab = lab_ref[...]
    cnt = cnt_ref[...]
    for c in range(nch):
        sl = slice(c * ch, (c + 1) * ch)
        a, b, cc = conv1_back(recv2_ref, recvu_ref, c, cnt)
        a_ref[sl, :] = a
        b_ref[sl, :] = b
        c_ref[sl, :] = cc
    for s in range(nch):
        base = pl.multiple_of((me ^ offs[s]) * ch, ch)

        def body(i, size, s=s, base=base):
            row = pl.multiple_of(base + i, size)
            at = pl.ds(row, size)
            gc = (
                gps[s][pl.ds(i, size), :].astype(F32) * spread(a_ref[at, :], lab)
                + c1s[s][pl.ds(i, size), :].astype(F32) * spread(b_ref[at, :], lab)
                + spread(c_ref[at, :], lab)
            )
            h_ref[at, :] = gc.astype(BF)

        chunks(ch, body)
    masked_conv(w_ref, h_ref, y_ref, acc_ref, mask_ref, None)
    stats = read_stats(recv1_ref, me, cnt)
    a, b = affine_of(stats)
    a_ref[0:ch, :] = a
    b_ref[0:ch, :] = b
    c_ref[0:ch, :] = stats[1]
    c_ref[ch : 2 * ch, :] = -stats[0] * stats[1]
    labc = lab[:, HP : HP + n]

    def finish(i, size):
        row = pl.ds(i, size)
        v = x_ref[row, HP : HP + n].astype(F32)
        pre = v * spread(a_ref[row, :], labc) + spread(b_ref[row, :], labc)
        gp = acc_ref[row, HP : HP + n] * slope(pre)
        gp1_ref[row, :] = gp
        normed = v * spread(c_ref[row, :], labc) + spread(
            c_ref[pl.ds(pl.multiple_of(ch + i, size), size), :], labc
        )
        st_ref[row, :] = crop_columns(gp, gp * normed, labc)

    chunks(ch, finish)
    u, t = payu_ref[0], payt_ref[0]
    smalls = jnp.zeros((16, ch), F32)
    at = lax.broadcasted_iota(jnp.int32, (16, ch), 0)
    for i, line in enumerate(
        (
            wg1_ref[0:1],
            wg2_ref[0:1],
            jnp.sum(u[:NC], axis=0, keepdims=True),
            jnp.sum(u[NC:], axis=0, keepdims=True),
            early_ref[1:2],
            early_ref[0:1],
            wg2_ref[1:2],
            jnp.sum(t[:NC], axis=0, keepdims=True),
            jnp.sum(t[NC:], axis=0, keepdims=True),
        )
    ):
        smalls = jnp.where(at == i, line, smalls)
    send_rows(pay_ref, st_ref, smalls)


def k_last(*refs):
    me_ref, recv1_ref, recvv_ref, cnt_ref, lab_ref, gp_ref, x_ref, gr_ref, par_ref = refs[:9]
    o_ref, one_ref, two_ref, mod_ref, emb_ref, qb_ref = refs[9:15]
    (n1g, n1b, c1b, n2g, n2b, c2b, n3g, n3b, pb) = refs[15:24]
    sum_ref, out_ref = refs[24:]
    ch, n = gp_ref.shape
    half = recvv_ref.shape[0] // 2
    lab = lab_ref[:, HP : HP + n]
    for m in range(2):
        tot = recvv_ref[m * half]
        for g in range(1, half):
            tot = tot + recvv_ref[m * half + g]
        sum_ref[m] = tot
    cnt = cnt_ref[...]
    mean, inv, gain = read_stats(recv1_ref, me_ref[0], cnt)[:3]
    v = turned(sum_ref[me_ref[1]][:16])
    a, b, c = norm_back(mean, inv, gain, v[:, :NC], v[:, NC:16], cnt)
    out = (
        gr_ref[...]
        + gp_ref[...] * spread(a, lab)
        + x_ref[:, HP : HP + n].astype(F32) * spread(b, lab)
        + spread(c, lab)
    )
    out_ref[0:ch, :] = o_ref[...].astype(F32)
    out_ref[ch:, :] = out
    mid = n // 2
    sides = out_ref[:, :mid], out_ref[:, mid:]
    one_ref[...] = jnp.where(me_ref[1] == 0, sides[0], sides[1]).astype(BF)
    two_ref[...] = jnp.where(me_ref[1] == 0, sides[1], sides[0]).astype(BF)
    both = sum_ref[0] + sum_ref[1]
    n1b[...] = jnp.sum(both[:NC], axis=0, keepdims=True)
    n1g[...] = jnp.sum(both[NC:16], axis=0, keepdims=True)
    for ref, at in ((c1b, 16), (c2b, 17), (pb, 20), (n3b, 23), (n3g, 24)):
        ref[...] = both[at : at + 1]
    qb_ref[...] = both[21:23]
    u1 = [sum_ref[m, 18:19] for m in range(2)]
    u2 = [sum_ref[m, 19:20] for m in range(2)]
    up = [1.0 + par_ref[2 + m : 3 + m] for m in range(2)]
    n2b[...] = up[0] * u1[0] + up[1] * u1[1]
    n2g[...] = up[0] * u2[0] + up[1] * u2[1]
    scales = [par_ref[0:1] * u2[m] + par_ref[1:2] * u1[m] for m in range(2)]
    mod_ref[...] = jnp.concatenate([scales[0], u1[0], scales[1], u1[1]], axis=0)
    emb_ref[...] = jnp.concatenate([scales[0] + scales[1], u1[0] + u1[1]], axis=0)


COST = {"k_stats": 2, "k_conv": 10, "k_qkv": 6, "k_gout": 3, "k_attend": 34, "k_turn": 5, "k_proj": 3, "k_gattend": 7, "k_early": 4, "k_back2": 17, "k_wgrad1": 5, "k_back1": 13, "k_last": 3, "k_place": 3, "k_place2": 3}
SM = pl.BlockSpec(memory_space=pltpu.SMEM)
VM = pl.BlockSpec(memory_space=pltpu.VMEM)


def call(kernel, args, outs, scratch=(), smem=1, flops=0, limit=60):
    name = getattr(kernel, "func", kernel).__name__
    flops = int(COST[name] * 1.15e9)
    bytes_all = sum(math.prod(a.shape) * a.dtype.itemsize for a in list(args) + list(outs))
    return pl.pallas_call(
        kernel,
        out_shape=tuple(outs),
        in_specs=[SM] * smem + [VM] * (len(args) - smem),
        out_specs=tuple(VM for _ in outs),
        scratch_shapes=list(scratch),
        compiler_params=pltpu.CompilerParams(vmem_limit_bytes=limit * 2**20),
        cost_estimate=pl.CostEstimate(flops=flops, bytes_accessed=bytes_all, transcendentals=0),
    )(*args)


def fence(*xs):
    return lax.optimization_barrier(xs)


def sd(shape, dtype):
    return jax.ShapeDtypeStruct(shape, dtype)


def swap(x, axis, bit):
    count = lax.axis_size(axis)
    return lax.ppermute(x, axis, [(i, i ^ bit) for i in range(count)])


def bits_of(count):
    return [1 << i for i in range(count.bit_length() - 1)]


def offsets(count):
    offs = [0]
    for bit in reversed(bits_of(count)):
        offs = offs + [o ^ bit for o in offs]
    return offs


def gather_ch(x):
    slots = [x]
    for bit in reversed(bits_of(lax.axis_size("ch"))):
        slots = slots + [swap(s, "ch", bit) for s in slots]
    return slots


def first_hops(x):
    return [x] + [swap(x, "ch", bit) for bit in reversed(bits_of(lax.axis_size("ch")))]


def last_hops(hops):
    bits = list(reversed(bits_of(lax.axis_size("ch"))))
    slots = [hops[0]]
    for at, bit in enumerate(bits):
        slots = slots + [hops[at + 1]] + [swap(s, "ch", bit) for s in slots[1:]]
    return slots


def gather_rows(x, bits):
    parts, places, offs = [x[None]], [(0, 0)], [0]
    for bit in bits:
        whole = parts[0] if len(parts) == 1 else jnp.concatenate(parts, axis=0)
        base = len(parts)
        parts = parts + [swap(whole, "rows", bit)]
        places = places + [(base, i) for i in range(len(offs))]
        offs = offs + [o ^ bit for o in offs]
    table = dict(zip(offs, places, strict=True))
    return parts, [table[o] for o in range(len(offs))]


def order_of(bits):
    keep = [0]
    for bit in reversed(bits[1:]):
        keep = keep + [o ^ bit for o in keep]
    return keep, [o ^ bits[0] for o in keep]


def add_low(a, b):
    return (a.astype(F32) + b.astype(F32)).astype(BF)


def scatter_rows(keep, got, bits):
    for bit in bits[1:]:
        mid = keep.shape[0] // 2
        give = add_low(keep[mid:], got[mid:])
        keep = add_low(keep[:mid], got[:mid])
        got = swap(give, "rows", bit)
    return add_low(keep[0], got[0])


class Chain:
    def __init__(self, parts, top):
        self.top, self.at, self.keep = top, 0, parts[0]
        self.flight = [swap(p, "rows", o) for o, p in enumerate(parts) if o]

    def advance(self):
        self.at += 1
        got = self.flight
        if self.at == 1:
            total = self.keep.astype(F32)
            for x in got:
                total = total + x.astype(F32)
            self.keep = total.astype(BF)
            self.flight = [swap(self.keep, "rows", self.top)]
        elif self.at == 2:
            self.keep = add_low(self.keep, got[0])
            self.flight = [swap(self.keep, "rows", o) for o in (1, 2, 3)]
        else:
            self.done = [self.keep, *got]


def meet(chains, *xs):
    flights, xs = lax.optimization_barrier(([c.flight for c in chains], xs))
    for c, flight in zip(chains, flights, strict=True):
        c.flight = flight
        c.advance()
    return xs


def per_device(
    features,
    crop_ids,
    timesteps,
    clip_embed,
    context,
    norm1_gain,
    norm1_bias,
    conv1_weight,
    conv1_bias,
    embed_weight,
    embed_bias,
    norm2_gain,
    norm2_bias,
    conv2_weight,
    conv2_bias,
    norm3_gain,
    norm3_bias,
    qkv_weight,
    qkv_bias,
    encoder_weight,
    encoder_bias,
    proj_weight,
    proj_bias,
    out_grad,
):
    batches, ch, pixels = features.shape
    rows_n = lax.axis_size("rows")
    nch = lax.axis_size("ch")
    half = rows_n // 2
    r = lax.axis_index("rows")
    me = lax.axis_index("ch")
    m, j = r // half, r % half
    even = r % 2 == 0
    n = 2 * pixels
    e = n + 2 * HP
    local_rows = n // W
    copies = half * nch
    offs = offsets(nch)
    flat = rows_n * nch
    teams = [list(range(copies)), list(range(copies, flat))]
    me1 = jnp.reshape(me, (1,)).astype(jnp.int32)
    me4 = jnp.stack([me, r % 4, m]).astype(jnp.int32)
    st8 = sd((8, ch), F32)

    evens, odds = range(0, rows_n, 2), range(1, rows_n, 2)
    first_perm = [(i, i // 2) for i in evens] + [(i, half + i // 2) for i in odds]
    second_perm = [(i, half + i // 2) for i in evens] + [(i, i // 2) for i in odds]

    def halo_perm(up, down):
        pairs = [(i, up * half + i // 2 - 1) for i in evens if i // 2 > 0]
        return pairs + [(i, down * half + i // 2 + 1) for i in odds if i // 2 < half - 1]

    def reshard(*xs):
        def side(when, cut):
            return jnp.concatenate([jnp.where(when, cut(x[0]), cut(x[1])) for x in xs], axis=0)

        def edge(x):
            return jnp.where(even, x[:, :HP], x[:, pixels - HP :])

        def all_of(x):
            return x

        one = lax.ppermute(side(even, all_of), "rows", first_perm)
        two = lax.ppermute(side(~even, all_of), "rows", second_perm)
        three = lax.ppermute(side(even, edge), "rows", halo_perm(0, 1))
        four = lax.ppermute(side(~even, edge), "rows", halo_perm(1, 0))
        return one, two, three, four

    def resharded(one, two, three, four):
        low = jnp.where(m == 0, one, two)
        high = jnp.where(m == 0, two, one)
        below = jnp.where(m == 0, three, four)
        above = jnp.where(m == 0, four, three)
        return jnp.concatenate([above, low, high, below], axis=1)

    def to_next(x):
        return lax.ppermute(
            x, "rows", [(i, i + 1) for i in range(rows_n - 1) if i % half != half - 1]
        )

    def to_prev(x):
        return lax.ppermute(x, "rows", [(i, i - 1) for i in range(1, rows_n) if i % half != 0])

    def team_exchange(x):
        got = lax.all_to_all(x, ("rows", "ch"), 0, 0, axis_index_groups=teams)
        return got.reshape((half, nch) + x.shape[1:])

    ids = lax.dynamic_index_in_dim(crop_ids, m, 0, keepdims=False)
    grid = jnp.pad(ids.reshape(-1, W), ((2, 2), (0, 0)), constant_values=-1)
    lab20 = lax.dynamic_slice_in_dim(grid, j * local_rows, local_rows + 4, 0)
    near = jnp.pad(lab20, 1, constant_values=-2)
    height = local_rows + 4
    masks = jnp.stack(
        [
            (near[1 + di : 1 + di + height, 1 + dj : 1 + dj + W] == lab20) & (lab20 >= 0)
            for di, dj in TAPS
        ]
    ).astype(F32)
    masks = jnp.pad(masks.reshape(9, e), ((0, 7), (0, 0)))
    lab = lab20.reshape(1, e)
    crops = jnp.arange(NC, dtype=jnp.int32)
    counted = jnp.sum((ids[None, :] == crops[:, None]).astype(F32), axis=1)
    cnt = jnp.maximum(counted, 1.0)[None, :] * GSZ

    w1 = conv1_weight.transpose(1, 2, 0, 3).reshape(9, ch, C)
    w2 = conv2_weight.transpose(1, 2, 0, 3).reshape(9, ch, C)

    parts = reshard(features, out_grad)
    x_own = resharded(*[x[:ch] for x in parts])
    g_own = resharded(*[x[ch:] for x in parts])
    x_own, clip_embed = fence(x_own, clip_embed)

    half_width = EMB // 2
    frequency = jnp.exp(-math.log(10000.0) * jnp.arange(half_width, dtype=F32) / half_width)
    angles = timesteps.astype(F32)[:, None] * frequency[None, :]
    embedded = jax.nn.silu(
        jnp.concatenate([jnp.cos(angles), jnp.sin(angles)], axis=1) + clip_embed
    )
    modulation = (
        jnp.einsum("be,jce->bjc", embedded, embed_weight.astype(F32), precision=PRECISE)
        + embed_bias
    )
    mod_here = lax.dynamic_index_in_dim(modulation, m, 0, keepdims=False)
    zero = jnp.zeros((1, ch), F32)

    def params(*rows):
        given = [x.reshape(1, ch).astype(F32) for x in rows]
        return jnp.concatenate(given + [zero] * (8 - len(given)), axis=0)

    par1 = params(norm1_gain, norm1_bias)
    blank = jnp.zeros((ch,), F32)
    par2 = params(norm2_gain, norm2_bias, mod_here[0], mod_here[1], blank, blank, blank, conv1_bias)
    par3 = params(norm3_gain, norm3_bias, blank, blank, blank, blank, blank, conv2_bias)
    par4 = params(qkv_bias[0], qkv_bias[1], proj_bias)

    x_slots = gather_ch(x_own)
    pay = sd((copies, 24, ch), F32)
    st = pltpu.VMEM((ch, 128), F32)
    (pay1,) = call(k_stats, (x_own, lab, par1), (pay,), [st], smem=0)
    recv1 = team_exchange(pay1)
    x_slots, recv1, g_own = fence(x_slots, recv1, g_own)
    g_slots = first_hops(g_own)
    conv_scratch = [
        pltpu.VMEM((3, 3 * ch, e), F32),
        pltpu.VMEM((ch, e), F32),
        pltpu.VMEM((C, NC), F32),
        pltpu.VMEM((C, NC), F32),
    ]
    conv_flops = 2 * 9 * ch * C * e

    low1, pay2, h1 = call(
        functools.partial(k_conv, nch, offs, False),
        (me1, recv1, cnt, lab, masks, w1, par2, *x_slots),
        (sd((ch, e), BF), pay, sd((C, e), BF)),
        conv_scratch + [st],
        flops=conv_flops,
    )
    low1, pay2, g_slots, w1, w2_cut, proj_weight_cut = fence(low1, pay2, g_slots, w1, w2, proj_weight)


    def packed(o):
        at = (me ^ o) * ch
        return jnp.concatenate(
            [
                lax.dynamic_slice_in_dim(w1, at, ch, 2),
                lax.dynamic_slice_in_dim(w2_cut, at, ch, 2),
                lax.dynamic_slice_in_dim(proj_weight_cut, at, ch, 1)[None],
            ],
            axis=0,
        )

    packs = [packed(o) for o in offs]
    c1_slots = gather_ch(low1)
    recv2 = team_exchange(pay2)
    c1_slots, recv2, g_slots, qkv_weight = fence(c1_slots, recv2, g_slots, qkv_weight)
    g_slots, wq_slots = last_hops(g_slots), first_hops(qkv_weight)
    low2, pay3, h2, resid = call(
        functools.partial(k_conv, nch, offs, True),
        (me1, recv2, cnt, lab, masks, w2, par3, *c1_slots, x_own),
        (sd((ch, n), BF), pay, sd((C, e), BF), sd((ch, n), F32)),
        conv_scratch + [st],
        flops=conv_flops,
    )
    low2, pay3, g_slots, wq_slots = fence(low2, pay3, g_slots, wq_slots)
    r_slots = gather_ch(low2)
    recv3 = team_exchange(pay3)
    r_slots, recv3, packs, wq_slots = fence(r_slots, recv3, packs, wq_slots)
    wq_slots = last_hops(wq_slots)
    packs = [w if o == 0 else swap(w, "ch", o) for o, w in zip(offs, packs, strict=True)]
    res_full, att_in, q, k, v = call(
        functools.partial(k_qkv, nch, offs),
        (me1, recv3, cnt, lab, qkv_weight, par4, *r_slots),
        (sd((C, n), BF), sd((C, n), BF), sd((ch, n), BF), sd((ch, n), BF), sd((ch, n), BF)),
        [pltpu.VMEM((C, NC), F32), pltpu.VMEM((C, NC), F32)],
        flops=2 * 3 * ch * C * n,
    )
    q, k, v, wq_slots = fence(q, k, v, wq_slots)
    row_bits = bits_of(half)
    k_parts, k_map = gather_rows(k, row_bits)
    v_parts, v_map = gather_rows(v, list(reversed(row_bits)))
    k_back, v_back = list(reversed(row_bits)), row_bits

    g_full, grad_att = call(
        functools.partial(k_gout, nch, offs),
        (me1, proj_weight, *g_slots),
        (sd((C, e), BF), sd((ch, n), BF)),
        flops=2 * ch * C * n,
    )
    ctx = lax.dynamic_index_in_dim(context, m, 0, keepdims=False)
    encoded = (
        jnp.einsum("te,jde->jdt", ctx, encoder_weight, preferred_element_type=F32)
        + encoder_bias[:, :, None]
    ).astype(BF)

    tiles = ids.reshape(half, n)
    key_ids = jnp.concatenate(
        [lax.dynamic_slice_in_dim(tiles, j ^ o, 1, 0) for o in range(half)], axis=1
    )
    crops16 = jnp.arange(16, dtype=jnp.int32)[:, None]
    one_k = jnp.where((key_ids == crops16) | (crops16 >= NC), 0.0, -FAR).astype(BF)
    one_q = (lab[:, HP : HP + n] == crops16).astype(BF)
    heads = ch // HD
    keys = half * n + 128
    tq = n if half * n <= 4096 else 256
    k_parts, v_parts, grad_att, encoded = fence(k_parts, v_parts, grad_att, encoded)
    attended, dq, dk0, dk1, dv0, dv1, dck, dcv = call(
        functools.partial(
            k_attend, k_map, v_map, len(k_parts), len(v_parts), order_of(k_back), order_of(v_back)
        ),
        (q, grad_att, one_q, one_k, encoded[0], encoded[1], *k_parts, *v_parts),
        (
            sd((ch, n), BF),
            sd((ch, n), BF),
            sd((half // 2, ch, n), BF),
            sd((half // 2, ch, n), BF),
            sd((half // 2, ch, n), BF),
            sd((half // 2, ch, n), BF),
            sd((ch, 128), F32),
            sd((ch, 128), F32),
        ),
        [
            pltpu.VMEM((heads, HD + 16, keys), BF),
            pltpu.VMEM((heads, HD, keys), BF),
            pltpu.VMEM((tq, keys), BF),
            pltpu.VMEM((tq, keys), F32),
            pltpu.VMEM((ch, keys), F32),
            pltpu.VMEM((ch, keys), F32),
        ],
        smem=0,
        flops=6 * 2 * heads * n * keys * HD,
        limit=60,
    )
    dk0, dk1, dv0, dv1, dq, attended, packs = fence(dk0, dk1, dv0, dv1, dq, attended, packs)
    got_k, got_v = swap(dk1, "rows", k_back[0]), swap(dv1, "rows", v_back[0])
    dq_slots = first_hops(dq)
    w1t, w2t, wqt, pwt = call(
        functools.partial(k_turn, nch, offs),
        (me1, *packs, *wq_slots),
        (sd((9, ch, C), BF), sd((9, ch, C), BF), sd((3, C, C), BF), sd((ch, C), BF)),
        [pltpu.VMEM((C, ch), F32), pltpu.VMEM((C, C), F32)],
    )
    split = rows_n == 8 and ch % 128 == 0
    blocks = rows_n if split else 1
    early, early_st = call(
        functools.partial(k_early, blocks),
        (me4, dq, att_in, attended, g_full, dck, dcv),
        (sd((blocks, 3, ch // blocks, C), BF), st8),
    )
    got_k, got_v, w1t, w2t, wqt, pwt, dq_slots, attended, early, early_st = fence(
        got_k, got_v, w1t, w2t, wqt, pwt, dq_slots, attended, early, early_st
    )
    dk = scatter_rows(dk0, got_k, k_back)
    dv = scatter_rows(dv0, got_v, v_back)
    dq_slots, a_slots = last_hops(dq_slots), first_hops(attended)
    dk, dv, dq_slots, a_slots, early = fence(dk, dv, dq_slots, a_slots, early)
    early = lax.all_to_all(early, "rows", 0, 0) if split else lax.psum(early, "rows")
    a_slots = last_hops(a_slots)
    dk_slots = gather_ch(dk)
    dv_slots = gather_ch(dv)
    (out_own,) = call(
        functools.partial(k_proj, nch, offs),
        (me1, resid, par4, pwt, *a_slots),
        (sd((ch, n), BF),),
        [pltpu.VMEM((C, n), BF)],
        flops=2 * ch * C * n,
    )
    dk_slots, dv_slots, out_own = fence(dk_slots, dv_slots, out_own)
    ga, pay_t = call(
        functools.partial(k_gattend, nch, offs),
        (me1, recv3, cnt, lab, wqt, res_full, *dq_slots, *dk_slots, *dv_slots),
        (sd((C, n), BF), sd((copies, 16, ch), F32)),
        [
            pltpu.VMEM((3, C, n), BF),
            pltpu.VMEM((C, n), F32),
            st,
        ],
        flops=2 * 3 * C * C * n,
    )
    if split:
        ga, pay_t, early = fence(ga, pay_t, early)
        early = jnp.sum(early.astype(F32), axis=0).astype(BF)
        early = lax.all_to_all(jnp.broadcast_to(early[None], (blocks, *early.shape)), "rows", 0, 0)
    recv_t = team_exchange(pay_t)
    top = to_next(jnp.concatenate([ga[:, n - HP :], res_full[:, n - HP :]], axis=0))
    bottom = to_prev(jnp.concatenate([ga[:, :HP], res_full[:, :HP]], axis=0))
    def pieces(units):
        return [sd((units, ch // 4, C), BF)] * 4 if split else [sd((units, ch, C), BF)]

    def begin(parts):
        return Chain(parts, 4) if split else lax.psum(parts[0], "rows")

    def moving(*chains):
        return list(chains) if split else []

    recv_t, top, bottom = fence(recv_t, top, bottom)
    wg_scratch = [pltpu.VMEM((9 * ch, e), BF), pltpu.VMEM((3 * ch, C), F32)]
    gp2, pay_u, grad_resid, *wg2, wg2_st = call(
        functools.partial(k_back2, nch, split),
        (
            me4, recv3, recv_t, recv2, cnt, lab, masks, w2t,
            ga, res_full, top, bottom, g_full, low1, h2, dk, dv, att_in,
        ),
        (sd((ch, e), BF), sd((copies, 16, ch), F32), sd((ch, n), F32), *pieces(11), st8),
        [
            pltpu.VMEM((C, e), BF),
            pltpu.VMEM((3, 3 * ch, e), F32),
            pltpu.VMEM((ch, e), F32),
            pltpu.VMEM((C, NC), F32),
            pltpu.VMEM((C, NC), F32),
            pltpu.VMEM((C, NC), F32),
            st,
            pltpu.VMEM((C, e), F32),
            *wg_scratch,
        ],
        flops=conv_flops,
    )
    gp2, pay_u, early_sum = fence(gp2, pay_u, early)
    gp_slots = first_hops(gp2)
    recv_u = team_exchange(pay_u)
    gp_slots = last_hops(gp_slots)
    wg2 = begin(wg2)
    *wg1, wg1_st = call(
        functools.partial(k_wgrad1, split),
        (me4, recv2, recv_u, cnt, lab, masks, gp2, low1, h1),
        (*pieces(9), st8),
        wg_scratch,
        flops=conv_flops,
    )
    wg1, gp_slots = meet(moving(wg2), wg1, gp_slots)
    wg1 = begin(wg1)
    gp1, pay_v = call(
        functools.partial(k_back1, nch, offs),
        (
            me1, recv1, recv2, recv_u, cnt, lab, masks, w1t, x_own,
            wg1_st, wg2_st, early_st, pay_u, pay_t, *gp_slots, *c1_slots,
        ),
        (sd((ch, n), F32), sd((rows_n, 32, ch), F32)),
        [
            pltpu.VMEM((C, e), BF),
            pltpu.VMEM((3, 3 * ch, e), F32),
            pltpu.VMEM((ch, e), F32),
            pltpu.VMEM((C, NC), F32),
            pltpu.VMEM((C, NC), F32),
            pltpu.VMEM((C, NC), F32),
            st,
        ],
        flops=conv_flops,
    )
    (gp1,) = meet(moving(wg2, wg1), gp1)
    recv_v = lax.all_to_all(pay_v, "rows", 0, 0)
    line = sd((1, ch), F32)
    one, two, mod_grad, embed_bias_grad, qkv_bias_grad, *lines = call(
        k_last,
        (
            jnp.stack([me, m]).astype(jnp.int32),
            recv1, recv_v, cnt, lab, gp1, x_own, grad_resid,
            params(norm2_gain, norm2_bias, modulation[0, 0], modulation[1, 0]), out_own,
        ),
        (*[sd((2 * ch, pixels), BF)] * 2, sd((4, ch), F32), sd((2, ch), F32), sd((2, ch), F32), *[line] * 9),
        [pltpu.VMEM((2, 32, ch), F32), pltpu.VMEM((2 * ch, n), F32)],
    )
    one, two = meet(moving(wg2, wg1), one, two)
    one = lax.ppermute(one, "rows", [(b, a) for a, b in first_perm])
    two = lax.ppermute(two, "rows", [(b, a) for a, b in second_perm])
    output, features_grad = [
        jnp.stack([jnp.where(even, x, y), jnp.where(even, y, x)])
        for x, y in ((one[:ch], two[:ch]), (one[ch:], two[ch:]))
    ]
    placed = (sd((9, ch, C), F32), sd((3, ch, C), F32), sd((ch, C), F32))
    if split:
        wg2_sum, qkv_sum, proj_sum = call(k_place2, (me4, early_sum, *wg2.done), placed)
        meet([wg1])
        (wg1_sum,) = call(k_place, (me4, *wg1.done), placed[:1])
    else:
        wg2_sum, wg1_sum = wg2[:9].astype(F32), wg1.astype(F32)
        qkv_sum = jnp.concatenate([early_sum[0, :1], wg2[9:]], axis=0).astype(F32)
        proj_sum = early_sum[0, 1].astype(F32)

    n1g, n1b, c1b, n2g, n2b, c2b, n3g, n3b, pb = [x.reshape(ch) for x in lines]
    mod_grad = mod_grad.reshape(2, 2, ch)
    embed_weight_grad = (
        mod_grad[0][:, :, None] * embedded[0][None, None, :]
        + mod_grad[1][:, :, None] * embedded[1][None, None, :]
    )
    encoder_grad = early_sum[:, 2].reshape(ch, batches, 2, -1)
    encoder_weight_grad = jnp.einsum(
        "dbjt,bte->jde", encoder_grad, context, preferred_element_type=F32
    )
    encoder_bias_grad = jnp.sum(encoder_grad.astype(F32), axis=(1, 3)).T

    def conv_out(x):
        return x.reshape(3, 3, ch, C).transpose(2, 0, 1, 3)

    return (
        output,
        features_grad,
        n1g,
        n1b,
        conv_out(wg1_sum),
        c1b,
        embed_weight_grad,
        embed_bias_grad,
        n2g,
        n2b,
        conv_out(wg2_sum),
        c2b,
        n3g,
        n3b,
        qkv_sum,
        qkv_bias_grad,
        encoder_weight_grad,
        encoder_bias_grad,
        proj_sum,
        pb,
    )


def solution(mesh):
    placed = (
        P(None, "ch", "rows"),
        P(),
        P(),
        P(),
        P(),
        P("ch"),
        P("ch"),
        P("ch", None, None, None),
        P("ch"),
        P(None, "ch", None),
        P(None, "ch"),
        P("ch"),
        P("ch"),
        P("ch", None, None, None),
        P("ch"),
        P("ch"),
        P("ch"),
        P(None, "ch", None),
        P(None, "ch"),
        P(None, "ch", None),
        P(None, "ch"),
        P("ch", None),
        P("ch"),
        P(None, "ch", "rows"),
    )
    return jax.shard_map(
        per_device,
        mesh=mesh,
        in_specs=placed,
        out_specs=(
            P(None, "ch", "rows"),
            P(None, "ch", "rows"),
            P("ch"),
            P("ch"),
            P("ch", None, None, None),
            P("ch"),
            P(None, "ch", None),
            P(None, "ch"),
            P("ch"),
            P("ch"),
            P("ch", None, None, None),
            P("ch"),
            P("ch"),
            P("ch"),
            P(None, "ch", None),
            P(None, "ch"),
            P(None, "ch", None),
            P(None, "ch"),
            P("ch", None),
            P("ch"),
        ),
        check_vma=False,
    )
```

```python
import functools
import math

import jax
import jax.numpy as jnp
from jax import lax
from jax.experimental import pallas as pl
from jax.experimental.pallas import tpu as pltpu
from jax.sharding import PartitionSpec as P

C = 512
HD = 64
GSZ = 16
EMB = 2048
W = 64
NCROP = 6
NC = 8
HP = 2 * W
TAPS = [(di, dj) for di in (-1, 0, 1) for dj in (-1, 0, 1)]

PRECISE = lax.Precision.HIGHEST
EPSILON = 1e-05
FAR = 2.0**100
SCORE = HD**-0.5
LOG2E = 1.4426950408889634
F32 = jnp.float32
BF = jnp.bfloat16


def spread(vals, lab):
    acc = vals[:, 0:1]
    for n in range(1, NCROP):
        acc = jnp.where(lab == n, vals[:, n : n + 1], acc)
    return acc


def crop_columns(first, second, lab):
    rows = first.shape[0]
    lane = lax.broadcasted_iota(jnp.int32, (rows, 128), 1)
    acc = jnp.zeros((rows, 128), F32)
    for n in range(NCROP):
        inside = lab == n
        one = jnp.sum(jnp.where(inside, first, 0.0), axis=1, keepdims=True)
        two = jnp.sum(jnp.where(inside, second, 0.0), axis=1, keepdims=True)
        acc = jnp.where(lane == n, one, acc)
        acc = jnp.where(lane == NC + n, two, acc)
    return acc


def put_column(acc, column, at):
    lane = lax.broadcasted_iota(jnp.int32, acc.shape, 1)
    return jnp.where(lane == at, column, acc)


def grouped(vals):
    rows, width = vals.shape
    parts = jnp.sum(vals.reshape(rows // GSZ, GSZ, width), axis=1, keepdims=True)
    return jnp.broadcast_to(parts, (rows // GSZ, GSZ, width)).reshape(rows, width)


def turned(block):
    rows, cols = block.shape
    if rows < 128:
        block = jnp.concatenate([block, jnp.zeros((128 - rows, cols), F32)], axis=0)
    return jnp.transpose(block)


def read_stats(recv_ref, which, cnt):
    members = recv_ref.shape[0]
    block = recv_ref[0, which]
    for g in range(1, members):
        other = recv_ref[g, which]
        block = jnp.concatenate([block[:16] + other[:16], block[16:]], axis=0)
    cols = turned(block)
    sums = grouped(cols[:, :16])
    mean = sums[:, :NC] / cnt
    inv = lax.rsqrt(sums[:, NC:16] / cnt - mean * mean + EPSILON)
    return mean, inv, cols[:, 16:17], cols[:, 17:18], cols[:, 18:19], cols[:, 19:20]


def read_sums(recv_ref, which):
    members = recv_ref.shape[0]
    block = recv_ref[0, which][:16]
    for g in range(1, members):
        block = block + recv_ref[g, which][:16]
    return turned(block)


def affine_of(stats):
    mean, inv, gain, bias, scale, offset = stats
    a = inv * gain * (1.0 + scale)
    b = (bias - mean * inv * gain) * (1.0 + scale) + offset
    return a, b


def sigmoid(v):
    return 0.5 * (1.0 + jnp.tanh(0.5 * v))


def slope(v):
    s = sigmoid(v)
    return s * (1.0 + v * (1.0 - s))


def masked_conv(w_ref, h_ref, y_ref, out_ref, mask_ref, bias):
    ch, width = out_ref.shape
    for g in range(3):
        w = w_ref[3 * g : 3 * g + 3].reshape(3 * ch, C)
        y_ref[g] = jnp.dot(w, h_ref[...], preferred_element_type=F32)
    size = min(ch, 64)

    def body(i, carry):
        i = pl.multiple_of(i * size, size)
        acc = None
        for g in range(3):
            for k in range(3):
                tap = 3 * g + k
                off = W * (g - 1) + k - 1
                y = y_ref[g, pl.ds(pl.multiple_of(k * ch + i, size), size), :]
                y = y if off == 0 else pltpu.roll(y, (-off) % width, 1)
                y = y * mask_ref[tap : tap + 1, :]
                acc = y if acc is None else acc + y
        if bias is not None:
            acc = acc + bias[pl.ds(i, size), 7:8]
        out_ref[pl.ds(i, size), :] = acc
        return carry

    lax.fori_loop(0, ch // size, body, 0)


def chunks(rows, body):
    size = min(128, rows)

    def step(i, carry):
        body(pl.multiple_of(i * size, size), size)
        return carry

    lax.fori_loop(0, rows // size, step, 0)


def send_rows(out_ref, st_ref, params):
    rows = jnp.transpose(st_ref[...])[:16]
    if params is not None:
        rows = jnp.concatenate([rows, params], axis=0)
    for k in range(out_ref.shape[0]):
        out_ref[k] = rows


def k_stats(x_ref, lab_ref, par_ref, out_ref, st_ref):
    n = x_ref.shape[1] - 2 * HP
    lab = lab_ref[:, HP : HP + n]

    def body(i, size):
        v = x_ref[pl.ds(i, size), HP : HP + n].astype(F32)
        st_ref[pl.ds(i, size), :] = crop_columns(v, v * v, lab)

    chunks(x_ref.shape[0], body)
    send_rows(out_ref, st_ref, par_ref[...])


def k_conv(nch, offs, resid, *refs):
    me_ref, recv_ref, cnt_ref, lab_ref, mask_ref, w_ref, par_ref = refs[:7]
    slots = refs[7 : 7 + nch]
    refs = refs[7 + nch :]
    if resid:
        x_ref, refs = refs[0], refs[1:]
        low_ref, pay_ref, h_ref, full_ref = refs[:4]
        refs = refs[4:]
    else:
        low_ref, pay_ref, h_ref = refs[:3]
        refs = refs[3:]
    y_ref, acc_ref, a_ref, b2_ref, st_ref = refs
    me = me_ref[0]
    ch, e = acc_ref.shape
    n = e - 2 * HP
    lab = lab_ref[...]
    for c in range(nch):
        a, b = affine_of(read_stats(recv_ref, c, cnt_ref[...]))
        a_ref[c * ch : (c + 1) * ch, :] = a
        b2_ref[c * ch : (c + 1) * ch, :] = b
    for s in range(nch):
        base = pl.multiple_of((me ^ offs[s]) * ch, ch)

        def body(i, size, s=s, base=base):
            row = pl.multiple_of(base + i, size)
            v = slots[s][pl.ds(i, size), :].astype(F32)
            pre = v * spread(a_ref[pl.ds(row, size), :], lab) + spread(b2_ref[pl.ds(row, size), :], lab)
            low = (pre * sigmoid(pre)).astype(BF)
            h_ref[pl.ds(row, size), :] = low

        chunks(ch, body)
    st_ref[...] = turned(par_ref[...])
    masked_conv(w_ref, h_ref, y_ref, acc_ref, mask_ref, st_ref)
    labc = lab[:, HP : HP + n]

    def finish(i, size):
        if resid:
            v = acc_ref[pl.ds(i, size), HP : HP + n] + x_ref[pl.ds(i, size), HP : HP + n].astype(F32)
            full_ref[pl.ds(i, size), :] = v
            low_ref[pl.ds(i, size), :] = v.astype(BF)
        else:
            low_ref[pl.ds(i, size), :] = acc_ref[pl.ds(i, size), :].astype(BF)
            v = acc_ref[pl.ds(i, size), HP : HP + n]
        st_ref[pl.ds(i, size), :] = crop_columns(v, v * v, labc)

    chunks(ch, finish)
    send_rows(pay_ref, st_ref, par_ref[...])


def k_qkv(nch, offs, *refs):
    me_ref, recv_ref, cnt_ref, lab_ref, w_ref, par_ref = refs[:6]
    slots = refs[6 : 6 + nch]
    res_ref, att_ref, q_ref, k_ref, v_ref, a_ref, b_ref = refs[6 + nch :]
    biases = turned(par_ref[...])
    me = me_ref[0]
    ch, n = q_ref.shape
    lab = lab_ref[:, HP : HP + n]
    for c in range(nch):
        a, b = affine_of(read_stats(recv_ref, c, cnt_ref[...]))
        a_ref[c * ch : (c + 1) * ch, :] = a
        b_ref[c * ch : (c + 1) * ch, :] = b
    for s in range(nch):
        base = pl.multiple_of((me ^ offs[s]) * ch, ch)

        def body(i, size, s=s, base=base):
            row = pl.multiple_of(base + i, size)
            low = slots[s][pl.ds(i, size), :]
            res_ref[pl.ds(row, size), :] = low
            out = low.astype(F32) * spread(a_ref[pl.ds(row, size), :], lab) + spread(
                b_ref[pl.ds(row, size), :], lab
            )
            att_ref[pl.ds(row, size), :] = out.astype(BF)

        chunks(ch, body)
    tile = 256

    def mul(i, _):
        at = pl.ds(pl.multiple_of(i * tile, tile), tile)
        x = att_ref[:, at]
        q_ref[:, at] = (jnp.dot(w_ref[0], x, preferred_element_type=F32) + biases[:, 0:1]).astype(BF)
        k_ref[:, at] = jnp.dot(w_ref[1], x, preferred_element_type=F32).astype(BF)
        v_ref[:, at] = (jnp.dot(w_ref[2], x, preferred_element_type=F32) + biases[:, 1:2]).astype(BF)
        return 0

    lax.fori_loop(0, n // tile, mul, 0)


def k_gout(nch, offs, *refs):
    me_ref, w_ref = refs[:2]
    slots = refs[2 : 2 + nch]
    g_ref, ga_ref = refs[2 + nch :]
    me = me_ref[0]
    ch, n = ga_ref.shape
    for s in range(nch):
        base = pl.multiple_of((me ^ offs[s]) * ch, ch)
        g_ref[pl.ds(base, ch), :] = slots[s][...]
    ga_ref[...] = jnp.dot(w_ref[...], g_ref[:, HP : HP + n], preferred_element_type=F32).astype(BF)


def k_turn(nch, offs, *refs):
    me_ref = refs[0]
    ins = refs[1 : 1 + nch]
    wqs = refs[1 + nch : 1 + 2 * nch]
    w1_ref, w2_ref, wq_ref, pw_ref, scr, scq = refs[1 + 2 * nch :]
    me = me_ref[0]
    ch = w1_ref.shape[1]
    for t in range(19):
        for s in range(nch):
            base = pl.multiple_of((me ^ offs[s]) * ch, ch)
            scr[pl.ds(base, ch), :] = ins[s][t].astype(F32)
        out = jnp.transpose(scr[...]).astype(BF)
        if t < 9:
            w1_ref[8 - t] = out
        elif t < 18:
            w2_ref[17 - t] = out
        else:
            pw_ref[...] = out
    for j in range(3):
        for s in range(nch):
            base = pl.multiple_of((me ^ offs[s]) * ch, ch)
            scq[pl.ds(base, ch), :] = wqs[s][j].astype(F32)
        wq_ref[j] = jnp.transpose(scq[...]).astype(BF)


def nt(a, b):
    return lax.dot_general(a, b, (((1,), (1,)), ((), ())), preferred_element_type=F32)


def tn(a, b):
    return lax.dot_general(a, b, (((0,), (0,)), ((), ())), preferred_element_type=F32)


def k_attend(kmap, vmap, nk, nv, korder, vorder, *refs):
    q_ref, ga_ref, oneq_ref, onek_ref, ck_ref, cv_ref = refs[:6]
    kparts = refs[6 : 6 + nk]
    vparts = refs[6 + nk : 6 + nk + nv]
    out_ref, dq_ref, dk0_ref, dk1_ref, dv0_ref, dv1_ref, dck_ref, dcv_ref = refs[
        6 + nk + nv : 14 + nk + nv
    ]
    ks_ref, vs_ref, e_ref, s_ref, ak_ref, av_ref = refs[14 + nk + nv :]
    ch, n = q_ref.shape
    heads = ch // HD
    slots = len(kmap)
    keys = slots * n
    tq = e_ref.shape[0]
    con = SCORE * LOG2E
    for h in range(heads):
        hs = slice(h * HD, (h + 1) * HD)
        for s in range(slots):
            i, j = kmap[s]
            ks_ref[h, 0:HD, s * n : (s + 1) * n] = kparts[i][j, hs, :]
            i, j = vmap[s]
            vs_ref[h, :, s * n : (s + 1) * n] = vparts[i][j, hs, :]
        ks_ref[h, HD : HD + 16, 0:keys] = onek_ref[...]
        ks_ref[h, 0:HD, keys:] = ck_ref[hs, :]
        ks_ref[h, HD : HD + 16, keys:] = jnp.zeros((16, 128), BF)
        vs_ref[h, :, keys:] = cv_ref[hs, :]
    once = n == tq
    if not once:
        ak_ref[...] = jnp.zeros_like(ak_ref)
        av_ref[...] = jnp.zeros_like(av_ref)
    spans = [(s * n, n) for s in range(slots)] + [(keys, 128)]

    for h in range(heads):
        hs = slice(h * HD, (h + 1) * HD)

        def block(b, _, h=h, hs=hs):
            at = pl.ds(pl.multiple_of(b * tq, tq), tq)
            qb = q_ref[hs, at]
            gb = ga_ref[hs, at]
            qa = jnp.transpose(
                jnp.concatenate([qb.astype(F32), oneq_ref[:, at].astype(F32)], axis=0)
            ).astype(BF)
            gt = jnp.transpose(gb.astype(F32))
            gtb = gt.astype(BF)
            top = jnp.full((tq, 128), -jnp.inf, F32)
            for k0, kn in spans:
                sc = jnp.dot(qa, ks_ref[h, :, k0 : k0 + kn], preferred_element_type=F32)
                s_ref[:, k0 : k0 + kn] = sc
                for u in range(kn // 128):
                    top = jnp.maximum(top, sc[:, u * 128 : (u + 1) * 128])
            top = jnp.max(top, axis=1, keepdims=True) * con
            tot = jnp.zeros((tq, 128), F32)
            acc = jnp.zeros((HD, tq), F32)
            for k0, kn in spans:
                ex = jnp.exp2(s_ref[:, k0 : k0 + kn] * con - top)
                for u in range(kn // 128):
                    tot = tot + ex[:, u * 128 : (u + 1) * 128]
                exb = ex.astype(BF)
                e_ref[:, k0 : k0 + kn] = exb
                acc = acc + nt(vs_ref[h, :, k0 : k0 + kn], exb)
            inv = 1.0 / jnp.sum(tot, axis=1, keepdims=True)
            acc = jnp.transpose(acc) * inv
            delta = jnp.sum(acc * gt, axis=1, keepdims=True)
            out_ref[hs, at] = jnp.transpose(acc).astype(BF)
            ql = jnp.transpose(qa[:, :HD].astype(F32) * (inv * SCORE)).astype(BF)
            gl = jnp.transpose(gt * inv).astype(BF)
            dq = jnp.zeros((HD, tq), F32)
            for k0, kn in spans:
                dp = jnp.dot(gtb, vs_ref[h, :, k0 : k0 + kn], preferred_element_type=F32)
                exb = e_ref[:, k0 : k0 + kn]
                ds = (exb.astype(F32) * (dp - delta)).astype(BF)
                dq = dq + nt(ks_ref[h, 0:HD, k0 : k0 + kn], ds)
                dk = jnp.dot(ql, ds, preferred_element_type=F32)
                dv = jnp.dot(gl, exb, preferred_element_type=F32)
                if not once:
                    dk = dk + ak_ref[hs, k0 : k0 + kn]
                    dv = dv + av_ref[hs, k0 : k0 + kn]
                ak_ref[hs, k0 : k0 + kn] = dk
                av_ref[hs, k0 : k0 + kn] = dv
            dq_ref[hs, at] = jnp.transpose(jnp.transpose(dq) * (inv * SCORE)).astype(BF)
            return 0

        lax.fori_loop(0, n // tq, block, 0)
    for order, acc_ref, outs in (
        (korder, ak_ref, (dk0_ref, dk1_ref)),
        (vorder, av_ref, (dv0_ref, dv1_ref)),
    ):
        for side in range(2):
            for i, s in enumerate(order[side]):
                outs[side][i] = acc_ref[:, s * n : (s + 1) * n].astype(BF)
    dck_ref[...] = ak_ref[:, keys:]
    dcv_ref[...] = av_ref[:, keys:]


def k_proj(nch, offs, *refs):
    me_ref, res_ref, par_ref, pw_ref = refs[:4]
    atts = refs[4 : 4 + nch]
    out_ref, att_s = refs[4 + nch :]
    me = me_ref[0]
    ch = res_ref.shape[0]
    for s in range(nch):
        base = pl.multiple_of((me ^ offs[s]) * ch, ch)
        att_s[pl.ds(base, ch), :] = atts[s][...]
    mixed = jnp.dot(pw_ref[...], att_s[...], preferred_element_type=F32)
    out_ref[...] = (res_ref[...] + mixed + turned(par_ref[...])[:, 2:3]).astype(BF)


def k_gattend(nch, offs, *refs):
    me_ref, recv_ref, cnt_ref, lab_ref, w_ref, res_ref = refs[:6]
    slots = [refs[6 + j * nch : 6 + (j + 1) * nch] for j in range(3)]
    ga_ref, pay_ref, d_s, acc_ref, st_ref = refs[6 + 3 * nch :]
    me = me_ref[0]
    n = ga_ref.shape[1]
    ch = C // nch
    lab = lab_ref[:, HP : HP + n]
    for j in range(3):
        for s in range(nch):
            base = pl.multiple_of((me ^ offs[s]) * ch, ch)
            d_s[j, pl.ds(base, ch), :] = slots[j][s][...]
    tile = 256

    def mul(i, _):
        at = pl.ds(pl.multiple_of(i * tile, tile), tile)
        acc = jnp.dot(w_ref[0], d_s[0, :, at], preferred_element_type=F32)
        acc = acc + jnp.dot(w_ref[1], d_s[1, :, at], preferred_element_type=F32)
        acc = acc + jnp.dot(w_ref[2], d_s[2, :, at], preferred_element_type=F32)
        acc_ref[:, at] = acc
        ga_ref[:, at] = acc.astype(BF)
        return 0

    lax.fori_loop(0, n // tile, mul, 0)
    mean, inv = read_stats(recv_ref, me, cnt_ref[...])[:2]
    own = pl.ds(pl.multiple_of(me * ch, ch), ch)
    ga = acc_ref[own, :]
    normed = (res_ref[own, :].astype(F32) - spread(mean, lab)) * spread(inv, lab)
    st_ref[...] = crop_columns(ga, ga * normed, lab)
    send_rows(pay_ref, st_ref, None)


def k_early(blocks, *refs):
    me_ref, dq_ref, in_ref, att_ref, g_ref, dck_ref, dcv_ref, out_ref, st_ref = refs
    ch, n = dq_ref.shape
    own = g_ref[pl.ds(pl.multiple_of(me_ref[0] * ch, ch), ch), HP : HP + n].astype(F32)
    acc = put_column(jnp.zeros((ch, 128), F32), jnp.sum(own, axis=1, keepdims=True), 1)
    dq = dq_ref[...]
    acc = put_column(acc, jnp.sum(dq.astype(F32), axis=1, keepdims=True), 0)
    both = jnp.concatenate([dck_ref[...], dcv_ref[...]], axis=1)
    ctx = jnp.concatenate([jnp.where(me_ref[2] == i, both, 0.0) for i in range(2)], axis=1)
    rows = ch // blocks
    for t, full in enumerate(
        (nt(dq, in_ref[...]), nt(att_ref[...], g_ref[:, HP : HP + n]), ctx)
    ):
        full = full.astype(BF)
        for i in range(blocks):
            out_ref[i, t] = full[i * rows : (i + 1) * rows]
    st_ref[...] = jnp.transpose(acc)[:8]


def norm_back(mean, inv, gain, t1, t2, cnt):
    m1 = grouped(gain * t1) / cnt
    m2 = grouped(gain * t2) / cnt
    return inv * gain, -inv * inv * m2, inv * (mean * inv * m2 - m1)


def k_back2(nch, split, *refs):
    (me_ref, recv3_ref, recvt_ref, recv2_ref, cnt_ref, lab_ref, mask_ref, w_ref) = refs[:8]
    ga_ref, res_ref, top_ref, bot_ref, g_ref, c1_ref, h2_ref = refs[8:15]
    more = refs[15:18]
    gp_ref, pay_ref, gr_ref = refs[18:21]
    outs, wst_ref = refs[21:-11], refs[-11]
    h_ref, y_ref, acc_ref, a_ref, b_ref, c_ref, st_ref, full_ref, w_scr, wy_ref = refs[-10:]
    me = me_ref[0]
    ch, e = acc_ref.shape
    n = e - 2 * HP
    lab = lab_ref[...]
    cnt = cnt_ref[...]
    for c in range(nch):
        sl = slice(c * ch, (c + 1) * ch)
        mean, inv, gain = read_stats(recv3_ref, c, cnt)[:3]
        t = read_sums(recvt_ref, c)
        a, b, cc = norm_back(mean, inv, gain, t[:, :NC], t[:, NC:16], cnt)
        a_ref[sl, :] = a
        b_ref[sl, :] = b
        c_ref[sl, :] = cc

    def body(i, size):
        row = pl.ds(i, size)
        low = pl.ds(pl.multiple_of(C + i, size), size)
        ga = jnp.concatenate([top_ref[row, :], ga_ref[row, :], bot_ref[row, :]], axis=1).astype(F32)
        v = jnp.concatenate([top_ref[low, :], res_ref[row, :], bot_ref[low, :]], axis=1).astype(F32)
        gr = (
            g_ref[row, :].astype(F32)
            + ga * spread(a_ref[row, :], lab)
            + v * spread(b_ref[row, :], lab)
            + spread(c_ref[row, :], lab)
        )
        full_ref[row, :] = gr
        h_ref[row, :] = gr.astype(BF)

    chunks(C, body)
    own = pl.multiple_of(me * ch, ch)
    gr_ref[...] = full_ref[pl.ds(own, ch), HP : HP + n]
    masked_conv(w_ref, h_ref, y_ref, acc_ref, mask_ref, None)
    stats = None
    mean, inv, gain, bias, scale, offset = read_stats(recv2_ref, me, cnt)
    a, b = affine_of((mean, inv, gain, bias, scale, offset))
    a_ref[0:ch, :] = a
    b_ref[0:ch, :] = b
    c_ref[0:ch, :] = inv
    a_ref[ch : 2 * ch, :] = -mean * inv

    def finish(i, size):
        row = pl.ds(i, size)
        v = c1_ref[row, :].astype(F32)
        pre = v * spread(a_ref[row, :], lab) + spread(b_ref[row, :], lab)
        gp = acc_ref[row, :] * slope(pre)
        gp_ref[row, :] = gp.astype(BF)
        labc = lab[:, HP : HP + n]
        normed = v[:, HP : HP + n] * spread(c_ref[row, :], labc) + spread(
            a_ref[pl.ds(pl.multiple_of(ch + i, size), size), :], labc
        )
        gpc = gp[:, HP : HP + n]
        acc = crop_columns(gpc, gpc * normed, labc)
        st_ref[row, :] = acc

    chunks(ch, finish)
    send_rows(pay_ref, st_ref, None)
    gc = gr_ref[...].astype(BF).astype(F32)
    wgrad_body(split, me_ref[1], gc, h2_ref, mask_ref, outs, wst_ref, w_scr, wy_ref, more)


def wgrad_body(split, pos, gc, h_ref, mask_ref, outs, st_ref, g_ref, y_ref, more=()):
    ch, n = gc.shape
    width = n + 2 * HP
    edge = jnp.zeros((ch, HP), F32)
    wide = jnp.concatenate([edge, gc, edge], axis=1)
    for t, (di, dj) in enumerate(TAPS):
        off = W * di + dj
        moved = wide * mask_ref[t : t + 1, :]
        moved = moved if off == 0 else pltpu.roll(moved, off % width, 1)
        g_ref[t * ch : (t + 1) * ch, :] = moved.astype(BF)
    rows = ch // 4

    def hand_out(k, t):
        if not split:
            outs[0][t] = y_ref[k * ch : (k + 1) * ch, :].astype(BF)
            return
        for o in range(4):
            at = pl.multiple_of(k * ch + (pos ^ o) * rows, rows)
            outs[o][t] = y_ref[pl.ds(at, rows), :].astype(BF)

    for g in range(3):
        y_ref[...] = nt(g_ref[3 * g * ch : 3 * (g + 1) * ch, :], h_ref[...])
        for k in range(3):
            hand_out(k, 3 * g + k)
    acc = jnp.zeros((ch, 128), F32)
    acc = put_column(acc, jnp.sum(gc, axis=1, keepdims=True), 0)
    if more:
        for k in range(2):
            y_ref[k * ch : (k + 1) * ch, :] = nt(more[k][...], more[2][...])
            hand_out(k, 9 + k)
        column = jnp.sum(more[1][...].astype(F32), axis=1, keepdims=True)
        acc = put_column(acc, column, 1)
    st_ref[...] = jnp.transpose(acc)[:8]


def k_place(me_ref, *refs):
    parts, out_ref = refs[:-1], refs[-1]
    rows = parts[0].shape[1]
    for o, part in enumerate(parts):
        at = pl.ds(pl.multiple_of((me_ref[1] ^ o) * rows, rows), rows)
        out_ref[:, at, :] = part[...].astype(F32)


def k_place2(me_ref, early_ref, *refs):
    parts, (out_ref, qkv_ref, proj_ref) = refs[:-3], refs[-3:]
    rows = parts[0].shape[1]
    for o, part in enumerate(parts):
        at = pl.ds(pl.multiple_of((me_ref[1] ^ o) * rows, rows), rows)
        out_ref[:, at, :] = part[:9].astype(F32)
        qkv_ref[1:3, at, :] = part[9:].astype(F32)
    low = early_ref.shape[2]
    for i in range(early_ref.shape[0]):
        qkv_ref[0, i * low : (i + 1) * low, :] = early_ref[i, 0].astype(F32)
        proj_ref[i * low : (i + 1) * low, :] = early_ref[i, 1].astype(F32)


def conv1_back(recv2_ref, recvu_ref, which, cnt):
    mean, inv, gain, _, scale, _ = read_stats(recv2_ref, which, cnt)
    u = read_sums(recvu_ref, which)
    return norm_back(mean, inv, gain * (1.0 + scale), u[:, :NC], u[:, NC:16], cnt)


def k_wgrad1(split, *refs):
    me_ref, recv2_ref, recvu_ref, cnt_ref, lab_ref, mask_ref, gp_ref, c1_ref, h_ref = refs[:9]
    outs, (st_ref, g_ref, y_ref) = refs[9:-3], refs[-3:]
    n = gp_ref.shape[1] - 2 * HP
    lab = lab_ref[:, HP : HP + n]
    a, b, c = conv1_back(recv2_ref, recvu_ref, me_ref[0], cnt_ref[...])
    gc = (
        gp_ref[:, HP : HP + n].astype(F32) * spread(a, lab)
        + c1_ref[:, HP : HP + n].astype(F32) * spread(b, lab)
        + spread(c, lab)
    ).astype(BF).astype(F32)
    wgrad_body(split, me_ref[1], gc, h_ref, mask_ref, outs, st_ref, g_ref, y_ref)


def k_back1(nch, offs, *refs):
    me_ref, recv1_ref, recv2_ref, recvu_ref, cnt_ref, lab_ref, mask_ref, w_ref, x_ref = refs[:9]
    wg1_ref, wg2_ref, early_ref, payu_ref, payt_ref = refs[9:14]
    gps = refs[14 : 14 + nch]
    c1s = refs[14 + nch : 14 + 2 * nch]
    gp1_ref, pay_ref = refs[14 + 2 * nch : 16 + 2 * nch]
    h_ref, y_ref, acc_ref, a_ref, b_ref, c_ref, st_ref = refs[16 + 2 * nch :]
    me = me_ref[0]
    ch, e = acc_ref.shape
    n = e - 2 * HP
    lab = lab_ref[...]
    cnt = cnt_ref[...]
    for c in range(nch):
        sl = slice(c * ch, (c + 1) * ch)
        a, b, cc = conv1_back(recv2_ref, recvu_ref, c, cnt)
        a_ref[sl, :] = a
        b_ref[sl, :] = b
        c_ref[sl, :] = cc
    for s in range(nch):
        base = pl.multiple_of((me ^ offs[s]) * ch, ch)

        def body(i, size, s=s, base=base):
            row = pl.multiple_of(base + i, size)
            at = pl.ds(row, size)
            gc = (
                gps[s][pl.ds(i, size), :].astype(F32) * spread(a_ref[at, :], lab)
                + c1s[s][pl.ds(i, size), :].astype(F32) * spread(b_ref[at, :], lab)
                + spread(c_ref[at, :], lab)
            )
            h_ref[at, :] = gc.astype(BF)

        chunks(ch, body)
    masked_conv(w_ref, h_ref, y_ref, acc_ref, mask_ref, None)
    stats = read_stats(recv1_ref, me, cnt)
    a, b = affine_of(stats)
    a_ref[0:ch, :] = a
    b_ref[0:ch, :] = b
    c_ref[0:ch, :] = stats[1]
    c_ref[ch : 2 * ch, :] = -stats[0] * stats[1]
    labc = lab[:, HP : HP + n]

    def finish(i, size):
        row = pl.ds(i, size)
        v = x_ref[row, HP : HP + n].astype(F32)
        pre = v * spread(a_ref[row, :], labc) + spread(b_ref[row, :], labc)
        gp = acc_ref[row, HP : HP + n] * slope(pre)
        gp1_ref[row, :] = gp
        normed = v * spread(c_ref[row, :], labc) + spread(
            c_ref[pl.ds(pl.multiple_of(ch + i, size), size), :], labc
        )
        st_ref[row, :] = crop_columns(gp, gp * normed, labc)

    chunks(ch, finish)
    u, t = payu_ref[0], payt_ref[0]
    smalls = jnp.zeros((16, ch), F32)
    at = lax.broadcasted_iota(jnp.int32, (16, ch), 0)
    for i, line in enumerate(
        (
            wg1_ref[0:1],
            wg2_ref[0:1],
            jnp.sum(u[:NC], axis=0, keepdims=True),
            jnp.sum(u[NC:], axis=0, keepdims=True),
            early_ref[1:2],
            early_ref[0:1],
            wg2_ref[1:2],
            jnp.sum(t[:NC], axis=0, keepdims=True),
            jnp.sum(t[NC:], axis=0, keepdims=True),
        )
    ):
        smalls = jnp.where(at == i, line, smalls)
    send_rows(pay_ref, st_ref, smalls)


def k_last(*refs):
    me_ref, recv1_ref, recvv_ref, cnt_ref, lab_ref, gp_ref, x_ref, gr_ref, par_ref = refs[:9]
    o_ref, one_ref, two_ref, mod_ref, emb_ref, qb_ref = refs[9:15]
    (n1g, n1b, c1b, n2g, n2b, c2b, n3g, n3b, pb) = refs[15:24]
    sum_ref, out_ref = refs[24:]
    ch, n = gp_ref.shape
    half = recvv_ref.shape[0] // 2
    lab = lab_ref[:, HP : HP + n]
    for m in range(2):
        tot = recvv_ref[m * half]
        for g in range(1, half):
            tot = tot + recvv_ref[m * half + g]
        sum_ref[m] = tot
    cnt = cnt_ref[...]
    mean, inv, gain = read_stats(recv1_ref, me_ref[0], cnt)[:3]
    v = turned(sum_ref[me_ref[1]][:16])
    a, b, c = norm_back(mean, inv, gain, v[:, :NC], v[:, NC:16], cnt)
    out = (
        gr_ref[...]
        + gp_ref[...] * spread(a, lab)
        + x_ref[:, HP : HP + n].astype(F32) * spread(b, lab)
        + spread(c, lab)
    )
    out_ref[0:ch, :] = o_ref[...].astype(F32)
    out_ref[ch:, :] = out
    mid = n // 2
    sides = out_ref[:, :mid], out_ref[:, mid:]
    one_ref[...] = jnp.where(me_ref[1] == 0, sides[0], sides[1]).astype(BF)
    two_ref[...] = jnp.where(me_ref[1] == 0, sides[1], sides[0]).astype(BF)
    both = sum_ref[0] + sum_ref[1]
    n1b[...] = jnp.sum(both[:NC], axis=0, keepdims=True)
    n1g[...] = jnp.sum(both[NC:16], axis=0, keepdims=True)
    for ref, at in ((c1b, 16), (c2b, 17), (pb, 20), (n3b, 23), (n3g, 24)):
        ref[...] = both[at : at + 1]
    qb_ref[...] = both[21:23]
    u1 = [sum_ref[m, 18:19] for m in range(2)]
    u2 = [sum_ref[m, 19:20] for m in range(2)]
    up = [1.0 + par_ref[2 + m : 3 + m] for m in range(2)]
    n2b[...] = up[0] * u1[0] + up[1] * u1[1]
    n2g[...] = up[0] * u2[0] + up[1] * u2[1]
    scales = [par_ref[0:1] * u2[m] + par_ref[1:2] * u1[m] for m in range(2)]
    mod_ref[...] = jnp.concatenate([scales[0], u1[0], scales[1], u1[1]], axis=0)
    emb_ref[...] = jnp.concatenate([scales[0] + scales[1], u1[0] + u1[1]], axis=0)


COST = {"k_stats": 2, "k_conv": 10, "k_qkv": 6, "k_gout": 3, "k_attend": 34, "k_turn": 5, "k_proj": 3, "k_gattend": 7, "k_early": 4, "k_back2": 17, "k_wgrad1": 5, "k_back1": 13, "k_last": 3, "k_place": 3, "k_place2": 3}
SM = pl.BlockSpec(memory_space=pltpu.SMEM)
VM = pl.BlockSpec(memory_space=pltpu.VMEM)


def call(kernel, args, outs, scratch=(), smem=1, flops=0, limit=53):
    name = getattr(kernel, "func", kernel).__name__
    flops = int(COST[name] * 1.8e9)
    bytes_all = sum(math.prod(a.shape) * a.dtype.itemsize for a in list(args) + list(outs))
    return pl.pallas_call(
        kernel,
        out_shape=tuple(outs),
        in_specs=[SM] * smem + [VM] * (len(args) - smem),
        out_specs=tuple(VM for _ in outs),
        scratch_shapes=list(scratch),
        compiler_params=pltpu.CompilerParams(vmem_limit_bytes=limit * 2**20),
        cost_estimate=pl.CostEstimate(flops=flops, bytes_accessed=bytes_all, transcendentals=0),
    )(*args)


def fence(*xs):
    return lax.optimization_barrier(xs)


def sd(shape, dtype):
    return jax.ShapeDtypeStruct(shape, dtype)


def swap(x, axis, bit):
    count = lax.axis_size(axis)
    return lax.ppermute(x, axis, [(i, i ^ bit) for i in range(count)])


def bits_of(count):
    return [1 << i for i in range(count.bit_length() - 1)]


def offsets(count):
    offs = [0]
    for bit in reversed(bits_of(count)):
        offs = offs + [o ^ bit for o in offs]
    return offs


def gather_ch(x):
    slots = [x]
    for bit in reversed(bits_of(lax.axis_size("ch"))):
        slots = slots + [swap(s, "ch", bit) for s in slots]
    return slots


def first_hops(x):
    return [x] + [swap(x, "ch", bit) for bit in reversed(bits_of(lax.axis_size("ch")))]


def last_hops(hops):
    bits = list(reversed(bits_of(lax.axis_size("ch"))))
    slots = [hops[0]]
    for at, bit in enumerate(bits):
        slots = slots + [hops[at + 1]] + [swap(s, "ch", bit) for s in slots[1:]]
    return slots


def gather_rows(x, bits):
    parts, places, offs = [x[None]], [(0, 0)], [0]
    for bit in bits:
        whole = parts[0] if len(parts) == 1 else jnp.concatenate(parts, axis=0)
        base = len(parts)
        parts = parts + [swap(whole, "rows", bit)]
        places = places + [(base, i) for i in range(len(offs))]
        offs = offs + [o ^ bit for o in offs]
    table = dict(zip(offs, places, strict=True))
    return parts, [table[o] for o in range(len(offs))]


def order_of(bits):
    keep = [0]
    for bit in reversed(bits[1:]):
        keep = keep + [o ^ bit for o in keep]
    return keep, [o ^ bits[0] for o in keep]


def add_low(a, b):
    return (a.astype(F32) + b.astype(F32)).astype(BF)


def scatter_rows(keep, got, bits):
    for bit in bits[1:]:
        mid = keep.shape[0] // 2
        give = add_low(keep[mid:], got[mid:])
        keep = add_low(keep[:mid], got[:mid])
        got = swap(give, "rows", bit)
    return add_low(keep[0], got[0])


class Chain:
    def __init__(self, parts, top):
        self.top, self.at, self.keep = top, 0, parts[0]
        self.flight = [swap(p, "rows", o) for o, p in enumerate(parts) if o]

    def advance(self):
        self.at += 1
        got = self.flight
        if self.at == 1:
            total = self.keep.astype(F32)
            for x in got:
                total = total + x.astype(F32)
            self.keep = total.astype(BF)
            self.flight = [swap(self.keep, "rows", self.top)]
        elif self.at == 2:
            self.keep = add_low(self.keep, got[0])
            self.flight = [swap(self.keep, "rows", o) for o in (1, 2, 3)]
        else:
            self.done = [self.keep, *got]


def meet(chains, *xs):
    flights, xs = lax.optimization_barrier(([c.flight for c in chains], xs))
    for c, flight in zip(chains, flights, strict=True):
        c.flight = flight
        c.advance()
    return xs


def per_device(
    features,
    crop_ids,
    timesteps,
    clip_embed,
    context,
    norm1_gain,
    norm1_bias,
    conv1_weight,
    conv1_bias,
    embed_weight,
    embed_bias,
    norm2_gain,
    norm2_bias,
    conv2_weight,
    conv2_bias,
    norm3_gain,
    norm3_bias,
    qkv_weight,
    qkv_bias,
    encoder_weight,
    encoder_bias,
    proj_weight,
    proj_bias,
    out_grad,
):
    batches, ch, pixels = features.shape
    rows_n = lax.axis_size("rows")
    nch = lax.axis_size("ch")
    half = rows_n // 2
    r = lax.axis_index("rows")
    me = lax.axis_index("ch")
    m, j = r // half, r % half
    even = r % 2 == 0
    n = 2 * pixels
    e = n + 2 * HP
    local_rows = n // W
    copies = half * nch
    offs = offsets(nch)
    flat = rows_n * nch
    teams = [list(range(copies)), list(range(copies, flat))]
    me1 = jnp.reshape(me, (1,)).astype(jnp.int32)
    me4 = jnp.stack([me, r % 4, m]).astype(jnp.int32)
    st8 = sd((8, ch), F32)

    evens, odds = range(0, rows_n, 2), range(1, rows_n, 2)
    first_perm = [(i, i // 2) for i in evens] + [(i, half + i // 2) for i in odds]
    second_perm = [(i, half + i // 2) for i in evens] + [(i, i // 2) for i in odds]

    def halo_perm(up, down):
        pairs = [(i, up * half + i // 2 - 1) for i in evens if i // 2 > 0]
        return pairs + [(i, down * half + i // 2 + 1) for i in odds if i // 2 < half - 1]

    def reshard(*xs):
        def side(when, cut):
            return jnp.concatenate([jnp.where(when, cut(x[0]), cut(x[1])) for x in xs], axis=0)

        def edge(x):
            return jnp.where(even, x[:, :HP], x[:, pixels - HP :])

        def all_of(x):
            return x

        one = lax.ppermute(side(even, all_of), "rows", first_perm)
        two = lax.ppermute(side(~even, all_of), "rows", second_perm)
        three = lax.ppermute(side(even, edge), "rows", halo_perm(0, 1))
        four = lax.ppermute(side(~even, edge), "rows", halo_perm(1, 0))
        return one, two, three, four

    def resharded(one, two, three, four):
        low = jnp.where(m == 0, one, two)
        high = jnp.where(m == 0, two, one)
        below = jnp.where(m == 0, three, four)
        above = jnp.where(m == 0, four, three)
        return jnp.concatenate([above, low, high, below], axis=1)

    def to_next(x):
        return lax.ppermute(
            x, "rows", [(i, i + 1) for i in range(rows_n - 1) if i % half != half - 1]
        )

    def to_prev(x):
        return lax.ppermute(x, "rows", [(i, i - 1) for i in range(1, rows_n) if i % half != 0])

    def team_exchange(x):
        got = lax.all_to_all(x, ("rows", "ch"), 0, 0, axis_index_groups=teams)
        return got.reshape((half, nch) + x.shape[1:])

    ids = lax.dynamic_index_in_dim(crop_ids, m, 0, keepdims=False)
    grid = jnp.pad(ids.reshape(-1, W), ((2, 2), (0, 0)), constant_values=-1)
    lab20 = lax.dynamic_slice_in_dim(grid, j * local_rows, local_rows + 4, 0)
    near = jnp.pad(lab20, 1, constant_values=-2)
    height = local_rows + 4
    masks = jnp.stack(
        [
            (near[1 + di : 1 + di + height, 1 + dj : 1 + dj + W] == lab20) & (lab20 >= 0)
            for di, dj in TAPS
        ]
    ).astype(F32)
    masks = jnp.pad(masks.reshape(9, e), ((0, 7), (0, 0)))
    lab = lab20.reshape(1, e)
    crops = jnp.arange(NC, dtype=jnp.int32)
    counted = jnp.sum((ids[None, :] == crops[:, None]).astype(F32), axis=1)
    cnt = jnp.maximum(counted, 1.0)[None, :] * GSZ

    w1 = conv1_weight.transpose(1, 2, 0, 3).reshape(9, ch, C)
    w2 = conv2_weight.transpose(1, 2, 0, 3).reshape(9, ch, C)

    parts = reshard(features, out_grad)
    x_own = resharded(*[x[:ch] for x in parts])
    g_own = resharded(*[x[ch:] for x in parts])
    x_own, clip_embed = fence(x_own, clip_embed)

    half_width = EMB // 2
    frequency = jnp.exp(-math.log(10000.0) * jnp.arange(half_width, dtype=F32) / half_width)
    angles = timesteps.astype(F32)[:, None] * frequency[None, :]
    embedded = jax.nn.silu(
        jnp.concatenate([jnp.cos(angles), jnp.sin(angles)], axis=1) + clip_embed
    )
    modulation = (
        jnp.einsum("be,jce->bjc", embedded, embed_weight.astype(F32), precision=PRECISE)
        + embed_bias
    )
    mod_here = lax.dynamic_index_in_dim(modulation, m, 0, keepdims=False)
    zero = jnp.zeros((1, ch), F32)

    def params(*rows):
        given = [x.reshape(1, ch).astype(F32) for x in rows]
        return jnp.concatenate(given + [zero] * (8 - len(given)), axis=0)

    par1 = params(norm1_gain, norm1_bias)
    blank = jnp.zeros((ch,), F32)
    par2 = params(norm2_gain, norm2_bias, mod_here[0], mod_here[1], blank, blank, blank, conv1_bias)
    par3 = params(norm3_gain, norm3_bias, blank, blank, blank, blank, blank, conv2_bias)
    par4 = params(qkv_bias[0], qkv_bias[1], proj_bias)

    x_slots = gather_ch(x_own)
    pay = sd((copies, 24, ch), F32)
    st = pltpu.VMEM((ch, 128), F32)
    (pay1,) = call(k_stats, (x_own, lab, par1), (pay,), [st], smem=0)
    recv1 = team_exchange(pay1)
    x_slots, recv1, g_own = fence(x_slots, recv1, g_own)
    g_slots = first_hops(g_own)
    conv_scratch = [
        pltpu.VMEM((3, 3 * ch, e), F32),
        pltpu.VMEM((ch, e), F32),
        pltpu.VMEM((C, NC), F32),
        pltpu.VMEM((C, NC), F32),
    ]
    conv_flops = 2 * 9 * ch * C * e

    low1, pay2, h1 = call(
        functools.partial(k_conv, nch, offs, False),
        (me1, recv1, cnt, lab, masks, w1, par2, *x_slots),
        (sd((ch, e), BF), pay, sd((C, e), BF)),
        conv_scratch + [st],
        flops=conv_flops,
    )
    low1, pay2, g_slots, w1, w2_cut, proj_weight_cut = fence(low1, pay2, g_slots, w1, w2, proj_weight)


    def packed(o):
        at = (me ^ o) * ch
        return jnp.concatenate(
            [
                lax.dynamic_slice_in_dim(w1, at, ch, 2),
                lax.dynamic_slice_in_dim(w2_cut, at, ch, 2),
                lax.dynamic_slice_in_dim(proj_weight_cut, at, ch, 1)[None],
            ],
            axis=0,
        )

    packs = [packed(o) for o in offs]
    c1_slots = gather_ch(low1)
    recv2 = team_exchange(pay2)
    c1_slots, recv2, g_slots, qkv_weight = fence(c1_slots, recv2, g_slots, qkv_weight)
    g_slots, wq_slots = last_hops(g_slots), first_hops(qkv_weight)
    low2, pay3, h2, resid = call(
        functools.partial(k_conv, nch, offs, True),
        (me1, recv2, cnt, lab, masks, w2, par3, *c1_slots, x_own),
        (sd((ch, n), BF), pay, sd((C, e), BF), sd((ch, n), F32)),
        conv_scratch + [st],
        flops=conv_flops,
    )
    low2, pay3, g_slots, wq_slots = fence(low2, pay3, g_slots, wq_slots)
    r_slots = gather_ch(low2)
    recv3 = team_exchange(pay3)
    r_slots, recv3, packs, wq_slots = fence(r_slots, recv3, packs, wq_slots)
    wq_slots = last_hops(wq_slots)
    packs = [w if o == 0 else swap(w, "ch", o) for o, w in zip(offs, packs, strict=True)]
    res_full, att_in, q, k, v = call(
        functools.partial(k_qkv, nch, offs),
        (me1, recv3, cnt, lab, qkv_weight, par4, *r_slots),
        (sd((C, n), BF), sd((C, n), BF), sd((ch, n), BF), sd((ch, n), BF), sd((ch, n), BF)),
        [pltpu.VMEM((C, NC), F32), pltpu.VMEM((C, NC), F32)],
        flops=2 * 3 * ch * C * n,
    )
    q, k, v, wq_slots = fence(q, k, v, wq_slots)
    row_bits = bits_of(half)
    k_parts, k_map = gather_rows(k, row_bits)
    v_parts, v_map = gather_rows(v, list(reversed(row_bits)))
    k_back, v_back = list(reversed(row_bits)), row_bits

    g_full, grad_att = call(
        functools.partial(k_gout, nch, offs),
        (me1, proj_weight, *g_slots),
        (sd((C, e), BF), sd((ch, n), BF)),
        flops=2 * ch * C * n,
    )
    ctx = lax.dynamic_index_in_dim(context, m, 0, keepdims=False)
    encoded = (
        jnp.einsum("te,jde->jdt", ctx, encoder_weight, preferred_element_type=F32)
        + encoder_bias[:, :, None]
    ).astype(BF)

    tiles = ids.reshape(half, n)
    key_ids = jnp.concatenate(
        [lax.dynamic_slice_in_dim(tiles, j ^ o, 1, 0) for o in range(half)], axis=1
    )
    crops16 = jnp.arange(16, dtype=jnp.int32)[:, None]
    one_k = jnp.where((key_ids == crops16) | (crops16 >= NC), 0.0, -FAR).astype(BF)
    one_q = (lab[:, HP : HP + n] == crops16).astype(BF)
    heads = ch // HD
    keys = half * n + 128
    tq = n if half * n <= 4096 else 256
    k_parts, v_parts, grad_att, encoded = fence(k_parts, v_parts, grad_att, encoded)
    attended, dq, dk0, dk1, dv0, dv1, dck, dcv = call(
        functools.partial(
            k_attend, k_map, v_map, len(k_parts), len(v_parts), order_of(k_back), order_of(v_back)
        ),
        (q, grad_att, one_q, one_k, encoded[0], encoded[1], *k_parts, *v_parts),
        (
            sd((ch, n), BF),
            sd((ch, n), BF),
            sd((half // 2, ch, n), BF),
            sd((half // 2, ch, n), BF),
            sd((half // 2, ch, n), BF),
            sd((half // 2, ch, n), BF),
            sd((ch, 128), F32),
            sd((ch, 128), F32),
        ),
        [
            pltpu.VMEM((heads, HD + 16, keys), BF),
            pltpu.VMEM((heads, HD, keys), BF),
            pltpu.VMEM((tq, keys), BF),
            pltpu.VMEM((tq, keys), F32),
            pltpu.VMEM((ch, keys), F32),
            pltpu.VMEM((ch, keys), F32),
        ],
        smem=0,
        flops=6 * 2 * heads * n * keys * HD,
        limit=60,
    )
    dk0, dk1, dv0, dv1, dq, attended, packs = fence(dk0, dk1, dv0, dv1, dq, attended, packs)
    got_k, got_v = swap(dk1, "rows", k_back[0]), swap(dv1, "rows", v_back[0])
    dq_slots = first_hops(dq)
    w1t, w2t, wqt, pwt = call(
        functools.partial(k_turn, nch, offs),
        (me1, *packs, *wq_slots),
        (sd((9, ch, C), BF), sd((9, ch, C), BF), sd((3, C, C), BF), sd((ch, C), BF)),
        [pltpu.VMEM((C, ch), F32), pltpu.VMEM((C, C), F32)],
    )
    split = rows_n == 8 and ch % 128 == 0
    blocks = rows_n if split else 1
    early, early_st = call(
        functools.partial(k_early, blocks),
        (me4, dq, att_in, attended, g_full, dck, dcv),
        (sd((blocks, 3, ch // blocks, C), BF), st8),
    )
    got_k, got_v, w1t, w2t, wqt, pwt, dq_slots, attended, early, early_st = fence(
        got_k, got_v, w1t, w2t, wqt, pwt, dq_slots, attended, early, early_st
    )
    dk = scatter_rows(dk0, got_k, k_back)
    dv = scatter_rows(dv0, got_v, v_back)
    dq_slots, a_slots = last_hops(dq_slots), first_hops(attended)
    dk, dv, dq_slots, a_slots, early = fence(dk, dv, dq_slots, a_slots, early)
    early = lax.all_to_all(early, "rows", 0, 0) if split else lax.psum(early, "rows")
    a_slots = last_hops(a_slots)
    dk_slots = gather_ch(dk)
    dv_slots = gather_ch(dv)
    (out_own,) = call(
        functools.partial(k_proj, nch, offs),
        (me1, resid, par4, pwt, *a_slots),
        (sd((ch, n), BF),),
        [pltpu.VMEM((C, n), BF)],
        flops=2 * ch * C * n,
    )
    dk_slots, dv_slots, out_own = fence(dk_slots, dv_slots, out_own)
    ga, pay_t = call(
        functools.partial(k_gattend, nch, offs),
        (me1, recv3, cnt, lab, wqt, res_full, *dq_slots, *dk_slots, *dv_slots),
        (sd((C, n), BF), sd((copies, 16, ch), F32)),
        [
            pltpu.VMEM((3, C, n), BF),
            pltpu.VMEM((C, n), F32),
            st,
        ],
        flops=2 * 3 * C * C * n,
    )
    if split:
        ga, pay_t, early = fence(ga, pay_t, early)
        early = jnp.sum(early.astype(F32), axis=0).astype(BF)
        early = lax.all_to_all(jnp.broadcast_to(early[None], (blocks, *early.shape)), "rows", 0, 0)
    recv_t = team_exchange(pay_t)
    top = to_next(jnp.concatenate([ga[:, n - HP :], res_full[:, n - HP :]], axis=0))
    bottom = to_prev(jnp.concatenate([ga[:, :HP], res_full[:, :HP]], axis=0))
    def pieces(units):
        return [sd((units, ch // 4, C), BF)] * 4 if split else [sd((units, ch, C), BF)]

    def begin(parts):
        return Chain(parts, 4) if split else lax.psum(parts[0], "rows")

    def moving(*chains):
        return list(chains) if split else []

    recv_t, top, bottom = fence(recv_t, top, bottom)
    wg_scratch = [pltpu.VMEM((9 * ch, e), BF), pltpu.VMEM((3 * ch, C), F32)]
    gp2, pay_u, grad_resid, *wg2, wg2_st = call(
        functools.partial(k_back2, nch, split),
        (
            me4, recv3, recv_t, recv2, cnt, lab, masks, w2t,
            ga, res_full, top, bottom, g_full, low1, h2, dk, dv, att_in,
        ),
        (sd((ch, e), BF), sd((copies, 16, ch), F32), sd((ch, n), F32), *pieces(11), st8),
        [
            pltpu.VMEM((C, e), BF),
            pltpu.VMEM((3, 3 * ch, e), F32),
            pltpu.VMEM((ch, e), F32),
            pltpu.VMEM((C, NC), F32),
            pltpu.VMEM((C, NC), F32),
            pltpu.VMEM((C, NC), F32),
            st,
            pltpu.VMEM((C, e), F32),
            *wg_scratch,
        ],
        flops=conv_flops,
    )
    gp2, pay_u, early_sum = fence(gp2, pay_u, early)
    gp_slots = first_hops(gp2)
    recv_u = team_exchange(pay_u)
    gp_slots = last_hops(gp_slots)
    wg2 = begin(wg2)
    *wg1, wg1_st = call(
        functools.partial(k_wgrad1, split),
        (me4, recv2, recv_u, cnt, lab, masks, gp2, low1, h1),
        (*pieces(9), st8),
        wg_scratch,
        flops=conv_flops,
    )
    wg1, gp_slots = meet(moving(wg2), wg1, gp_slots)
    wg1 = begin(wg1)
    gp1, pay_v = call(
        functools.partial(k_back1, nch, offs),
        (
            me1, recv1, recv2, recv_u, cnt, lab, masks, w1t, x_own,
            wg1_st, wg2_st, early_st, pay_u, pay_t, *gp_slots, *c1_slots,
        ),
        (sd((ch, n), F32), sd((rows_n, 32, ch), F32)),
        [
            pltpu.VMEM((C, e), BF),
            pltpu.VMEM((3, 3 * ch, e), F32),
            pltpu.VMEM((ch, e), F32),
            pltpu.VMEM((C, NC), F32),
            pltpu.VMEM((C, NC), F32),
            pltpu.VMEM((C, NC), F32),
            st,
        ],
        flops=conv_flops,
    )
    (gp1,) = meet(moving(wg2, wg1), gp1)
    recv_v = lax.all_to_all(pay_v, "rows", 0, 0)
    line = sd((1, ch), F32)
    one, two, mod_grad, embed_bias_grad, qkv_bias_grad, *lines = call(
        k_last,
        (
            jnp.stack([me, m]).astype(jnp.int32),
            recv1, recv_v, cnt, lab, gp1, x_own, grad_resid,
            params(norm2_gain, norm2_bias, modulation[0, 0], modulation[1, 0]), out_own,
        ),
        (*[sd((2 * ch, pixels), BF)] * 2, sd((4, ch), F32), sd((2, ch), F32), sd((2, ch), F32), *[line] * 9),
        [pltpu.VMEM((2, 32, ch), F32), pltpu.VMEM((2 * ch, n), F32)],
    )
    one, two = meet(moving(wg2, wg1), one, two)
    one = lax.ppermute(one, "rows", [(b, a) for a, b in first_perm])
    two = lax.ppermute(two, "rows", [(b, a) for a, b in second_perm])
    output, features_grad = [
        jnp.stack([jnp.where(even, x, y), jnp.where(even, y, x)])
        for x, y in ((one[:ch], two[:ch]), (one[ch:], two[ch:]))
    ]
    placed = (sd((9, ch, C), F32), sd((3, ch, C), F32), sd((ch, C), F32))
    if split:
        wg2_sum, qkv_sum, proj_sum = call(k_place2, (me4, early_sum, *wg2.done), placed)
        meet([wg1])
        (wg1_sum,) = call(k_place, (me4, *wg1.done), placed[:1])
    else:
        wg2_sum, wg1_sum = wg2[:9].astype(F32), wg1.astype(F32)
        qkv_sum = jnp.concatenate([early_sum[0, :1], wg2[9:]], axis=0).astype(F32)
        proj_sum = early_sum[0, 1].astype(F32)

    n1g, n1b, c1b, n2g, n2b, c2b, n3g, n3b, pb = [x.reshape(ch) for x in lines]
    mod_grad = mod_grad.reshape(2, 2, ch)
    embed_weight_grad = (
        mod_grad[0][:, :, None] * embedded[0][None, None, :]
        + mod_grad[1][:, :, None] * embedded[1][None, None, :]
    )
    encoder_grad = early_sum[:, 2].reshape(ch, batches, 2, -1)
    encoder_weight_grad = jnp.einsum(
        "dbjt,bte->jde", encoder_grad, context, preferred_element_type=F32
    )
    encoder_bias_grad = jnp.sum(encoder_grad.astype(F32), axis=(1, 3)).T

    def conv_out(x):
        return x.reshape(3, 3, ch, C).transpose(2, 0, 1, 3)

    return (
        output,
        features_grad,
        n1g,
        n1b,
        conv_out(wg1_sum),
        c1b,
        embed_weight_grad,
        embed_bias_grad,
        n2g,
        n2b,
        conv_out(wg2_sum),
        c2b,
        n3g,
        n3b,
        qkv_sum,
        qkv_bias_grad,
        encoder_weight_grad,
        encoder_bias_grad,
        proj_sum,
        pb,
    )


def solution(mesh):
    placed = (
        P(None, "ch", "rows"),
        P(),
        P(),
        P(),
        P(),
        P("ch"),
        P("ch"),
        P("ch", None, None, None),
        P("ch"),
        P(None, "ch", None),
        P(None, "ch"),
        P("ch"),
        P("ch"),
        P("ch", None, None, None),
        P("ch"),
        P("ch"),
        P("ch"),
        P(None, "ch", None),
        P(None, "ch"),
        P(None, "ch", None),
        P(None, "ch"),
        P("ch", None),
        P("ch"),
        P(None, "ch", "rows"),
    )
    return jax.shard_map(
        per_device,
        mesh=mesh,
        in_specs=placed,
        out_specs=(
            P(None, "ch", "rows"),
            P(None, "ch", "rows"),
            P("ch"),
            P("ch"),
            P("ch", None, None, None),
            P("ch"),
            P(None, "ch", None),
            P(None, "ch"),
            P("ch"),
            P("ch"),
            P("ch", None, None, None),
            P("ch"),
            P("ch"),
            P("ch"),
            P(None, "ch", None),
            P(None, "ch"),
            P(None, "ch", None),
            P(None, "ch"),
            P("ch", None),
            P("ch"),
        ),
        check_vma=False,
    )
```

```python
import functools
import math

import jax
import jax.numpy as jnp
from jax import lax
from jax.experimental import pallas as pl
from jax.experimental.pallas import tpu as pltpu
from jax.sharding import PartitionSpec as P

C = 512
HD = 64
GSZ = 16
EMB = 2048
W = 64
NCROP = 6
NC = 8
HP = 2 * W
TAPS = [(di, dj) for di in (-1, 0, 1) for dj in (-1, 0, 1)]

PRECISE = lax.Precision.HIGHEST
EPSILON = 1e-05
FAR = 2.0**100
SCORE = HD**-0.5
LOG2E = 1.4426950408889634
F32 = jnp.float32
BF = jnp.bfloat16


def spread(vals, lab):
    acc = vals[:, 0:1]
    for n in range(1, NCROP):
        acc = jnp.where(lab == n, vals[:, n : n + 1], acc)
    return acc


def crop_columns(first, second, lab):
    rows = first.shape[0]
    lane = lax.broadcasted_iota(jnp.int32, (rows, 128), 1)
    acc = jnp.zeros((rows, 128), F32)
    for n in range(NCROP):
        inside = lab == n
        one = jnp.sum(jnp.where(inside, first, 0.0), axis=1, keepdims=True)
        two = jnp.sum(jnp.where(inside, second, 0.0), axis=1, keepdims=True)
        acc = jnp.where(lane == n, one, acc)
        acc = jnp.where(lane == NC + n, two, acc)
    return acc


def put_column(acc, column, at):
    lane = lax.broadcasted_iota(jnp.int32, acc.shape, 1)
    return jnp.where(lane == at, column, acc)


def grouped(vals):
    rows, width = vals.shape
    parts = jnp.sum(vals.reshape(rows // GSZ, GSZ, width), axis=1, keepdims=True)
    return jnp.broadcast_to(parts, (rows // GSZ, GSZ, width)).reshape(rows, width)


def turned(block):
    rows, cols = block.shape
    if rows < 128:
        block = jnp.concatenate([block, jnp.zeros((128 - rows, cols), F32)], axis=0)
    return jnp.transpose(block)


def read_stats(recv_ref, which, cnt):
    members = recv_ref.shape[0]
    block = recv_ref[0, which]
    for g in range(1, members):
        other = recv_ref[g, which]
        block = jnp.concatenate([block[:16] + other[:16], block[16:]], axis=0)
    cols = turned(block)
    sums = grouped(cols[:, :16])
    mean = sums[:, :NC] / cnt
    inv = lax.rsqrt(sums[:, NC:16] / cnt - mean * mean + EPSILON)
    return mean, inv, cols[:, 16:17], cols[:, 17:18], cols[:, 18:19], cols[:, 19:20]


def read_sums(recv_ref, which):
    members = recv_ref.shape[0]
    block = recv_ref[0, which][:16]
    for g in range(1, members):
        block = block + recv_ref[g, which][:16]
    return turned(block)


def affine_of(stats):
    mean, inv, gain, bias, scale, offset = stats
    a = inv * gain * (1.0 + scale)
    b = (bias - mean * inv * gain) * (1.0 + scale) + offset
    return a, b


def sigmoid(v):
    return 0.5 * (1.0 + jnp.tanh(0.5 * v))


def slope(v):
    s = sigmoid(v)
    return s * (1.0 + v * (1.0 - s))


def masked_conv(w_ref, h_ref, y_ref, out_ref, mask_ref, bias):
    ch, width = out_ref.shape
    for g in range(3):
        w = w_ref[3 * g : 3 * g + 3].reshape(3 * ch, C)
        y_ref[g] = jnp.dot(w, h_ref[...], preferred_element_type=F32)
    size = min(ch, 64)

    def body(i, carry):
        i = pl.multiple_of(i * size, size)
        acc = None
        for g in range(3):
            for k in range(3):
                tap = 3 * g + k
                off = W * (g - 1) + k - 1
                y = y_ref[g, pl.ds(pl.multiple_of(k * ch + i, size), size), :]
                y = y if off == 0 else pltpu.roll(y, (-off) % width, 1)
                y = y * mask_ref[tap : tap + 1, :]
                acc = y if acc is None else acc + y
        if bias is not None:
            acc = acc + bias[pl.ds(i, size), 7:8]
        out_ref[pl.ds(i, size), :] = acc
        return carry

    lax.fori_loop(0, ch // size, body, 0)


def chunks(rows, body):
    size = min(128, rows)

    def step(i, carry):
        body(pl.multiple_of(i * size, size), size)
        return carry

    lax.fori_loop(0, rows // size, step, 0)


def send_rows(out_ref, st_ref, params):
    rows = jnp.transpose(st_ref[...])[:16]
    if params is not None:
        rows = jnp.concatenate([rows, params], axis=0)
    for k in range(out_ref.shape[0]):
        out_ref[k] = rows


def k_stats(x_ref, lab_ref, par_ref, out_ref, st_ref):
    n = x_ref.shape[1] - 2 * HP
    lab = lab_ref[:, HP : HP + n]

    def body(i, size):
        v = x_ref[pl.ds(i, size), HP : HP + n].astype(F32)
        st_ref[pl.ds(i, size), :] = crop_columns(v, v * v, lab)

    chunks(x_ref.shape[0], body)
    send_rows(out_ref, st_ref, par_ref[...])


def k_conv(nch, offs, resid, *refs):
    me_ref, recv_ref, cnt_ref, lab_ref, mask_ref, w_ref, par_ref = refs[:7]
    slots = refs[7 : 7 + nch]
    refs = refs[7 + nch :]
    if resid:
        x_ref, refs = refs[0], refs[1:]
        low_ref, pay_ref, h_ref, full_ref = refs[:4]
        refs = refs[4:]
    else:
        low_ref, pay_ref, h_ref = refs[:3]
        refs = refs[3:]
    y_ref, acc_ref, a_ref, b2_ref, st_ref = refs
    me = me_ref[0]
    ch, e = acc_ref.shape
    n = e - 2 * HP
    lab = lab_ref[...]
    for c in range(nch):
        a, b = affine_of(read_stats(recv_ref, c, cnt_ref[...]))
        a_ref[c * ch : (c + 1) * ch, :] = a
        b2_ref[c * ch : (c + 1) * ch, :] = b
    for s in range(nch):
        base = pl.multiple_of((me ^ offs[s]) * ch, ch)

        def body(i, size, s=s, base=base):
            row = pl.multiple_of(base + i, size)
            v = slots[s][pl.ds(i, size), :].astype(F32)
            pre = v * spread(a_ref[pl.ds(row, size), :], lab) + spread(b2_ref[pl.ds(row, size), :], lab)
            low = (pre * sigmoid(pre)).astype(BF)
            h_ref[pl.ds(row, size), :] = low

        chunks(ch, body)
    st_ref[...] = turned(par_ref[...])
    masked_conv(w_ref, h_ref, y_ref, acc_ref, mask_ref, st_ref)
    labc = lab[:, HP : HP + n]

    def finish(i, size):
        if resid:
            v = acc_ref[pl.ds(i, size), HP : HP + n] + x_ref[pl.ds(i, size), HP : HP + n].astype(F32)
            full_ref[pl.ds(i, size), :] = v
            low_ref[pl.ds(i, size), :] = v.astype(BF)
        else:
            low_ref[pl.ds(i, size), :] = acc_ref[pl.ds(i, size), :].astype(BF)
            v = acc_ref[pl.ds(i, size), HP : HP + n]
        st_ref[pl.ds(i, size), :] = crop_columns(v, v * v, labc)

    chunks(ch, finish)
    send_rows(pay_ref, st_ref, par_ref[...])


def k_qkv(nch, offs, *refs):
    me_ref, recv_ref, cnt_ref, lab_ref, w_ref, par_ref = refs[:6]
    slots = refs[6 : 6 + nch]
    res_ref, att_ref, q_ref, k_ref, v_ref, a_ref, b_ref = refs[6 + nch :]
    biases = turned(par_ref[...])
    me = me_ref[0]
    ch, n = q_ref.shape
    lab = lab_ref[:, HP : HP + n]
    for c in range(nch):
        a, b = affine_of(read_stats(recv_ref, c, cnt_ref[...]))
        a_ref[c * ch : (c + 1) * ch, :] = a
        b_ref[c * ch : (c + 1) * ch, :] = b
    for s in range(nch):
        base = pl.multiple_of((me ^ offs[s]) * ch, ch)

        def body(i, size, s=s, base=base):
            row = pl.multiple_of(base + i, size)
            low = slots[s][pl.ds(i, size), :]
            res_ref[pl.ds(row, size), :] = low
            out = low.astype(F32) * spread(a_ref[pl.ds(row, size), :], lab) + spread(
                b_ref[pl.ds(row, size), :], lab
            )
            att_ref[pl.ds(row, size), :] = out.astype(BF)

        chunks(ch, body)
    tile = 256

    def mul(i, _):
        at = pl.ds(pl.multiple_of(i * tile, tile), tile)
        x = att_ref[:, at]
        q_ref[:, at] = (jnp.dot(w_ref[0], x, preferred_element_type=F32) + biases[:, 0:1]).astype(BF)
        k_ref[:, at] = jnp.dot(w_ref[1], x, preferred_element_type=F32).astype(BF)
        v_ref[:, at] = (jnp.dot(w_ref[2], x, preferred_element_type=F32) + biases[:, 1:2]).astype(BF)
        return 0

    lax.fori_loop(0, n // tile, mul, 0)


def k_gout(nch, offs, *refs):
    me_ref, w_ref = refs[:2]
    slots = refs[2 : 2 + nch]
    g_ref, ga_ref = refs[2 + nch :]
    me = me_ref[0]
    ch, n = ga_ref.shape
    for s in range(nch):
        base = pl.multiple_of((me ^ offs[s]) * ch, ch)
        g_ref[pl.ds(base, ch), :] = slots[s][...]
    ga_ref[...] = jnp.dot(w_ref[...], g_ref[:, HP : HP + n], preferred_element_type=F32).astype(BF)


def k_turn(nch, offs, *refs):
    me_ref = refs[0]
    ins = refs[1 : 1 + nch]
    wqs = refs[1 + nch : 1 + 2 * nch]
    w1_ref, w2_ref, wq_ref, pw_ref, scr, scq = refs[1 + 2 * nch :]
    me = me_ref[0]
    ch = w1_ref.shape[1]
    for t in range(19):
        for s in range(nch):
            base = pl.multiple_of((me ^ offs[s]) * ch, ch)
            scr[pl.ds(base, ch), :] = ins[s][t].astype(F32)
        out = jnp.transpose(scr[...]).astype(BF)
        if t < 9:
            w1_ref[8 - t] = out
        elif t < 18:
            w2_ref[17 - t] = out
        else:
            pw_ref[...] = out
    for j in range(3):
        for s in range(nch):
            base = pl.multiple_of((me ^ offs[s]) * ch, ch)
            scq[pl.ds(base, ch), :] = wqs[s][j].astype(F32)
        wq_ref[j] = jnp.transpose(scq[...]).astype(BF)


def nt(a, b):
    return lax.dot_general(a, b, (((1,), (1,)), ((), ())), preferred_element_type=F32)


def tn(a, b):
    return lax.dot_general(a, b, (((0,), (0,)), ((), ())), preferred_element_type=F32)


def k_attend(kmap, vmap, nk, nv, korder, vorder, *refs):
    q_ref, ga_ref, oneq_ref, onek_ref, ck_ref, cv_ref = refs[:6]
    kparts = refs[6 : 6 + nk]
    vparts = refs[6 + nk : 6 + nk + nv]
    out_ref, dq_ref, dk0_ref, dk1_ref, dv0_ref, dv1_ref, dck_ref, dcv_ref = refs[
        6 + nk + nv : 14 + nk + nv
    ]
    ks_ref, vs_ref, e_ref, s_ref, ak_ref, av_ref = refs[14 + nk + nv :]
    ch, n = q_ref.shape
    heads = ch // HD
    slots = len(kmap)
    keys = slots * n
    tq = e_ref.shape[0]
    con = SCORE * LOG2E
    for h in range(heads):
        hs = slice(h * HD, (h + 1) * HD)
        for s in range(slots):
            i, j = kmap[s]
            ks_ref[h, 0:HD, s * n : (s + 1) * n] = kparts[i][j, hs, :]
            i, j = vmap[s]
            vs_ref[h, :, s * n : (s + 1) * n] = vparts[i][j, hs, :]
        ks_ref[h, HD : HD + 16, 0:keys] = onek_ref[...]
        ks_ref[h, 0:HD, keys:] = ck_ref[hs, :]
        ks_ref[h, HD : HD + 16, keys:] = jnp.zeros((16, 128), BF)
        vs_ref[h, :, keys:] = cv_ref[hs, :]
    once = n == tq
    if not once:
        ak_ref[...] = jnp.zeros_like(ak_ref)
        av_ref[...] = jnp.zeros_like(av_ref)
    spans = [(s * n, n) for s in range(slots)] + [(keys, 128)]

    for h in range(heads):
        hs = slice(h * HD, (h + 1) * HD)

        def block(b, _, h=h, hs=hs):
            at = pl.ds(pl.multiple_of(b * tq, tq), tq)
            qb = q_ref[hs, at]
            gb = ga_ref[hs, at]
            qa = jnp.transpose(
                jnp.concatenate([qb.astype(F32), oneq_ref[:, at].astype(F32)], axis=0)
            ).astype(BF)
            gt = jnp.transpose(gb.astype(F32))
            gtb = gt.astype(BF)
            top = jnp.full((tq, 128), -jnp.inf, F32)
            for k0, kn in spans:
                sc = jnp.dot(qa, ks_ref[h, :, k0 : k0 + kn], preferred_element_type=F32)
                s_ref[:, k0 : k0 + kn] = sc
                for u in range(kn // 128):
                    top = jnp.maximum(top, sc[:, u * 128 : (u + 1) * 128])
            top = jnp.max(top, axis=1, keepdims=True) * con
            tot = jnp.zeros((tq, 128), F32)
            acc = jnp.zeros((HD, tq), F32)
            for k0, kn in spans:
                ex = jnp.exp2(s_ref[:, k0 : k0 + kn] * con - top)
                for u in range(kn // 128):
                    tot = tot + ex[:, u * 128 : (u + 1) * 128]
                exb = ex.astype(BF)
                e_ref[:, k0 : k0 + kn] = exb
                acc = acc + nt(vs_ref[h, :, k0 : k0 + kn], exb)
            inv = 1.0 / jnp.sum(tot, axis=1, keepdims=True)
            acc = jnp.transpose(acc) * inv
            delta = jnp.sum(acc * gt, axis=1, keepdims=True)
            out_ref[hs, at] = jnp.transpose(acc).astype(BF)
            ql = jnp.transpose(qa[:, :HD].astype(F32) * (inv * SCORE)).astype(BF)
            gl = jnp.transpose(gt * inv).astype(BF)
            dq = jnp.zeros((HD, tq), F32)
            for k0, kn in spans:
                dp = jnp.dot(gtb, vs_ref[h, :, k0 : k0 + kn], preferred_element_type=F32)
                exb = e_ref[:, k0 : k0 + kn]
                ds = (exb.astype(F32) * (dp - delta)).astype(BF)
                dq = dq + nt(ks_ref[h, 0:HD, k0 : k0 + kn], ds)
                dk = jnp.dot(ql, ds, preferred_element_type=F32)
                dv = jnp.dot(gl, exb, preferred_element_type=F32)
                if not once:
                    dk = dk + ak_ref[hs, k0 : k0 + kn]
                    dv = dv + av_ref[hs, k0 : k0 + kn]
                ak_ref[hs, k0 : k0 + kn] = dk
                av_ref[hs, k0 : k0 + kn] = dv
            dq_ref[hs, at] = jnp.transpose(jnp.transpose(dq) * (inv * SCORE)).astype(BF)
            return 0

        lax.fori_loop(0, n // tq, block, 0)
    for order, acc_ref, outs in (
        (korder, ak_ref, (dk0_ref, dk1_ref)),
        (vorder, av_ref, (dv0_ref, dv1_ref)),
    ):
        for side in range(2):
            for i, s in enumerate(order[side]):
                outs[side][i] = acc_ref[:, s * n : (s + 1) * n].astype(BF)
    dck_ref[...] = ak_ref[:, keys:]
    dcv_ref[...] = av_ref[:, keys:]


def k_proj(nch, offs, *refs):
    me_ref, res_ref, par_ref, pw_ref = refs[:4]
    atts = refs[4 : 4 + nch]
    out_ref, att_s = refs[4 + nch :]
    me = me_ref[0]
    ch = res_ref.shape[0]
    for s in range(nch):
        base = pl.multiple_of((me ^ offs[s]) * ch, ch)
        att_s[pl.ds(base, ch), :] = atts[s][...]
    mixed = jnp.dot(pw_ref[...], att_s[...], preferred_element_type=F32)
    out_ref[...] = (res_ref[...] + mixed + turned(par_ref[...])[:, 2:3]).astype(BF)


def k_gattend(nch, offs, *refs):
    me_ref, recv_ref, cnt_ref, lab_ref, w_ref, res_ref = refs[:6]
    slots = [refs[6 + j * nch : 6 + (j + 1) * nch] for j in range(3)]
    ga_ref, pay_ref, d_s, acc_ref, st_ref = refs[6 + 3 * nch :]
    me = me_ref[0]
    n = ga_ref.shape[1]
    ch = C // nch
    lab = lab_ref[:, HP : HP + n]
    for j in range(3):
        for s in range(nch):
            base = pl.multiple_of((me ^ offs[s]) * ch, ch)
            d_s[j, pl.ds(base, ch), :] = slots[j][s][...]
    tile = 256

    def mul(i, _):
        at = pl.ds(pl.multiple_of(i * tile, tile), tile)
        acc = jnp.dot(w_ref[0], d_s[0, :, at], preferred_element_type=F32)
        acc = acc + jnp.dot(w_ref[1], d_s[1, :, at], preferred_element_type=F32)
        acc = acc + jnp.dot(w_ref[2], d_s[2, :, at], preferred_element_type=F32)
        acc_ref[:, at] = acc
        ga_ref[:, at] = acc.astype(BF)
        return 0

    lax.fori_loop(0, n // tile, mul, 0)
    mean, inv = read_stats(recv_ref, me, cnt_ref[...])[:2]
    own = pl.ds(pl.multiple_of(me * ch, ch), ch)
    ga = acc_ref[own, :]
    normed = (res_ref[own, :].astype(F32) - spread(mean, lab)) * spread(inv, lab)
    st_ref[...] = crop_columns(ga, ga * normed, lab)
    send_rows(pay_ref, st_ref, None)


def k_early(blocks, *refs):
    me_ref, dq_ref, in_ref, att_ref, g_ref, dck_ref, dcv_ref, out_ref, st_ref = refs
    ch, n = dq_ref.shape
    own = g_ref[pl.ds(pl.multiple_of(me_ref[0] * ch, ch), ch), HP : HP + n].astype(F32)
    acc = put_column(jnp.zeros((ch, 128), F32), jnp.sum(own, axis=1, keepdims=True), 1)
    dq = dq_ref[...]
    acc = put_column(acc, jnp.sum(dq.astype(F32), axis=1, keepdims=True), 0)
    both = jnp.concatenate([dck_ref[...], dcv_ref[...]], axis=1)
    ctx = jnp.concatenate([jnp.where(me_ref[2] == i, both, 0.0) for i in range(2)], axis=1)
    rows = ch // blocks
    for t, full in enumerate(
        (nt(dq, in_ref[...]), nt(att_ref[...], g_ref[:, HP : HP + n]), ctx)
    ):
        full = full.astype(BF)
        for i in range(blocks):
            out_ref[i, t] = full[i * rows : (i + 1) * rows]
    st_ref[...] = jnp.transpose(acc)[:8]


def norm_back(mean, inv, gain, t1, t2, cnt):
    m1 = grouped(gain * t1) / cnt
    m2 = grouped(gain * t2) / cnt
    return inv * gain, -inv * inv * m2, inv * (mean * inv * m2 - m1)


def k_back2(nch, split, *refs):
    (me_ref, recv3_ref, recvt_ref, recv2_ref, cnt_ref, lab_ref, mask_ref, w_ref) = refs[:8]
    ga_ref, res_ref, top_ref, bot_ref, g_ref, c1_ref, h2_ref = refs[8:15]
    more = refs[15:18]
    gp_ref, pay_ref, gr_ref = refs[18:21]
    outs, wst_ref = refs[21:-11], refs[-11]
    h_ref, y_ref, acc_ref, a_ref, b_ref, c_ref, st_ref, full_ref, w_scr, wy_ref = refs[-10:]
    me = me_ref[0]
    ch, e = acc_ref.shape
    n = e - 2 * HP
    lab = lab_ref[...]
    cnt = cnt_ref[...]
    for c in range(nch):
        sl = slice(c * ch, (c + 1) * ch)
        mean, inv, gain = read_stats(recv3_ref, c, cnt)[:3]
        t = read_sums(recvt_ref, c)
        a, b, cc = norm_back(mean, inv, gain, t[:, :NC], t[:, NC:16], cnt)
        a_ref[sl, :] = a
        b_ref[sl, :] = b
        c_ref[sl, :] = cc

    def body(i, size):
        row = pl.ds(i, size)
        low = pl.ds(pl.multiple_of(C + i, size), size)
        ga = jnp.concatenate([top_ref[row, :], ga_ref[row, :], bot_ref[row, :]], axis=1).astype(F32)
        v = jnp.concatenate([top_ref[low, :], res_ref[row, :], bot_ref[low, :]], axis=1).astype(F32)
        gr = (
            g_ref[row, :].astype(F32)
            + ga * spread(a_ref[row, :], lab)
            + v * spread(b_ref[row, :], lab)
            + spread(c_ref[row, :], lab)
        )
        full_ref[row, :] = gr
        h_ref[row, :] = gr.astype(BF)

    chunks(C, body)
    own = pl.multiple_of(me * ch, ch)
    gr_ref[...] = full_ref[pl.ds(own, ch), HP : HP + n]
    masked_conv(w_ref, h_ref, y_ref, acc_ref, mask_ref, None)
    stats = None
    mean, inv, gain, bias, scale, offset = read_stats(recv2_ref, me, cnt)
    a, b = affine_of((mean, inv, gain, bias, scale, offset))
    a_ref[0:ch, :] = a
    b_ref[0:ch, :] = b
    c_ref[0:ch, :] = inv
    a_ref[ch : 2 * ch, :] = -mean * inv

    def finish(i, size):
        row = pl.ds(i, size)
        v = c1_ref[row, :].astype(F32)
        pre = v * spread(a_ref[row, :], lab) + spread(b_ref[row, :], lab)
        gp = acc_ref[row, :] * slope(pre)
        gp_ref[row, :] = gp.astype(BF)
        labc = lab[:, HP : HP + n]
        normed = v[:, HP : HP + n] * spread(c_ref[row, :], labc) + spread(
            a_ref[pl.ds(pl.multiple_of(ch + i, size), size), :], labc
        )
        gpc = gp[:, HP : HP + n]
        acc = crop_columns(gpc, gpc * normed, labc)
        st_ref[row, :] = acc

    chunks(ch, finish)
    send_rows(pay_ref, st_ref, None)
    gc = gr_ref[...].astype(BF).astype(F32)
    wgrad_body(split, me_ref[1], gc, h2_ref, mask_ref, outs, wst_ref, w_scr, wy_ref, more)


def wgrad_body(split, pos, gc, h_ref, mask_ref, outs, st_ref, g_ref, y_ref, more=()):
    ch, n = gc.shape
    width = n + 2 * HP
    edge = jnp.zeros((ch, HP), F32)
    wide = jnp.concatenate([edge, gc, edge], axis=1)
    for t, (di, dj) in enumerate(TAPS):
        off = W * di + dj
        moved = wide * mask_ref[t : t + 1, :]
        moved = moved if off == 0 else pltpu.roll(moved, off % width, 1)
        g_ref[t * ch : (t + 1) * ch, :] = moved.astype(BF)
    rows = ch // 4

    def hand_out(k, t):
        if not split:
            outs[0][t] = y_ref[k * ch : (k + 1) * ch, :].astype(BF)
            return
        for o in range(4):
            at = pl.multiple_of(k * ch + (pos ^ o) * rows, rows)
            outs[o][t] = y_ref[pl.ds(at, rows), :].astype(BF)

    for g in range(3):
        y_ref[...] = nt(g_ref[3 * g * ch : 3 * (g + 1) * ch, :], h_ref[...])
        for k in range(3):
            hand_out(k, 3 * g + k)
    acc = jnp.zeros((ch, 128), F32)
    acc = put_column(acc, jnp.sum(gc, axis=1, keepdims=True), 0)
    if more:
        for k in range(2):
            y_ref[k * ch : (k + 1) * ch, :] = nt(more[k][...], more[2][...])
            hand_out(k, 9 + k)
        column = jnp.sum(more[1][...].astype(F32), axis=1, keepdims=True)
        acc = put_column(acc, column, 1)
    st_ref[...] = jnp.transpose(acc)[:8]


def k_place(me_ref, *refs):
    parts, out_ref = refs[:-1], refs[-1]
    rows = parts[0].shape[1]
    for o, part in enumerate(parts):
        at = pl.ds(pl.multiple_of((me_ref[1] ^ o) * rows, rows), rows)
        out_ref[:, at, :] = part[...].astype(F32)


def k_place2(me_ref, early_ref, *refs):
    parts, (out_ref, qkv_ref, proj_ref) = refs[:-3], refs[-3:]
    rows = parts[0].shape[1]
    for o, part in enumerate(parts):
        at = pl.ds(pl.multiple_of((me_ref[1] ^ o) * rows, rows), rows)
        out_ref[:, at, :] = part[:9].astype(F32)
        qkv_ref[1:3, at, :] = part[9:].astype(F32)
    low = early_ref.shape[2]
    for i in range(early_ref.shape[0]):
        qkv_ref[0, i * low : (i + 1) * low, :] = early_ref[i, 0].astype(F32)
        proj_ref[i * low : (i + 1) * low, :] = early_ref[i, 1].astype(F32)


def conv1_back(recv2_ref, recvu_ref, which, cnt):
    mean, inv, gain, _, scale, _ = read_stats(recv2_ref, which, cnt)
    u = read_sums(recvu_ref, which)
    return norm_back(mean, inv, gain * (1.0 + scale), u[:, :NC], u[:, NC:16], cnt)


def k_wgrad1(split, *refs):
    me_ref, recv2_ref, recvu_ref, cnt_ref, lab_ref, mask_ref, gp_ref, c1_ref, h_ref = refs[:9]
    outs, (st_ref, g_ref, y_ref) = refs[9:-3], refs[-3:]
    n = gp_ref.shape[1] - 2 * HP
    lab = lab_ref[:, HP : HP + n]
    a, b, c = conv1_back(recv2_ref, recvu_ref, me_ref[0], cnt_ref[...])
    gc = (
        gp_ref[:, HP : HP + n].astype(F32) * spread(a, lab)
        + c1_ref[:, HP : HP + n].astype(F32) * spread(b, lab)
        + spread(c, lab)
    ).astype(BF).astype(F32)
    wgrad_body(split, me_ref[1], gc, h_ref, mask_ref, outs, st_ref, g_ref, y_ref)


def k_back1(nch, offs, *refs):
    me_ref, recv1_ref, recv2_ref, recvu_ref, cnt_ref, lab_ref, mask_ref, w_ref, x_ref = refs[:9]
    wg1_ref, wg2_ref, early_ref, payu_ref, payt_ref = refs[9:14]
    gps = refs[14 : 14 + nch]
    c1s = refs[14 + nch : 14 + 2 * nch]
    gp1_ref, pay_ref = refs[14 + 2 * nch : 16 + 2 * nch]
    h_ref, y_ref, acc_ref, a_ref, b_ref, c_ref, st_ref = refs[16 + 2 * nch :]
    me = me_ref[0]
    ch, e = acc_ref.shape
    n = e - 2 * HP
    lab = lab_ref[...]
    cnt = cnt_ref[...]
    for c in range(nch):
        sl = slice(c * ch, (c + 1) * ch)
        a, b, cc = conv1_back(recv2_ref, recvu_ref, c, cnt)
        a_ref[sl, :] = a
        b_ref[sl, :] = b
        c_ref[sl, :] = cc
    for s in range(nch):
        base = pl.multiple_of((me ^ offs[s]) * ch, ch)

        def body(i, size, s=s, base=base):
            row = pl.multiple_of(base + i, size)
            at = pl.ds(row, size)
            gc = (
                gps[s][pl.ds(i, size), :].astype(F32) * spread(a_ref[at, :], lab)
                + c1s[s][pl.ds(i, size), :].astype(F32) * spread(b_ref[at, :], lab)
                + spread(c_ref[at, :], lab)
            )
            h_ref[at, :] = gc.astype(BF)

        chunks(ch, body)
    masked_conv(w_ref, h_ref, y_ref, acc_ref, mask_ref, None)
    stats = read_stats(recv1_ref, me, cnt)
    a, b = affine_of(stats)
    a_ref[0:ch, :] = a
    b_ref[0:ch, :] = b
    c_ref[0:ch, :] = stats[1]
    c_ref[ch : 2 * ch, :] = -stats[0] * stats[1]
    labc = lab[:, HP : HP + n]

    def finish(i, size):
        row = pl.ds(i, size)
        v = x_ref[row, HP : HP + n].astype(F32)
        pre = v * spread(a_ref[row, :], labc) + spread(b_ref[row, :], labc)
        gp = acc_ref[row, HP : HP + n] * slope(pre)
        gp1_ref[row, :] = gp
        normed = v * spread(c_ref[row, :], labc) + spread(
            c_ref[pl.ds(pl.multiple_of(ch + i, size), size), :], labc
        )
        st_ref[row, :] = crop_columns(gp, gp * normed, labc)

    chunks(ch, finish)
    u, t = payu_ref[0], payt_ref[0]
    smalls = jnp.zeros((16, ch), F32)
    at = lax.broadcasted_iota(jnp.int32, (16, ch), 0)
    for i, line in enumerate(
        (
            wg1_ref[0:1],
            wg2_ref[0:1],
            jnp.sum(u[:NC], axis=0, keepdims=True),
            jnp.sum(u[NC:], axis=0, keepdims=True),
            early_ref[1:2],
            early_ref[0:1],
            wg2_ref[1:2],
            jnp.sum(t[:NC], axis=0, keepdims=True),
            jnp.sum(t[NC:], axis=0, keepdims=True),
        )
    ):
        smalls = jnp.where(at == i, line, smalls)
    send_rows(pay_ref, st_ref, smalls)


def k_last(*refs):
    me_ref, recv1_ref, recvv_ref, cnt_ref, lab_ref, gp_ref, x_ref, gr_ref, par_ref = refs[:9]
    o_ref, one_ref, two_ref, mod_ref, emb_ref, qb_ref = refs[9:15]
    (n1g, n1b, c1b, n2g, n2b, c2b, n3g, n3b, pb) = refs[15:24]
    sum_ref, out_ref = refs[24:]
    ch, n = gp_ref.shape
    half = recvv_ref.shape[0] // 2
    lab = lab_ref[:, HP : HP + n]
    for m in range(2):
        tot = recvv_ref[m * half]
        for g in range(1, half):
            tot = tot + recvv_ref[m * half + g]
        sum_ref[m] = tot
    cnt = cnt_ref[...]
    mean, inv, gain = read_stats(recv1_ref, me_ref[0], cnt)[:3]
    v = turned(sum_ref[me_ref[1]][:16])
    a, b, c = norm_back(mean, inv, gain, v[:, :NC], v[:, NC:16], cnt)
    out = (
        gr_ref[...]
        + gp_ref[...] * spread(a, lab)
        + x_ref[:, HP : HP + n].astype(F32) * spread(b, lab)
        + spread(c, lab)
    )
    out_ref[0:ch, :] = o_ref[...].astype(F32)
    out_ref[ch:, :] = out
    mid = n // 2
    sides = out_ref[:, :mid], out_ref[:, mid:]
    one_ref[...] = jnp.where(me_ref[1] == 0, sides[0], sides[1]).astype(BF)
    two_ref[...] = jnp.where(me_ref[1] == 0, sides[1], sides[0]).astype(BF)
    both = sum_ref[0] + sum_ref[1]
    n1b[...] = jnp.sum(both[:NC], axis=0, keepdims=True)
    n1g[...] = jnp.sum(both[NC:16], axis=0, keepdims=True)
    for ref, at in ((c1b, 16), (c2b, 17), (pb, 20), (n3b, 23), (n3g, 24)):
        ref[...] = both[at : at + 1]
    qb_ref[...] = both[21:23]
    u1 = [sum_ref[m, 18:19] for m in range(2)]
    u2 = [sum_ref[m, 19:20] for m in range(2)]
    up = [1.0 + par_ref[2 + m : 3 + m] for m in range(2)]
    n2b[...] = up[0] * u1[0] + up[1] * u1[1]
    n2g[...] = up[0] * u2[0] + up[1] * u2[1]
    scales = [par_ref[0:1] * u2[m] + par_ref[1:2] * u1[m] for m in range(2)]
    mod_ref[...] = jnp.concatenate([scales[0], u1[0], scales[1], u1[1]], axis=0)
    emb_ref[...] = jnp.concatenate([scales[0] + scales[1], u1[0] + u1[1]], axis=0)


COST = {"k_stats": 2, "k_conv": 10, "k_qkv": 6, "k_gout": 3, "k_attend": 34, "k_turn": 5, "k_proj": 3, "k_gattend": 7, "k_early": 4, "k_back2": 17, "k_wgrad1": 5, "k_back1": 13, "k_last": 3, "k_place": 3, "k_place2": 3}
SM = pl.BlockSpec(memory_space=pltpu.SMEM)
VM = pl.BlockSpec(memory_space=pltpu.VMEM)


def call(kernel, args, outs, scratch=(), smem=1, flops=0, limit=48):
    name = getattr(kernel, "func", kernel).__name__
    flops = int(COST[name] * 1.8e9)
    bytes_all = sum(math.prod(a.shape) * a.dtype.itemsize for a in list(args) + list(outs))
    return pl.pallas_call(
        kernel,
        out_shape=tuple(outs),
        in_specs=[SM] * smem + [VM] * (len(args) - smem),
        out_specs=tuple(VM for _ in outs),
        scratch_shapes=list(scratch),
        compiler_params=pltpu.CompilerParams(vmem_limit_bytes=limit * 2**20),
        cost_estimate=pl.CostEstimate(flops=flops, bytes_accessed=bytes_all, transcendentals=0),
    )(*args)


def fence(*xs):
    return lax.optimization_barrier(xs)


def sd(shape, dtype):
    return jax.ShapeDtypeStruct(shape, dtype)


def swap(x, axis, bit):
    count = lax.axis_size(axis)
    return lax.ppermute(x, axis, [(i, i ^ bit) for i in range(count)])


def bits_of(count):
    return [1 << i for i in range(count.bit_length() - 1)]


def offsets(count):
    offs = [0]
    for bit in reversed(bits_of(count)):
        offs = offs + [o ^ bit for o in offs]
    return offs


def gather_ch(x):
    slots = [x]
    for bit in reversed(bits_of(lax.axis_size("ch"))):
        slots = slots + [swap(s, "ch", bit) for s in slots]
    return slots


def first_hops(x):
    return [x] + [swap(x, "ch", bit) for bit in reversed(bits_of(lax.axis_size("ch")))]


def last_hops(hops):
    bits = list(reversed(bits_of(lax.axis_size("ch"))))
    slots = [hops[0]]
    for at, bit in enumerate(bits):
        slots = slots + [hops[at + 1]] + [swap(s, "ch", bit) for s in slots[1:]]
    return slots


def gather_rows(x, bits):
    parts, places, offs = [x[None]], [(0, 0)], [0]
    for bit in bits:
        whole = parts[0] if len(parts) == 1 else jnp.concatenate(parts, axis=0)
        base = len(parts)
        parts = parts + [swap(whole, "rows", bit)]
        places = places + [(base, i) for i in range(len(offs))]
        offs = offs + [o ^ bit for o in offs]
    table = dict(zip(offs, places, strict=True))
    return parts, [table[o] for o in range(len(offs))]


def order_of(bits):
    keep = [0]
    for bit in reversed(bits[1:]):
        keep = keep + [o ^ bit for o in keep]
    return keep, [o ^ bits[0] for o in keep]


def add_low(a, b):
    return (a.astype(F32) + b.astype(F32)).astype(BF)


def scatter_rows(keep, got, bits):
    for bit in bits[1:]:
        mid = keep.shape[0] // 2
        give = add_low(keep[mid:], got[mid:])
        keep = add_low(keep[:mid], got[:mid])
        got = swap(give, "rows", bit)
    return add_low(keep[0], got[0])


class Chain:
    def __init__(self, parts, top):
        self.top, self.at, self.keep = top, 0, parts[0]
        self.flight = [swap(p, "rows", o) for o, p in enumerate(parts) if o]

    def advance(self):
        self.at += 1
        got = self.flight
        if self.at == 1:
            total = self.keep.astype(F32)
            for x in got:
                total = total + x.astype(F32)
            self.keep = total.astype(BF)
            self.flight = [swap(self.keep, "rows", self.top)]
        elif self.at == 2:
            self.keep = add_low(self.keep, got[0])
            self.flight = [swap(self.keep, "rows", o) for o in (1, 2, 3)]
        else:
            self.done = [self.keep, *got]


def meet(chains, *xs):
    flights, xs = lax.optimization_barrier(([c.flight for c in chains], xs))
    for c, flight in zip(chains, flights, strict=True):
        c.flight = flight
        c.advance()
    return xs


def per_device(
    features,
    crop_ids,
    timesteps,
    clip_embed,
    context,
    norm1_gain,
    norm1_bias,
    conv1_weight,
    conv1_bias,
    embed_weight,
    embed_bias,
    norm2_gain,
    norm2_bias,
    conv2_weight,
    conv2_bias,
    norm3_gain,
    norm3_bias,
    qkv_weight,
    qkv_bias,
    encoder_weight,
    encoder_bias,
    proj_weight,
    proj_bias,
    out_grad,
):
    batches, ch, pixels = features.shape
    rows_n = lax.axis_size("rows")
    nch = lax.axis_size("ch")
    half = rows_n // 2
    r = lax.axis_index("rows")
    me = lax.axis_index("ch")
    m, j = r // half, r % half
    even = r % 2 == 0
    n = 2 * pixels
    e = n + 2 * HP
    local_rows = n // W
    copies = half * nch
    offs = offsets(nch)
    flat = rows_n * nch
    teams = [list(range(copies)), list(range(copies, flat))]
    me1 = jnp.reshape(me, (1,)).astype(jnp.int32)
    me4 = jnp.stack([me, r % 4, m]).astype(jnp.int32)
    st8 = sd((8, ch), F32)

    evens, odds = range(0, rows_n, 2), range(1, rows_n, 2)
    first_perm = [(i, i // 2) for i in evens] + [(i, half + i // 2) for i in odds]
    second_perm = [(i, half + i // 2) for i in evens] + [(i, i // 2) for i in odds]

    def halo_perm(up, down):
        pairs = [(i, up * half + i // 2 - 1) for i in evens if i // 2 > 0]
        return pairs + [(i, down * half + i // 2 + 1) for i in odds if i // 2 < half - 1]

    def reshard(*xs):
        def side(when, cut):
            return jnp.concatenate([jnp.where(when, cut(x[0]), cut(x[1])) for x in xs], axis=0)

        def edge(x):
            return jnp.where(even, x[:, :HP], x[:, pixels - HP :])

        def all_of(x):
            return x

        one = lax.ppermute(side(even, all_of), "rows", first_perm)
        two = lax.ppermute(side(~even, all_of), "rows", second_perm)
        three = lax.ppermute(side(even, edge), "rows", halo_perm(0, 1))
        four = lax.ppermute(side(~even, edge), "rows", halo_perm(1, 0))
        return one, two, three, four

    def resharded(one, two, three, four):
        low = jnp.where(m == 0, one, two)
        high = jnp.where(m == 0, two, one)
        below = jnp.where(m == 0, three, four)
        above = jnp.where(m == 0, four, three)
        return jnp.concatenate([above, low, high, below], axis=1)

    def to_next(x):
        return lax.ppermute(
            x, "rows", [(i, i + 1) for i in range(rows_n - 1) if i % half != half - 1]
        )

    def to_prev(x):
        return lax.ppermute(x, "rows", [(i, i - 1) for i in range(1, rows_n) if i % half != 0])

    def team_exchange(x):
        got = lax.all_to_all(x, ("rows", "ch"), 0, 0, axis_index_groups=teams)
        return got.reshape((half, nch) + x.shape[1:])

    ids = lax.dynamic_index_in_dim(crop_ids, m, 0, keepdims=False)
    grid = jnp.pad(ids.reshape(-1, W), ((2, 2), (0, 0)), constant_values=-1)
    lab20 = lax.dynamic_slice_in_dim(grid, j * local_rows, local_rows + 4, 0)
    near = jnp.pad(lab20, 1, constant_values=-2)
    height = local_rows + 4
    masks = jnp.stack(
        [
            (near[1 + di : 1 + di + height, 1 + dj : 1 + dj + W] == lab20) & (lab20 >= 0)
            for di, dj in TAPS
        ]
    ).astype(F32)
    masks = jnp.pad(masks.reshape(9, e), ((0, 7), (0, 0)))
    lab = lab20.reshape(1, e)
    crops = jnp.arange(NC, dtype=jnp.int32)
    counted = jnp.sum((ids[None, :] == crops[:, None]).astype(F32), axis=1)
    cnt = jnp.maximum(counted, 1.0)[None, :] * GSZ

    w1 = conv1_weight.transpose(1, 2, 0, 3).reshape(9, ch, C)
    w2 = conv2_weight.transpose(1, 2, 0, 3).reshape(9, ch, C)

    parts = reshard(features, out_grad)
    x_own = resharded(*[x[:ch] for x in parts])
    g_own = resharded(*[x[ch:] for x in parts])
    x_own, clip_embed = fence(x_own, clip_embed)

    half_width = EMB // 2
    frequency = jnp.exp(-math.log(10000.0) * jnp.arange(half_width, dtype=F32) / half_width)
    angles = timesteps.astype(F32)[:, None] * frequency[None, :]
    embedded = jax.nn.silu(
        jnp.concatenate([jnp.cos(angles), jnp.sin(angles)], axis=1) + clip_embed
    )
    modulation = (
        jnp.einsum("be,jce->bjc", embedded, embed_weight.astype(F32), precision=PRECISE)
        + embed_bias
    )
    mod_here = lax.dynamic_index_in_dim(modulation, m, 0, keepdims=False)
    zero = jnp.zeros((1, ch), F32)

    def params(*rows):
        given = [x.reshape(1, ch).astype(F32) for x in rows]
        return jnp.concatenate(given + [zero] * (8 - len(given)), axis=0)

    par1 = params(norm1_gain, norm1_bias)
    blank = jnp.zeros((ch,), F32)
    par2 = params(norm2_gain, norm2_bias, mod_here[0], mod_here[1], blank, blank, blank, conv1_bias)
    par3 = params(norm3_gain, norm3_bias, blank, blank, blank, blank, blank, conv2_bias)
    par4 = params(qkv_bias[0], qkv_bias[1], proj_bias)

    x_slots = gather_ch(x_own)
    pay = sd((copies, 24, ch), F32)
    st = pltpu.VMEM((ch, 128), F32)
    (pay1,) = call(k_stats, (x_own, lab, par1), (pay,), [st], smem=0)
    recv1 = team_exchange(pay1)
    x_slots, recv1, g_own = fence(x_slots, recv1, g_own)
    g_slots = first_hops(g_own)
    conv_scratch = [
        pltpu.VMEM((3, 3 * ch, e), F32),
        pltpu.VMEM((ch, e), F32),
        pltpu.VMEM((C, NC), F32),
        pltpu.VMEM((C, NC), F32),
    ]
    conv_flops = 2 * 9 * ch * C * e

    low1, pay2, h1 = call(
        functools.partial(k_conv, nch, offs, False),
        (me1, recv1, cnt, lab, masks, w1, par2, *x_slots),
        (sd((ch, e), BF), pay, sd((C, e), BF)),
        conv_scratch + [st],
        flops=conv_flops,
    )
    low1, pay2, g_slots, w1, w2_cut, proj_weight_cut = fence(low1, pay2, g_slots, w1, w2, proj_weight)


    def packed(o):
        at = (me ^ o) * ch
        return jnp.concatenate(
            [
                lax.dynamic_slice_in_dim(w1, at, ch, 2),
                lax.dynamic_slice_in_dim(w2_cut, at, ch, 2),
                lax.dynamic_slice_in_dim(proj_weight_cut, at, ch, 1)[None],
            ],
            axis=0,
        )

    packs = [packed(o) for o in offs]
    c1_slots = gather_ch(low1)
    recv2 = team_exchange(pay2)
    c1_slots, recv2, g_slots, qkv_weight = fence(c1_slots, recv2, g_slots, qkv_weight)
    g_slots, wq_slots = last_hops(g_slots), first_hops(qkv_weight)
    low2, pay3, h2, resid = call(
        functools.partial(k_conv, nch, offs, True),
        (me1, recv2, cnt, lab, masks, w2, par3, *c1_slots, x_own),
        (sd((ch, n), BF), pay, sd((C, e), BF), sd((ch, n), F32)),
        conv_scratch + [st],
        flops=conv_flops,
    )
    low2, pay3, g_slots, wq_slots = fence(low2, pay3, g_slots, wq_slots)
    r_slots = gather_ch(low2)
    recv3 = team_exchange(pay3)
    r_slots, recv3, packs, wq_slots = fence(r_slots, recv3, packs, wq_slots)
    wq_slots = last_hops(wq_slots)
    packs = [w if o == 0 else swap(w, "ch", o) for o, w in zip(offs, packs, strict=True)]
    res_full, att_in, q, k, v = call(
        functools.partial(k_qkv, nch, offs),
        (me1, recv3, cnt, lab, qkv_weight, par4, *r_slots),
        (sd((C, n), BF), sd((C, n), BF), sd((ch, n), BF), sd((ch, n), BF), sd((ch, n), BF)),
        [pltpu.VMEM((C, NC), F32), pltpu.VMEM((C, NC), F32)],
        flops=2 * 3 * ch * C * n,
    )
    q, k, v, wq_slots = fence(q, k, v, wq_slots)
    row_bits = bits_of(half)
    k_parts, k_map = gather_rows(k, row_bits)
    v_parts, v_map = gather_rows(v, list(reversed(row_bits)))
    k_back, v_back = list(reversed(row_bits)), row_bits

    g_full, grad_att = call(
        functools.partial(k_gout, nch, offs),
        (me1, proj_weight, *g_slots),
        (sd((C, e), BF), sd((ch, n), BF)),
        flops=2 * ch * C * n,
    )
    ctx = lax.dynamic_index_in_dim(context, m, 0, keepdims=False)
    encoded = (
        jnp.einsum("te,jde->jdt", ctx, encoder_weight, preferred_element_type=F32)
        + encoder_bias[:, :, None]
    ).astype(BF)

    tiles = ids.reshape(half, n)
    key_ids = jnp.concatenate(
        [lax.dynamic_slice_in_dim(tiles, j ^ o, 1, 0) for o in range(half)], axis=1
    )
    crops16 = jnp.arange(16, dtype=jnp.int32)[:, None]
    one_k = jnp.where((key_ids == crops16) | (crops16 >= NC), 0.0, -FAR).astype(BF)
    one_q = (lab[:, HP : HP + n] == crops16).astype(BF)
    heads = ch // HD
    keys = half * n + 128
    tq = n if half * n <= 4096 else 256
    k_parts, v_parts, grad_att, encoded = fence(k_parts, v_parts, grad_att, encoded)
    attended, dq, dk0, dk1, dv0, dv1, dck, dcv = call(
        functools.partial(
            k_attend, k_map, v_map, len(k_parts), len(v_parts), order_of(k_back), order_of(v_back)
        ),
        (q, grad_att, one_q, one_k, encoded[0], encoded[1], *k_parts, *v_parts),
        (
            sd((ch, n), BF),
            sd((ch, n), BF),
            sd((half // 2, ch, n), BF),
            sd((half // 2, ch, n), BF),
            sd((half // 2, ch, n), BF),
            sd((half // 2, ch, n), BF),
            sd((ch, 128), F32),
            sd((ch, 128), F32),
        ),
        [
            pltpu.VMEM((heads, HD + 16, keys), BF),
            pltpu.VMEM((heads, HD, keys), BF),
            pltpu.VMEM((tq, keys), BF),
            pltpu.VMEM((tq, keys), F32),
            pltpu.VMEM((ch, keys), F32),
            pltpu.VMEM((ch, keys), F32),
        ],
        smem=0,
        flops=6 * 2 * heads * n * keys * HD,
        limit=60,
    )
    dk0, dk1, dv0, dv1, dq, attended, packs = fence(dk0, dk1, dv0, dv1, dq, attended, packs)
    got_k, got_v = swap(dk1, "rows", k_back[0]), swap(dv1, "rows", v_back[0])
    dq_slots = first_hops(dq)
    w1t, w2t, wqt, pwt = call(
        functools.partial(k_turn, nch, offs),
        (me1, *packs, *wq_slots),
        (sd((9, ch, C), BF), sd((9, ch, C), BF), sd((3, C, C), BF), sd((ch, C), BF)),
        [pltpu.VMEM((C, ch), F32), pltpu.VMEM((C, C), F32)],
    )
    split = rows_n == 8 and ch % 128 == 0
    blocks = rows_n if split else 1
    early, early_st = call(
        functools.partial(k_early, blocks),
        (me4, dq, att_in, attended, g_full, dck, dcv),
        (sd((blocks, 3, ch // blocks, C), BF), st8),
    )
    got_k, got_v, w1t, w2t, wqt, pwt, dq_slots, attended, early, early_st = fence(
        got_k, got_v, w1t, w2t, wqt, pwt, dq_slots, attended, early, early_st
    )
    dk = scatter_rows(dk0, got_k, k_back)
    dv = scatter_rows(dv0, got_v, v_back)
    dq_slots, a_slots = last_hops(dq_slots), first_hops(attended)
    dk, dv, dq_slots, a_slots, early = fence(dk, dv, dq_slots, a_slots, early)
    early = lax.all_to_all(early, "rows", 0, 0) if split else lax.psum(early, "rows")
    a_slots = last_hops(a_slots)
    dk_slots = gather_ch(dk)
    dv_slots = gather_ch(dv)
    (out_own,) = call(
        functools.partial(k_proj, nch, offs),
        (me1, resid, par4, pwt, *a_slots),
        (sd((ch, n), BF),),
        [pltpu.VMEM((C, n), BF)],
        flops=2 * ch * C * n,
    )
    dk_slots, dv_slots, out_own = fence(dk_slots, dv_slots, out_own)
    ga, pay_t = call(
        functools.partial(k_gattend, nch, offs),
        (me1, recv3, cnt, lab, wqt, res_full, *dq_slots, *dk_slots, *dv_slots),
        (sd((C, n), BF), sd((copies, 16, ch), F32)),
        [
            pltpu.VMEM((3, C, n), BF),
            pltpu.VMEM((C, n), F32),
            st,
        ],
        flops=2 * 3 * C * C * n,
    )
    if split:
        ga, pay_t, early = fence(ga, pay_t, early)
        early = jnp.sum(early.astype(F32), axis=0).astype(BF)
        early = lax.all_to_all(jnp.broadcast_to(early[None], (blocks, *early.shape)), "rows", 0, 0)
    recv_t = team_exchange(pay_t)
    top = to_next(jnp.concatenate([ga[:, n - HP :], res_full[:, n - HP :]], axis=0))
    bottom = to_prev(jnp.concatenate([ga[:, :HP], res_full[:, :HP]], axis=0))
    def pieces(units):
        return [sd((units, ch // 4, C), BF)] * 4 if split else [sd((units, ch, C), BF)]

    def begin(parts):
        return Chain(parts, 4) if split else lax.psum(parts[0], "rows")

    def moving(*chains):
        return list(chains) if split else []

    recv_t, top, bottom = fence(recv_t, top, bottom)
    wg_scratch = [pltpu.VMEM((9 * ch, e), BF), pltpu.VMEM((3 * ch, C), F32)]
    gp2, pay_u, grad_resid, *wg2, wg2_st = call(
        functools.partial(k_back2, nch, split),
        (
            me4, recv3, recv_t, recv2, cnt, lab, masks, w2t,
            ga, res_full, top, bottom, g_full, low1, h2, dk, dv, att_in,
        ),
        (sd((ch, e), BF), sd((copies, 16, ch), F32), sd((ch, n), F32), *pieces(11), st8),
        [
            pltpu.VMEM((C, e), BF),
            pltpu.VMEM((3, 3 * ch, e), F32),
            pltpu.VMEM((ch, e), F32),
            pltpu.VMEM((C, NC), F32),
            pltpu.VMEM((C, NC), F32),
            pltpu.VMEM((C, NC), F32),
            st,
            pltpu.VMEM((C, e), F32),
            *wg_scratch,
        ],
        flops=conv_flops,
    )
    gp2, pay_u, early_sum = fence(gp2, pay_u, early)
    gp_slots = first_hops(gp2)
    recv_u = team_exchange(pay_u)
    gp_slots = last_hops(gp_slots)
    wg2 = begin(wg2)
    *wg1, wg1_st = call(
        functools.partial(k_wgrad1, split),
        (me4, recv2, recv_u, cnt, lab, masks, gp2, low1, h1),
        (*pieces(9), st8),
        wg_scratch,
        flops=conv_flops,
    )
    wg1, gp_slots = meet(moving(wg2), wg1, gp_slots)
    wg1 = begin(wg1)
    gp1, pay_v = call(
        functools.partial(k_back1, nch, offs),
        (
            me1, recv1, recv2, recv_u, cnt, lab, masks, w1t, x_own,
            wg1_st, wg2_st, early_st, pay_u, pay_t, *gp_slots, *c1_slots,
        ),
        (sd((ch, n), F32), sd((rows_n, 32, ch), F32)),
        [
            pltpu.VMEM((C, e), BF),
            pltpu.VMEM((3, 3 * ch, e), F32),
            pltpu.VMEM((ch, e), F32),
            pltpu.VMEM((C, NC), F32),
            pltpu.VMEM((C, NC), F32),
            pltpu.VMEM((C, NC), F32),
            st,
        ],
        flops=conv_flops,
    )
    (gp1,) = meet(moving(wg2, wg1), gp1)
    recv_v = lax.all_to_all(pay_v, "rows", 0, 0)
    line = sd((1, ch), F32)
    one, two, mod_grad, embed_bias_grad, qkv_bias_grad, *lines = call(
        k_last,
        (
            jnp.stack([me, m]).astype(jnp.int32),
            recv1, recv_v, cnt, lab, gp1, x_own, grad_resid,
            params(norm2_gain, norm2_bias, modulation[0, 0], modulation[1, 0]), out_own,
        ),
        (*[sd((2 * ch, pixels), BF)] * 2, sd((4, ch), F32), sd((2, ch), F32), sd((2, ch), F32), *[line] * 9),
        [pltpu.VMEM((2, 32, ch), F32), pltpu.VMEM((2 * ch, n), F32)],
    )
    one, two = meet(moving(wg2, wg1), one, two)
    one = lax.ppermute(one, "rows", [(b, a) for a, b in first_perm])
    two = lax.ppermute(two, "rows", [(b, a) for a, b in second_perm])
    output, features_grad = [
        jnp.stack([jnp.where(even, x, y), jnp.where(even, y, x)])
        for x, y in ((one[:ch], two[:ch]), (one[ch:], two[ch:]))
    ]
    placed = (sd((9, ch, C), F32), sd((3, ch, C), F32), sd((ch, C), F32))
    if split:
        wg2_sum, qkv_sum, proj_sum = call(k_place2, (me4, early_sum, *wg2.done), placed)
        meet([wg1])
        (wg1_sum,) = call(k_place, (me4, *wg1.done), placed[:1])
    else:
        wg2_sum, wg1_sum = wg2[:9].astype(F32), wg1.astype(F32)
        qkv_sum = jnp.concatenate([early_sum[0, :1], wg2[9:]], axis=0).astype(F32)
        proj_sum = early_sum[0, 1].astype(F32)

    n1g, n1b, c1b, n2g, n2b, c2b, n3g, n3b, pb = [x.reshape(ch) for x in lines]
    mod_grad = mod_grad.reshape(2, 2, ch)
    embed_weight_grad = (
        mod_grad[0][:, :, None] * embedded[0][None, None, :]
        + mod_grad[1][:, :, None] * embedded[1][None, None, :]
    )
    encoder_grad = early_sum[:, 2].reshape(ch, batches, 2, -1)
    encoder_weight_grad = jnp.einsum(
        "dbjt,bte->jde", encoder_grad, context, preferred_element_type=F32
    )
    encoder_bias_grad = jnp.sum(encoder_grad.astype(F32), axis=(1, 3)).T

    def conv_out(x):
        return x.reshape(3, 3, ch, C).transpose(2, 0, 1, 3)

    return (
        output,
        features_grad,
        n1g,
        n1b,
        conv_out(wg1_sum),
        c1b,
        embed_weight_grad,
        embed_bias_grad,
        n2g,
        n2b,
        conv_out(wg2_sum),
        c2b,
        n3g,
        n3b,
        qkv_sum,
        qkv_bias_grad,
        encoder_weight_grad,
        encoder_bias_grad,
        proj_sum,
        pb,
    )


def solution(mesh):
    placed = (
        P(None, "ch", "rows"),
        P(),
        P(),
        P(),
        P(),
        P("ch"),
        P("ch"),
        P("ch", None, None, None),
        P("ch"),
        P(None, "ch", None),
        P(None, "ch"),
        P("ch"),
        P("ch"),
        P("ch", None, None, None),
        P("ch"),
        P("ch"),
        P("ch"),
        P(None, "ch", None),
        P(None, "ch"),
        P(None, "ch", None),
        P(None, "ch"),
        P("ch", None),
        P("ch"),
        P(None, "ch", "rows"),
    )
    return jax.shard_map(
        per_device,
        mesh=mesh,
        in_specs=placed,
        out_specs=(
            P(None, "ch", "rows"),
            P(None, "ch", "rows"),
            P("ch"),
            P("ch"),
            P("ch", None, None, None),
            P("ch"),
            P(None, "ch", None),
            P(None, "ch"),
            P("ch"),
            P("ch"),
            P("ch", None, None, None),
            P("ch"),
            P("ch"),
            P("ch"),
            P(None, "ch", None),
            P(None, "ch"),
            P(None, "ch", None),
            P(None, "ch"),
            P("ch", None),
            P("ch"),
        ),
        check_vma=False,
    )
```
